512 devices in a mesh: gx: 16 (over y, z_hi), gy: 8 (over z_lo, core), gz: 4 (over x).
Axes of the slice: x: 4, y: 4, z: 16 (z_hi: 4, z_lo: 4; z = z_hi * 4 + z_lo), core: 2. Of those that a mesh axis runs over, the one named last changes fastest.
Arguments:
- e_field: float32 [3, 64, 128, 512], P(None, 'gx', 'gy', 'gz'), may hold values from -6 to 6
- h_field: float32 [3, 64, 128, 512], P(None, 'gx', 'gy', 'gz'), may hold values from -6 to 6
- current: float32 [3, 64, 128, 512], P(None, 'gx', 'gy', 'gz'), may hold values from -6 to 6
- material: int32 [64, 128, 512], P('gx', 'gy', 'gz'), may hold values from 0 to 2
- sigma_table: float32 [3], replicated, may hold values from 0.05 to 2
- gamma_table: float32 [3], replicated, may hold values from 0.05 to 1
- plasma_table: float32 [3], replicated, may hold values from 0.3 to 2
- g_kernel: float32 [4], replicated, may hold values from -4 to 4
- surf_cell: int32 [16, 8, 4, 1024], P('gx', 'gy', 'gz'), may hold values from 0 to 8191
- surf_owner: int32 [16, 8, 4, 1024, 1], P('gx', 'gy', 'gz'), may hold values from 0 to 127; in each aligned block of 1024 rows (0 to 1023, 1024 to 2047, ..., all dimensions but the last counted through in order) at most 12 rows name the same one
- surf_tile: int32 [16, 8, 4, 1024], P('gx', 'gy', 'gz'), may hold values from 0 to 127
- surf_normal: int32 [16, 8, 4, 1024], P('gx', 'gy', 'gz'), may hold values from 0 to 5
- row_count: int32 [16, 8, 4], P('gx', 'gy', 'gz'), may hold values from 256 to 1024, as said below
Outputs:
- e_out: float32 [3, 64, 128, 512], P(None, 'gx', 'gy', 'gz')
- h_out: float32 [3, 64, 128, 512], P(None, 'gx', 'gy', 'gz')
- force: float32 [3, 65536], P(None, ('gx', 'gy', 'gz'))
The draws below stay inside these ranges and needn't reach their ends.
Inputs may be any that keep to these rules, and one draw needn't show every extreme that they name: `surf_owner`: among the slots of one device no owner is named more than 12 times, a bound that some block reaches. `row_count`: some brick has all 1024 slots live.
All inputs are finite; a program needn't handle non-finite values.
Results may differ from the reference program's by a relative error of at most 0.00019.
Values sent between devices are 32-bit elements; how exact they have to be, the bound alone decides.
A program may use at most 64 MiB of HBM per device.

```python
import math
import jax
import jax.numpy as jnp
import numpy as np
from jax import lax

CX = 4
CY = 16
CZ = 128
STEPS = 4
MATERIALS = 3
SLOTS = 1024
TILE_DEV = 128
CAP = 12
NX = 64
NY = 128
NZ = 512
TILES = 65536
N_GX = 16
N_GY = 8
N_GZ = 4


def draw_row_count(key, part):
    bricks = N_GX * N_GY * N_GZ
    key_a, key_b, key_c = jax.random.split(key, 3)
    row_loads = jax.random.randint(key_a, (bricks,), SLOTS // 4, SLOTS + 1, dtype=jnp.int32)
    first = jax.random.randint(key_b, (), 0, bricks, dtype=jnp.int32)
    second = (first + 1 + jax.random.randint(key_c, (), 0, bricks - 1, dtype=jnp.int32)) % bricks
    row_loads = row_loads.at[second].set(SLOTS // 4)
    row_loads = row_loads.at[first].set(SLOTS)
    return row_loads.reshape(N_GX, N_GY, N_GZ)


def with_ends(drawn, rng, low, high):
    index_at = [jax.random.randint(jax.random.fold_in(rng, axis), (), 0, length) for axis, length in enumerate(drawn.shape)]
    main_axis = drawn.shape.index(max(drawn.shape))
    beside = index_at[:main_axis] + [(index_at[main_axis] + 1) % drawn.shape[main_axis]] + index_at[main_axis + 1:]
    return drawn.at[tuple(index_at)].set(low).at[tuple(beside)].set(high)


def steps_of(rng, dims, pieces, low, largest):
    def one(position, blocks):
        heights = jax.random.uniform(jax.random.fold_in(jax.random.fold_in(rng, 6), position), (blocks,), jnp.float32, low / len(pieces), largest / len(pieces))
        return jnp.repeat(jnp.exp(heights), dims[position] // blocks).reshape((-1,) + (1,) * (len(dims) - position - 1))

    level = one(*pieces[0])
    for cut in pieces[1:]:
        level = level * one(*cut)
    return level


def routed_block(key, own, number, rows, amount, top, limit, slope):
    ranking = jax.random.permutation(key, amount)
    crowded, common = portions_of(amount, rows * top, limit, slope, True), portions_of(amount, rows * top, limit, slope, False)
    places = jnp.arange(amount)

    def named(tallies, offset_by):
        used = int((tallies > 0).sum())
        fixed = max(1, used // 4)
        shifted = fixed + (places - fixed + offset_by * (used - fixed)) % max(1, amount - fixed)
        return jnp.zeros((amount,), jnp.int32).at[ranking[jnp.where(places < fixed, places, shifted)]].set(jnp.asarray(tallies, jnp.int32))

    tallies = jnp.where(number % 4 == 0, named(crowded, number // 4), named(common, number - number // 4 - 1))
    mixed = jax.random.permutation(jax.random.fold_in(own, 3), amount)
    donor, sink = mixed[0:amount // 2 * 2:2], mixed[1:amount // 2 * 2:2]
    margin = jnp.minimum(tallies[donor] - 1, limit - tallies[sink]) // 2
    margin = jnp.where((donor == ranking[0]) | (sink == ranking[0]) | (tallies[sink] == 0), 0, jnp.maximum(margin, 0))
    shifted = jax.random.randint(jax.random.fold_in(own, 4), (amount // 2,), 0, 1 << 20) % (margin + 1)
    tallies = tallies.at[donor].add(-shifted).at[sink].add(shifted)
    items = jnp.searchsorted(jnp.cumsum(tallies), jnp.arange(rows * top), side="right").astype(jnp.int32)
    listing = items.reshape(top, rows).T
    listing = listing[jax.random.permutation(jax.random.fold_in(own, 1), rows)]
    offset_by = jax.random.randint(jax.random.fold_in(own, 2), (rows, 1), 0, top)
    return jnp.take_along_axis(listing, (jnp.arange(top)[None, :] + offset_by) % top, axis=1)


def portions_of(number_of, total, bound, slope, full):
    portions = [(1 << 20) // math.isqrt(rank ** slope) + 1 for rank in range(1, number_of + 1)]
    largest = bound if full else min(bound, max(-(-total // number_of), total * portions[0] // sum(portions)))
    least = 1 if total - largest >= number_of - 1 else 0
    given, spare = [largest] + [least] * (number_of - 1), total - largest - least * (number_of - 1)
    while spare > 0:
        free = [i for i in range(1, number_of) if given[i] < largest] or [i for i in range(1, number_of) if given[i] < bound]
        whole, left = sum([portions[i] for i in free]), spare
        for i in free:
            extra = min(bound - given[i], max(1, left * portions[i] // whole), spare)
            given[i] = given[i] + extra
            spare = spare - extra
    return np.array(given)


def centred(own_key, shape, scale, reach, pieces=(), kind=jnp.bfloat16):
    drawn = scale * jax.random.normal(own_key, shape, jnp.float32)
    if pieces:
        drawn = drawn * steps_of(own_key, shape, pieces, -0.22, 0.18)
    return jnp.clip(drawn, -reach, reach).astype(kind)


def setup_inputs(seed: int = 0) -> dict:
    keys = jax.random.split(jax.random.key(seed), 14)
    e_field = centred(keys[0], (3, NX, NY, NZ), 1.0, 6.0, ((1, 16), (2, 8), (3, 4)), jnp.float32)
    h_field = centred(keys[1], (3, NX, NY, NZ), 1.0, 6.0, ((1, 16), (2, 8), (3, 4)), jnp.float32)
    current = centred(keys[2], (3, NX, NY, NZ), 1.0, 6.0, ((1, 16), (2, 8), (3, 4)), jnp.float32)
    material = with_ends(jax.random.randint(keys[3], (NX, NY, NZ), 0, MATERIALS), jax.random.fold_in(keys[3], 1), 0, MATERIALS - 1).astype(jnp.int32)
    sigma_table = jnp.clip(jnp.exp(jax.random.uniform(keys[4], (MATERIALS,), jnp.float32, math.log(0.05), math.log(2.0))), 0.05, 2.0)
    gamma_table = jnp.clip(jnp.exp(jax.random.uniform(keys[5], (MATERIALS,), jnp.float32, math.log(0.05), math.log(1.0))), 0.05, 1.0)
    plasma_table = jnp.clip(jnp.exp(jax.random.uniform(keys[6], (MATERIALS,), jnp.float32, math.log(0.3), math.log(2.0))), 0.3, 2.0)
    g_kernel = centred(keys[7], (STEPS,), 1.0, 4.0, (), jnp.float32)
    surf_cell = with_ends(jax.random.randint(keys[8], (N_GX, N_GY, N_GZ, SLOTS), 0, CX * CY * CZ), jax.random.fold_in(keys[8], 1), 0, (CX * CY * CZ) - 1).astype(jnp.int32)
    surf_owner_keys = jax.random.split(jax.random.fold_in(keys[9], 1), N_GX * N_GY * N_GZ * SLOTS // SLOTS)
    surf_owner_turns = jax.random.permutation(jax.random.fold_in(keys[9], 3), N_GX * N_GY * N_GZ * SLOTS // SLOTS)
    surf_owner = jax.vmap(lambda own, number: routed_block(jax.random.fold_in(keys[9], 2), own, number, SLOTS, N_GX * N_GY, 1, CAP, 2))(surf_owner_keys, surf_owner_turns).reshape((N_GX, N_GY, N_GZ, SLOTS, 1))
    surf_tile = with_ends(jax.random.randint(keys[10], (N_GX, N_GY, N_GZ, SLOTS), 0, TILE_DEV), jax.random.fold_in(keys[10], 1), 0, TILE_DEV - 1).astype(jnp.int32)
    surf_normal = with_ends(jax.random.randint(keys[11], (N_GX, N_GY, N_GZ, SLOTS), 0, 6), jax.random.fold_in(keys[11], 1), 0, 5).astype(jnp.int32)
    row_count = draw_row_count(jax.random.fold_in(keys[13], 71), 0)
    return dict(e_field=e_field, h_field=h_field, current=current, material=material, sigma_table=sigma_table, gamma_table=gamma_table, plasma_table=plasma_table, g_kernel=g_kernel, surf_cell=surf_cell, surf_owner=surf_owner, surf_tile=surf_tile, surf_normal=surf_normal, row_count=row_count)


STEP_DT = 0.5
FACE_AREA = 0.25


def forward_curl(padded):
    elec_x, elec_y, elec_z = padded[0], padded[1], padded[2]
    curl_x = (elec_z[:-1, 1:, :-1] - elec_z[:-1, :-1, :-1]) - (elec_y[:-1, :-1, 1:] - elec_y[:-1, :-1, :-1])
    curl_y = (elec_x[:-1, :-1, 1:] - elec_x[:-1, :-1, :-1]) - (elec_z[1:, :-1, :-1] - elec_z[:-1, :-1, :-1])
    curl_z = (elec_y[1:, :-1, :-1] - elec_y[:-1, :-1, :-1]) - (elec_x[:-1, 1:, :-1] - elec_x[:-1, :-1, :-1])
    return jnp.stack([curl_x, curl_y, curl_z])


def backward_curl(padded):
    magn_x, magn_y, magn_z = padded[0], padded[1], padded[2]
    curl_x = (magn_z[1:, 1:, 1:] - magn_z[1:, :-1, 1:]) - (magn_y[1:, 1:, 1:] - magn_y[1:, 1:, :-1])
    curl_y = (magn_x[1:, 1:, 1:] - magn_x[1:, 1:, :-1]) - (magn_z[1:, 1:, 1:] - magn_z[:-1, 1:, 1:])
    curl_z = (magn_y[1:, 1:, 1:] - magn_y[:-1, 1:, 1:]) - (magn_x[1:, 1:, 1:] - magn_x[1:, :-1, 1:])
    return jnp.stack([curl_x, curl_y, curl_z])


def lookup(material, table):
    result = jnp.zeros(material.shape, table.dtype)
    for which in range(table.shape[0]):
        result = result + jnp.where(material == which, table[which], jnp.zeros((), table.dtype))
    return result


def coefficients(material, sigma_table, gamma_table, plasma_table):
    sigma = lookup(material, sigma_table)
    gamma = lookup(material, gamma_table)
    plasma = lookup(material, plasma_table)
    keep_e = (1.0 - sigma * STEP_DT / 2) / (1.0 + sigma * STEP_DT / 2)
    gain_e = STEP_DT / (1.0 + sigma * STEP_DT / 2)
    keep_j = (1.0 - gamma * STEP_DT / 2) / (1.0 + gamma * STEP_DT / 2)
    gain_j = plasma * STEP_DT / (1.0 + gamma * STEP_DT / 2)
    return keep_e, gain_e, keep_j, gain_j


def row_forces(elec_rows, magn_rows, normal):
    axis_of = normal // 2
    sign_of = (1 - 2 * (normal % 2)).astype(elec_rows.dtype)
    picked = (axis_of[None, :] == jnp.arange(3, dtype=jnp.int32)[:, None]).astype(elec_rows.dtype)
    elec_n = jnp.sum(elec_rows * picked, axis=0)
    magn_n = jnp.sum(magn_rows * picked, axis=0)
    energy = 0.5 * (jnp.sum(elec_rows * elec_rows, axis=0) + jnp.sum(magn_rows * magn_rows, axis=0))
    return sign_of * (elec_rows * elec_n + magn_rows * magn_n - picked * energy)


def reference(e_field, h_field, current, material, sigma_table, gamma_table, plasma_table, g_kernel, surf_cell, surf_owner, surf_tile, surf_normal, row_count):
    keep_e, gain_e, keep_j, gain_j = coefficients(material, sigma_table, gamma_table, plasma_table)
    electric, magnetic, drude = e_field, h_field, current
    grid_shape = (N_GX, N_GY, N_GZ, SLOTS)
    brick_x = lax.broadcasted_iota(jnp.int32, grid_shape, 0)
    brick_y = lax.broadcasted_iota(jnp.int32, grid_shape, 1)
    brick_z = lax.broadcasted_iota(jnp.int32, grid_shape, 2)
    slot_pos = lax.broadcasted_iota(jnp.int32, grid_shape, 3)
    glob_x = (brick_x * CX + surf_cell // (CY * CZ)).reshape(-1)
    glob_y = (brick_y * CY + (surf_cell // CZ) % CY).reshape(-1)
    glob_z = (brick_z * CZ + surf_cell % CZ).reshape(-1)
    normal = surf_normal.reshape(-1)
    live_mask = (slot_pos < row_count[:, :, :, None]).astype(e_field.dtype).reshape(-1)
    summed = jnp.zeros((3, normal.shape[0]), e_field.dtype)
    for moment in range(STEPS):
        magnetic = magnetic - STEP_DT * forward_curl(jnp.pad(electric, ((0, 0), (0, 1), (0, 1), (0, 1))))
        drude = keep_j * drude + gain_j * electric
        electric = keep_e * electric + gain_e * (backward_curl(jnp.pad(magnetic, ((0, 0), (1, 0), (1, 0), (1, 0)))) - drude)
        elec_rows = electric[:, glob_x, glob_y, glob_z]
        magn_rows = magnetic[:, glob_x, glob_y, glob_z]
        summed = summed + g_kernel[moment] * row_forces(elec_rows, magn_rows, normal)
    row_force = FACE_AREA * summed * live_mask
    segment = ((surf_owner.reshape(-1) * N_GZ + brick_z.reshape(-1)) * TILE_DEV + surf_tile.reshape(-1)).astype(jnp.int32)
    force = jax.ops.segment_sum(row_force.T, segment, num_segments=TILES).T
    return electric, magnetic, force
```

```python
import functools

import jax
import jax.numpy as jnp
from jax import lax
from jax.experimental import pallas as pl
from jax.experimental.pallas import tpu as pltpu
from jax.sharding import PartitionSpec as P

MESH = pl.DeviceIdType.MESH
F32 = jnp.float32
BF16 = jnp.bfloat16

DT = 0.5
FACE_AREA = 0.25
STEPS = 4
CX, CY, CZ = 4, 16, 128
SLOTS = 1024
TILE_DEV = 128
NGX, NGY, NGZ = 16, 8, 4
LANES = 16 * NGX

(XE, XQ, YE, YQ, ZE, ZQ, E_XZ, E_XY, E_YZ, E_YX, E_ZY, E_ZX) = range(12)
ROUTES = (
    (-1, 0, 0),
    (1, 0, 0),
    (0, -1, 0),
    (0, 1, 0),
    (0, 0, -1),
    (0, 0, 1),
    (1, 0, -1),
    (1, -1, 0),
    (0, 1, -1),
    (-1, 1, 0),
    (0, -1, 1),
    (-1, 0, 1),
)


def iota(shape, axis):
    return lax.broadcasted_iota(jnp.int32, shape, axis)


def dot(a, b, contract):
    return lax.dot_general(a, b, ((contract[:1], contract[1:]), ((), ())), preferred_element_type=F32)


def halves(x):
    high = x.astype(BF16)
    return high, (x - high.astype(F32)).astype(BF16)


def kernel(
    e_in,
    h_in,
    j_in,
    mat_in,
    cell_ref,
    owner_ref,
    tile_ref,
    normal_ref,
    sig_ref,
    gam_ref,
    pla_ref,
    g_ref,
    count_ref,
    e_out,
    h_out,
    force_ref,
    e_ref,
    h_ref,
    j_ref,
    part,
    mat_ref,
    coef,
    tensor,
    sx,
    rx,
    sy,
    ry,
    sz,
    rz,
    sr,
    rr,
    bucket,
    lane_hot,
    tile_hot,
    stl,
    rtl,
    sval,
    rval,
    sdense,
    rdense,
    in_sem,
    out_sem,
    hs_sem,
    hr_sem,
    ts_sem,
    tr_sem,
    vs_sem,
    vr_sem,
    ds_sem,
    dr_sem,
):
    gx, gy, gz = lax.axis_index("gx"), lax.axis_index("gy"), lax.axis_index("gz")

    loads = [
        pltpu.make_async_copy(src, dst, in_sem.at[n])
        for n, (src, dst) in enumerate(((e_in, e_ref), (h_in, h_ref), (j_in, j_ref), (mat_in, mat_ref)))
    ]
    for load in loads:
        load.start()

    def at(dx, dy, dz):
        where = {}
        if dx:
            where["gx"] = lax.rem(gx + (dx + NGX), NGX)
        if dy:
            where["gy"] = lax.rem(gy + (dy + NGY), NGY)
        if dz:
            where["gz"] = lax.rem(gz + (dz + NGZ), NGZ)
        return where

    barrier = pltpu.get_barrier_semaphore()
    greeted = list(ROUTES)
    greeted += [(0, d, 0) for d in range(2, NGY - 1)]
    greeted += [(d, 0, 0) for d in range(2, NGX - 1)]
    for route in greeted:
        pl.semaphore_signal(barrier, inc=1, device_id=at(*route), device_id_type=MESH)

    one, zero = jnp.float32(1.0), jnp.float32(0.0)
    low_x = jnp.where(gx > 0, one, zero)
    low_y = jnp.where(gy > 0, one, zero)
    low_z = jnp.where(gz > 0, one, zero)
    top_x = jnp.where(gx < NGX - 1, one, zero)
    top_y = jnp.where(gy < NGY - 1, one, zero)
    top_z = jnp.where(gz < NGZ - 1, one, zero)

    brick = (CX, CY, CZ)
    jj, kk = iota(brick, 1), iota(brick, 2)
    n_hot = (iota((16, 8, CZ), 0) == iota((16, 8, CZ), 2)).astype(F32)
    row_hot = (iota((CY, CZ), 0) == iota((CY, CZ), 1)).astype(F32)

    def y_next(f):
        return pltpu.roll(f, CY - 1, 1)

    def z_next(f):
        return pltpu.roll(f, CZ - 1, 2)

    def packed(columns):
        return jnp.sum(columns.reshape(16, 8, -1) * n_hot, axis=0)

    def unpacked(tile):
        return jnp.sum(tile[None] * n_hot, axis=2, keepdims=True).reshape(2, CX, CY, 1)

    def message(step, which):
        src, dst = {
            XE: (sx.at[step, 0], rx.at[step, 0]),
            XQ: (sx.at[step, 1], rx.at[step, 1]),
            YE: (sy.at[step, pl.ds(0, 2)], ry.at[step, pl.ds(0, 2)]),
            YQ: (sy.at[step, pl.ds(2, 2)], ry.at[step, pl.ds(2, 2)]),
            ZE: (sz.at[step, 0], rz.at[step, 0]),
            ZQ: (sz.at[step, 1], rz.at[step, 1]),
            E_XZ: (sr.at[step, 0], rr.at[step, 0]),
            E_XY: (sr.at[step, 1], rr.at[step, 1]),
            E_YX: (sr.at[step, 2], rr.at[step, 2]),
            E_ZX: (sr.at[step, 3], rr.at[step, 3]),
            E_YZ: (sy.at[step, 4], ry.at[step, 4]),
            E_ZY: (sy.at[step, 5], ry.at[step, 5]),
        }[which]
        return pltpu.make_async_remote_copy(
            src_ref=src,
            dst_ref=dst,
            send_sem=hs_sem.at[step, which],
            recv_sem=hr_sem.at[step, which],
            device_id=at(*ROUTES[which]),
            device_id_type=MESH,
        )

    def send_electric(step):
        ex, ey, ez = e_ref[0], e_ref[1], e_ref[2]
        sx[step, 0, 0] = ey[0]
        sx[step, 0, 1] = ez[0]
        message(step, XE).start()
        sr[step, 1] = ex[CX - 1, 0:1, :]
        sr[step, 2] = ey[0, CY - 1 : CY, :]
        sr[step, 0] = jnp.sum(ex[CX - 1, :, 0:1] * row_hot, axis=0, keepdims=True)
        sr[step, 3] = jnp.sum(ez[0, :, CZ - 1 : CZ] * row_hot, axis=0, keepdims=True)
        for which in (E_XY, E_YX, E_XZ, E_ZX):
            message(step, which).start()
        sy[step, 0] = ex[:, 0:1, :]
        sy[step, 1] = ez[:, 0:1, :]
        sy[step, 4] = ey[:, CY - 1 : CY, :]
        sy[step, 5] = ez[:, 0:1, :]
        sz[step, 0] = packed(e_ref[0:2][:, :, :, 0:1])
        for which in (YE, ZE, E_YZ, E_ZY):
            message(step, which).start()

    def send_magnetic(step):
        ex, ey, ez = e_ref[0], e_ref[1], e_ref[2]
        nothing = jnp.zeros((1, CY, CZ), F32)
        last_y, last_z = jj == CY - 1, kk == CZ - 1
        y_ez = jnp.where(last_y, zero, y_next(ez))
        y_ex = jnp.where(last_y, zero, y_next(ex))
        z_ey = jnp.where(last_z, zero, z_next(ey))
        z_ex = jnp.where(last_z, zero, z_next(ex))
        x_ez = jnp.concatenate([ez[1:], nothing], 0)
        x_ey = jnp.concatenate([ey[1:], nothing], 0)
        hx = h_ref[0] - DT * ((y_ez - ez) - (z_ey - ey))
        hy = h_ref[1] - DT * ((z_ex - ex) - (x_ez - ez))
        hz = h_ref[2] - DT * ((x_ey - ey) - (y_ex - ex))
        sx[step, 1, 0] = hy[CX - 1]
        sx[step, 1, 1] = hz[CX - 1]
        message(step, XQ).start()
        part[0], part[1], part[2] = hx, hy, hz
        sy[step, 2] = hx[:, CY - 1 : CY, :]
        sy[step, 3] = hz[:, CY - 1 : CY, :]
        sz[step, 1] = packed(part[0:2][:, :, :, CZ - 1 : CZ])
        message(step, YQ).start()
        message(step, ZQ).start()
        j_ref[...] = coef[2][None] * j_ref[...] + coef[3][None] * e_ref[...]

    def update(step):
        ex, ey, ez = e_ref[0], e_ref[1], e_ref[2]
        for which in range(12):
            message(step, which).wait_recv()
        above_x = rx[step, 0] * top_x
        above_y = ry[step, 0:2] * top_y
        above_z = unpacked(rz[step, 0]) * top_z
        hx, hy, hz = part[0], part[1], part[2]
        last_y, last_z = jj == CY - 1, kk == CZ - 1
        hx = hx + jnp.where(last_z, DT * above_z[1], zero) - jnp.where(last_y, DT * above_y[1], zero)
        hy = hy - jnp.where(last_z, DT * above_z[0], zero)
        hz = hz + jnp.where(last_y, DT * above_y[0], zero)
        hy = jnp.concatenate([hy[: CX - 1], (hy[CX - 1] + DT * above_x[1])[None]], 0)
        hz = jnp.concatenate([hz[: CX - 1], (hz[CX - 1] - DT * above_x[0])[None]], 0)
        h_ref[0], h_ref[1], h_ref[2] = hx, hy, hz
        e_xz = jnp.sum(rr[step, 0] * row_hot, axis=1, keepdims=True) * top_z
        e_zx = jnp.sum(rr[step, 3] * row_hot, axis=1, keepdims=True) * top_x
        e_xy = rr[step, 1] * top_y
        e_yx = rr[step, 2] * top_x
        e_yz = ry[step, 4] * top_z
        e_zy = ry[step, 5] * top_y
        jr, kr = iota((CY, CZ), 0), iota((CY, CZ), 1)
        below_xy = rx[step, 1, 0] + DT * ez[0] - jnp.where(kr == CZ - 1, DT * e_xz, zero)
        below_xz = rx[step, 1, 1] - DT * ey[0] + jnp.where(jr == CY - 1, DT * e_xy, zero)
        ky = iota((CX, 1, CZ), 2)
        below_yx = ry[step, 2] - DT * ez[:, 0:1, :] + jnp.where(ky == CZ - 1, DT * e_yz[:, :, 0:1], zero)
        below_yz = ry[step, 3] + DT * ex[:, 0:1, :]
        below_yz = jnp.concatenate([below_yz[: CX - 1], (below_yz[CX - 1] - DT * e_yx)[None]], 0)
        below_z = unpacked(rz[step, 1])
        jz = iota((CX, CY, 1), 1)
        below_zx = below_z[0] + DT * ey[:, :, 0:1] - jnp.where(jz == CY - 1, DT * e_zy[:, :, CZ - 1 : CZ], zero)
        below_zy = below_z[1] - DT * ex[:, :, 0:1]
        below_zy = jnp.concatenate([below_zy[: CX - 1], (below_zy[CX - 1] + DT * e_zx)[None]], 0)

        first_y, first_z = jj == 0, kk == 0
        y_hx = jnp.where(first_y, low_y * below_yx, pltpu.roll(hx, 1, 1))
        y_hz = jnp.where(first_y, low_y * below_yz, pltpu.roll(hz, 1, 1))
        z_hx = jnp.where(first_z, low_z * below_zx, pltpu.roll(hx, 1, 2))
        z_hy = jnp.where(first_z, low_z * below_zy, pltpu.roll(hy, 1, 2))
        x_hy = jnp.concatenate([(low_x * below_xy)[None], hy[: CX - 1]], 0)
        x_hz = jnp.concatenate([(low_x * below_xz)[None], hz[: CX - 1]], 0)
        keep, gain = coef[0], coef[1]
        e_ref[0] = keep * ex + gain * (((hz - y_hz) - (hy - z_hy)) - j_ref[0])
        e_ref[1] = keep * ey + gain * (((hx - z_hx) - (hz - x_hz)) - j_ref[1])
        e_ref[2] = keep * ez + gain * (((hy - x_hy) - (hx - y_hx)) - j_ref[2])

    def stress(step):
        ex, ey, ez = e_ref[0], e_ref[1], e_ref[2]
        hx, hy, hz = h_ref[0], h_ref[1], h_ref[2]
        g = g_ref[step]
        xx, yy, zz = ex * ex + hx * hx, ey * ey + hy * hy, ez * ez + hz * hz
        energy = 0.5 * (xx + yy + zz)
        found = (xx - energy, ex * ey + hx * hy, ex * ez + hx * hz, yy - energy, ey * ez + hy * hz, zz - energy)
        for n, value in enumerate(found):
            tensor[n] = g * value if step == 0 else tensor[n] + g * value

    def ranks_and_buckets():
        owner = owner_ref[...]
        block = SLOTS // 4
        groups = NGX * NGY
        earlier = (iota((block, block), 0) < iota((block, block), 1)).astype(F32).astype(BF16)
        lane = iota((1, block), 1)
        before = jnp.zeros((groups, 1), F32)
        made = jnp.zeros((5 * NGY, LANES), F32)
        for b in range(4):
            cut = slice(b * block, (b + 1) * block)
            own = owner[:, cut]
            hot = (own == iota((groups, block), 0)).astype(F32)
            ahead = dot(hot.astype(BF16), earlier, (1, 0)) + before
            rank = jnp.sum(ahead * hot, axis=0, keepdims=True).astype(jnp.int32)
            before = before + jnp.sum(hot, axis=1, keepdims=True)
            place = rank * NGX + lax.shift_right_logical(own, 3)
            place_hot = (place == iota((LANES, block), 0)).astype(F32).astype(BF16)
            cell, normal = cell_ref[:, cut], normal_ref[:, cut]
            live = (lane + b * block < count_ref[0]).astype(F32)
            weight = live * (FACE_AREA * (1 - 2 * (normal & 1)).astype(F32))
            mine = (own & 7) == iota((NGY, block), 0)
            entries = (
                (cell & 127).astype(F32),
                lax.shift_right_logical(cell, 7).astype(F32),
                weight,
                lax.shift_right_logical(normal, 1).astype(F32),
                tile_ref[:, cut].astype(F32),
            )
            rows = jnp.concatenate([jnp.where(mine, entry, zero) for entry in entries], 0)
            made = made + dot(rows.astype(BF16), place_hot, (1, 1))
        for n in range(5):
            bucket[n] = made[n * NGY : (n + 1) * NGY].reshape(NGY, 1, LANES)
        stl[...] = bucket[4]

    def to_gy(src, dst, send, recv, d):
        return pltpu.make_async_remote_copy(
            src_ref=src.at[lax.rem(gy + d, NGY)],
            dst_ref=dst.at[gy],
            send_sem=send.at[d],
            recv_sem=recv.at[d],
            device_id={"gy": lax.rem(gy + d, NGY)},
            device_id_type=MESH,
        )

    def from_gy(src, dst, send, recv, d):
        return pltpu.make_async_remote_copy(
            src_ref=src.at[lax.rem(gy + d, NGY)],
            dst_ref=dst.at[lax.rem(gy + NGY - d, NGY)],
            send_sem=send.at[d],
            recv_sem=recv.at[d],
            device_id={"gy": lax.rem(gy + d, NGY)},
            device_id_type=MESH,
        )

    def lane_hots():
        for n in range(NGY):
            lane_hot[n] = (bucket[0, n] == iota((CZ, LANES), 0).astype(F32)).astype(F32).astype(BF16)

    def tile_hots():
        for d in range(1, NGY):
            from_gy(stl, rtl, ts_sem, tr_sem, d).wait_recv()
        for n in range(NGY):
            tile_hot[n] = (rtl[n] == iota((TILE_DEV, LANES), 0).astype(F32)).astype(F32).astype(BF16)

    for load in loads:
        load.wait()
    material = mat_ref[...]

    def of_material(table):
        result = jnp.where(material == 0, table[0], zero)
        for which in (1, 2):
            result = jnp.where(material == which, table[which], result)
        return result

    sigma, gamma, plasma = of_material(sig_ref), of_material(gam_ref), of_material(pla_ref)
    coef[0] = (1.0 - sigma * DT / 2) / (1.0 + sigma * DT / 2)
    coef[1] = DT / (1.0 + sigma * DT / 2)
    coef[2] = (1.0 - gamma * DT / 2) / (1.0 + gamma * DT / 2)
    coef[3] = plasma * DT / (1.0 + gamma * DT / 2)

    pl.semaphore_wait(barrier, len(greeted))

    for step in range(STEPS):
        send_electric(step)
        send_magnetic(step)
        if step == 0:
            ranks_and_buckets()
            for d in range(1, NGY):
                to_gy(stl, rtl, ts_sem, tr_sem, d).start()
            rtl[gy] = stl[gy]
        else:
            stress(step - 1)
        if step == 1:
            lane_hots()
        if step == 2:
            tile_hots()
        update(step)
    stores = [
        pltpu.make_async_copy(src, dst, out_sem.at[n]) for n, (src, dst) in enumerate(((e_ref, e_out), (h_ref, h_out)))
    ]
    for store in stores:
        store.start()
    stress(STEPS - 1)

    cells = CX * CY
    high, low = halves(tensor[...].reshape(6 * cells, CZ))
    parts = jnp.concatenate([high, low], 1)
    for n in range(NGY):
        hot = lane_hot[n]
        read = dot(parts, jnp.concatenate([hot, hot], 0), (1, 0))
        row = bucket[1, n] == iota((cells, LANES), 0).astype(F32)
        xx, xy, xz, yy, yz, zz = [
            jnp.sum(jnp.where(row, read[c * cells : (c + 1) * cells], zero), axis=0, keepdims=True) for c in range(6)
        ]
        axis, weight = bucket[3, n], bucket[2, n]
        along_x, along_y = axis == 0.0, axis == 1.0
        sval[n, 0:1] = weight * jnp.where(along_x, xx, jnp.where(along_y, xy, xz))
        sval[n, 1:2] = weight * jnp.where(along_x, xy, jnp.where(along_y, yy, yz))
        sval[n, 2:3] = weight * jnp.where(along_x, xz, jnp.where(along_y, yz, zz))
    for d in range(1, NGY):
        to_gy(sval, rval, vs_sem, vr_sem, d).start()
    rval[gy] = sval[gy]

    for d in range(1, NGY):
        from_gy(sval, rval, vs_sem, vr_sem, d).wait_recv()
    row16 = iota((NGX * 16, LANES), 0)
    mine = (lax.shift_right_logical(row16, 4) == (iota((NGX * 16, LANES), 1) & (NGX - 1))).astype(F32).astype(BF16)
    dense = jnp.zeros((NGX * 16, TILE_DEV), F32)
    for n in range(NGY):
        value = jnp.concatenate([rval[n], jnp.zeros((5, LANES), F32)], 0)
        high = value.astype(BF16).astype(F32)
        both = jnp.concatenate([high, value - high], 0).astype(BF16)
        spread = jnp.concatenate([both] * NGX, 0) * mine
        dense = dense + dot(spread, tile_hot[n], (1, 1))
    dense = dense.reshape(NGX, 16, TILE_DEV)
    sdense[...] = (dense[:, 0:8] + dense[:, 8:16])[:, 0:3]

    def to_gx(d):
        return pltpu.make_async_remote_copy(
            src_ref=sdense.at[lax.rem(gx + d, NGX)],
            dst_ref=rdense.at[gx],
            send_sem=ds_sem.at[d],
            recv_sem=dr_sem.at[d],
            device_id={"gx": lax.rem(gx + d, NGX)},
            device_id_type=MESH,
        )

    for d in range(1, NGX):
        to_gx(d).start()
    rdense[gx] = sdense[gx]
    for d in range(1, NGX):
        pltpu.make_async_remote_copy(
            src_ref=sdense.at[lax.rem(gx + d, NGX)],
            dst_ref=rdense.at[lax.rem(gx + NGX - d, NGX)],
            send_sem=ds_sem.at[d],
            recv_sem=dr_sem.at[d],
            device_id={"gx": lax.rem(gx + d, NGX)},
            device_id_type=MESH,
        ).wait_recv()
    force_ref[...] = jnp.sum(rdense[...], axis=0)

    for step in range(STEPS):
        for which in range(12):
            message(step, which).wait_send()
    for d in range(1, NGY):
        to_gy(stl, rtl, ts_sem, tr_sem, d).wait_send()
        to_gy(sval, rval, vs_sem, vr_sem, d).wait_send()
    for d in range(1, NGX):
        to_gx(d).wait_send()
    for store in stores:
        store.wait()


def local(
    e_field,
    h_field,
    current,
    material,
    sigma_table,
    gamma_table,
    plasma_table,
    g_kernel,
    surf_cell,
    surf_owner,
    surf_tile,
    surf_normal,
    row_count,
):
    field = jax.ShapeDtypeStruct((3, CX, CY, CZ), F32)
    hbm = pl.BlockSpec(memory_space=pl.ANY)
    vmem = pl.BlockSpec(memory_space=pltpu.VMEM)
    smem = pl.BlockSpec(memory_space=pltpu.SMEM)
    dma = pltpu.SemaphoreType.DMA
    slots = [a.reshape(1, SLOTS) for a in (surf_cell, surf_owner, surf_tile, surf_normal)]
    return pl.pallas_call(
        kernel,
        out_shape=(field, field, jax.ShapeDtypeStruct((3, TILE_DEV), F32)),
        in_specs=[hbm] * 4 + [vmem] * 4 + [smem] * 5,
        out_specs=(hbm, hbm, vmem),
        scratch_shapes=[
            pltpu.VMEM((3, CX, CY, CZ), F32),
            pltpu.VMEM((3, CX, CY, CZ), F32),
            pltpu.VMEM((3, CX, CY, CZ), F32),
            pltpu.VMEM((3, CX, CY, CZ), F32),
            pltpu.VMEM((CX, CY, CZ), jnp.int32),
            pltpu.VMEM((4, CX, CY, CZ), F32),
            pltpu.VMEM((6, CX, CY, CZ), F32),
            pltpu.VMEM((STEPS, 2, 2, CY, CZ), F32),
            pltpu.VMEM((STEPS, 2, 2, CY, CZ), F32),
            pltpu.VMEM((STEPS, 6, CX, 1, CZ), F32),
            pltpu.VMEM((STEPS, 6, CX, 1, CZ), F32),
            pltpu.VMEM((STEPS, 2, 8, CZ), F32),
            pltpu.VMEM((STEPS, 2, 8, CZ), F32),
            pltpu.VMEM((STEPS, 4, 1, CZ), F32),
            pltpu.VMEM((STEPS, 4, 1, CZ), F32),
            pltpu.VMEM((5, NGY, 1, LANES), F32),
            pltpu.VMEM((NGY, CZ, LANES), BF16),
            pltpu.VMEM((NGY, TILE_DEV, LANES), BF16),
            pltpu.VMEM((NGY, 1, LANES), F32),
            pltpu.VMEM((NGY, 1, LANES), F32),
            pltpu.VMEM((NGY, 3, LANES), F32),
            pltpu.VMEM((NGY, 3, LANES), F32),
            pltpu.VMEM((NGX, 3, TILE_DEV), F32),
            pltpu.VMEM((NGX, 3, TILE_DEV), F32),
            dma((4,)),
            dma((2,)),
            dma((STEPS, 12)),
            dma((STEPS, 12)),
            dma((NGY,)),
            dma((NGY,)),
            dma((NGY,)),
            dma((NGY,)),
            dma((NGX,)),
            dma((NGX,)),
        ],
        compiler_params=pltpu.CompilerParams(
            collective_id=0, has_side_effects=True, vmem_limit_bytes=24 * 2**20
        ),
    )(
        e_field,
        h_field,
        current,
        material,
        *slots,
        sigma_table,
        gamma_table,
        plasma_table,
        g_kernel,
        row_count.reshape(1),
    )


def solution(mesh):
    cells = P("gx", "gy", "gz")
    field = P(None, "gx", "gy", "gz")
    slots = P("gx", "gy", "gz", None)
    return jax.shard_map(
        local,
        mesh=mesh,
        in_specs=(
            field,
            field,
            field,
            cells,
            P(),
            P(),
            P(),
            P(),
            slots,
            P("gx", "gy", "gz", None, None),
            slots,
            slots,
            cells,
        ),
        out_specs=(field, field, P(None, ("gx", "gy", "gz"))),
        check_vma=False,
    )
```

```python
import functools

import jax
import jax.numpy as jnp
from jax import lax
from jax.experimental import pallas as pl
from jax.experimental.pallas import tpu as pltpu
from jax.sharding import PartitionSpec as P

MESH = pl.DeviceIdType.MESH
F32 = jnp.float32
BF16 = jnp.bfloat16

DT = 0.5
FACE_AREA = 0.25
STEPS = 4
CX, CY, CZ = 4, 16, 128
SLOTS = 1024
TILE_DEV = 128
NGX, NGY, NGZ = 16, 8, 4
NY_CHIPS, NZ_HI, NZ_LO, CORES = 4, 4, 4, 2
NNEAR, NFAR = NY_CHIPS * CORES, NZ_HI * NZ_LO
LANES = 16 * NFAR

(XE, XQ, YE, YQ, ZE, ZQ, E_XZ, E_XY, E_YZ, E_YX, E_ZY, E_ZX) = range(12)
ROUTES = (
    (-1, 0, 0),
    (1, 0, 0),
    (0, -1, 0),
    (0, 1, 0),
    (0, 0, -1),
    (0, 0, 1),
    (1, 0, -1),
    (1, -1, 0),
    (0, 1, -1),
    (-1, 1, 0),
    (0, -1, 1),
    (-1, 0, 1),
)


def iota(shape, axis):
    return lax.broadcasted_iota(jnp.int32, shape, axis)


def dot(a, b, contract):
    return lax.dot_general(a, b, ((contract[:1], contract[1:]), ((), ())), preferred_element_type=F32)


def halves(x):
    high = x.astype(BF16)
    return high, (x - high.astype(F32)).astype(BF16)


def kernel(
    e_in,
    h_in,
    j_in,
    mat_in,
    cell_in,
    owner_in,
    tile_in,
    normal_in,
    sig_in,
    gam_in,
    pla_in,
    g_in,
    count_ref,
    e_out,
    h_out,
    force_out,
    e_ref,
    h_ref,
    j_ref,
    part,
    mat_ref,
    cell_ref,
    owner_ref,
    tile_ref,
    normal_ref,
    sig_ref,
    gam_ref,
    pla_ref,
    g_ref,
    force_ref,
    coef,
    tensor,
    sx,
    rx,
    sy,
    ry,
    sz,
    rz,
    sr,
    rr,
    bucket,
    lane_hot,
    tile_hot,
    stl,
    rtl,
    sval,
    rval,
    sdense,
    rdense,
    in_sem,
    out_sem,
    hs_sem,
    hr_sem,
    ts_sem,
    tr_sem,
    vs_sem,
    vr_sem,
    ds_sem,
    dr_sem,
):
    gx, gy, gz = lax.axis_index("gx"), lax.axis_index("gy"), lax.axis_index("gz")

    loads = [
        pltpu.make_async_copy(src, dst, in_sem.at[n])
        for n, (src, dst) in enumerate(
            (
                (e_in, e_ref),
                (h_in, h_ref),
                (j_in, j_ref),
                (mat_in, mat_ref),
                (sig_in, sig_ref),
                (gam_in, gam_ref),
                (pla_in, pla_ref),
                (g_in, g_ref),
                (cell_in, cell_ref),
                (owner_in, owner_ref),
                (tile_in, tile_ref),
                (normal_in, normal_ref),
            )
        )
    ]
    for load in loads:
        load.start()

    def at(dx, dy, dz):
        where = {}
        if dx:
            where["gx"] = lax.rem(gx + (dx + NGX), NGX)
        if dy:
            where["gy"] = gy + dy
        if dz:
            where["gz"] = lax.rem(gz + (dz + NGZ), NGZ)
        return where

    y_chip, z_hi = lax.div(gx, NZ_HI), lax.rem(gx, NZ_HI)
    z_lo, core = lax.div(gy, CORES), lax.rem(gy, CORES)
    near, far = y_chip * CORES + core, z_hi * NZ_LO + z_lo

    def near_at(n):
        return {"gx": lax.div(n, CORES) * NZ_HI + z_hi, "gy": z_lo * CORES + lax.rem(n, CORES)}

    def far_at(n):
        return {"gx": y_chip * NZ_HI + lax.div(n, NZ_LO), "gy": lax.rem(n, NZ_LO) * CORES + core}

    def sent(dy):
        return gy > 0 if dy < 0 else gy < NGY - 1

    def when(dy, do):
        if dy:
            pl.when(sent(dy))(do)
        else:
            do()

    @pl.when(gy == NGY - 1)
    def _():
        for step in range(STEPS):
            ry[step, 0:2] = jnp.zeros((2, CX, 1, CZ), F32)
            ry[step, 5] = jnp.zeros((CX, 1, CZ), F32)
            rr[step, 1] = jnp.zeros((1, CZ), F32)

    @pl.when(gy == 0)
    def _():
        for step in range(STEPS):
            ry[step, 2:5] = jnp.zeros((3, CX, 1, CZ), F32)
            rr[step, 2] = jnp.zeros((1, CZ), F32)

    barrier = pltpu.get_barrier_semaphore()

    def greet(where):
        pl.semaphore_signal(barrier, inc=1, device_id=where, device_id_type=MESH)

    for route in ROUTES:
        when(route[1], functools.partial(lambda r: greet(at(*r)), route))
    for d in range(1, NNEAR):
        greet(near_at(lax.rem(near + d, NNEAR)))
    for d in range(1, NFAR):
        greet(far_at(lax.rem(far + d, NFAR)))
    greeted = sum(route[1] == 0 for route in ROUTES) + NNEAR - 1 + NFAR - 1
    greeted = greeted + sum(route[1] < 0 for route in ROUTES) * jnp.where(gy > 0, 1, 0)
    greeted = greeted + sum(route[1] > 0 for route in ROUTES) * jnp.where(gy < NGY - 1, 1, 0)

    one, zero = jnp.float32(1.0), jnp.float32(0.0)
    low_x = jnp.where(gx > 0, one, zero)
    low_y = jnp.where(gy > 0, one, zero)
    low_z = jnp.where(gz > 0, one, zero)
    top_x = jnp.where(gx < NGX - 1, one, zero)
    top_y = jnp.where(gy < NGY - 1, one, zero)
    top_z = jnp.where(gz < NGZ - 1, one, zero)

    brick = (CX, CY, CZ)
    jj, kk = iota(brick, 1), iota(brick, 2)
    n_hot = (iota((16, 8, CZ), 0) == iota((16, 8, CZ), 2)).astype(F32)
    row_hot = (iota((CY, CZ), 0) == iota((CY, CZ), 1)).astype(F32)

    def y_next(f):
        return pltpu.roll(f, CY - 1, 1)

    def z_next(f):
        return pltpu.roll(f, CZ - 1, 2)

    def packed(columns):
        return jnp.sum(columns.reshape(16, 8, -1) * n_hot, axis=0)

    def unpacked(tile):
        return jnp.sum(tile[None] * n_hot, axis=2, keepdims=True).reshape(2, CX, CY, 1)

    def message(step, which):
        src, dst = {
            XE: (sx.at[step, 0], rx.at[step, 0]),
            XQ: (sx.at[step, 1], rx.at[step, 1]),
            YE: (sy.at[step, pl.ds(0, 2)], ry.at[step, pl.ds(0, 2)]),
            YQ: (sy.at[step, pl.ds(2, 2)], ry.at[step, pl.ds(2, 2)]),
            ZE: (sz.at[step, 0], rz.at[step, 0]),
            ZQ: (sz.at[step, 1], rz.at[step, 1]),
            E_XZ: (sr.at[step, 0], rr.at[step, 0]),
            E_XY: (sr.at[step, 1], rr.at[step, 1]),
            E_YX: (sr.at[step, 2], rr.at[step, 2]),
            E_ZX: (sr.at[step, 3], rr.at[step, 3]),
            E_YZ: (sy.at[step, 4], ry.at[step, 4]),
            E_ZY: (sy.at[step, 5], ry.at[step, 5]),
        }[which]
        return pltpu.make_async_remote_copy(
            src_ref=src,
            dst_ref=dst,
            send_sem=hs_sem.at[step, which],
            recv_sem=hr_sem.at[step, which],
            device_id=at(*ROUTES[which]),
            device_id_type=MESH,
        )

    def start(step, *which):
        for n in which:
            when(ROUTES[n][1], lambda n=n: message(step, n).start())

    def send(step):
        ex, ey, ez = e_ref[0], e_ref[1], e_ref[2]
        sx[step, 0, 0] = ey[0]
        sx[step, 0, 1] = ez[0]
        start(step, XE)
        nothing = jnp.zeros((1, CY, CZ), F32)
        last_y, last_z = jj == CY - 1, kk == CZ - 1
        y_ez = jnp.where(last_y, zero, y_next(ez))
        y_ex = jnp.where(last_y, zero, y_next(ex))
        z_ey = jnp.where(last_z, zero, z_next(ey))
        z_ex = jnp.where(last_z, zero, z_next(ex))
        x_ez = jnp.concatenate([ez[1:], nothing], 0)
        x_ey = jnp.concatenate([ey[1:], nothing], 0)
        hy = h_ref[1] - DT * ((z_ex - ex) - (x_ez - ez))
        hz = h_ref[2] - DT * ((x_ey - ey) - (y_ex - ex))
        sx[step, 1, 0] = hy[CX - 1]
        sx[step, 1, 1] = hz[CX - 1]
        start(step, XQ)
        sr[step, 0] = jnp.sum(ex[CX - 1, :, 0:1] * row_hot, axis=0, keepdims=True)
        sr[step, 1] = ex[CX - 1, 0:1, :]
        sr[step, 2] = ey[0, CY - 1 : CY, :]
        sr[step, 3] = jnp.sum(ez[0, :, CZ - 1 : CZ] * row_hot, axis=0, keepdims=True)
        start(step, E_XZ, E_ZX, E_XY, E_YX)
        hx = h_ref[0] - DT * ((y_ez - ez) - (z_ey - ey))
        part[0], part[1], part[2] = hx, hy, hz
        sy[step, 0] = ex[:, 0:1, :]
        sy[step, 1] = ez[:, 0:1, :]
        sy[step, 2] = hx[:, CY - 1 : CY, :]
        sy[step, 3] = hz[:, CY - 1 : CY, :]
        sy[step, 4] = ey[:, CY - 1 : CY, :]
        sy[step, 5] = ez[:, 0:1, :]
        start(step, YE, YQ, E_YZ, E_ZY)
        sz[step, 0] = packed(e_ref[0:2][:, :, :, 0:1])
        sz[step, 1] = packed(part[0:2][:, :, :, CZ - 1 : CZ])
        start(step, ZE, ZQ)

    def update(step):
        j_ref[...] = coef[2][None] * j_ref[...] + coef[3][None] * e_ref[...]
        ex, ey, ez = e_ref[0], e_ref[1], e_ref[2]
        for which in range(12):
            when(-ROUTES[which][1], lambda which=which: message(step, which).wait_recv())
        above_x = rx[step, 0] * top_x
        above_y = ry[step, 0:2] * top_y
        above_z = unpacked(rz[step, 0]) * top_z
        hx, hy, hz = part[0], part[1], part[2]
        last_y, last_z = jj == CY - 1, kk == CZ - 1
        hx = hx + jnp.where(last_z, DT * above_z[1], zero) - jnp.where(last_y, DT * above_y[1], zero)
        hy = hy - jnp.where(last_z, DT * above_z[0], zero)
        hz = hz + jnp.where(last_y, DT * above_y[0], zero)
        hy = jnp.concatenate([hy[: CX - 1], (hy[CX - 1] + DT * above_x[1])[None]], 0)
        hz = jnp.concatenate([hz[: CX - 1], (hz[CX - 1] - DT * above_x[0])[None]], 0)
        h_ref[0], h_ref[1], h_ref[2] = hx, hy, hz
        e_xz = jnp.sum(rr[step, 0] * row_hot, axis=1, keepdims=True) * top_z
        e_zx = jnp.sum(rr[step, 3] * row_hot, axis=1, keepdims=True) * top_x
        e_xy = rr[step, 1] * top_y
        e_yx = rr[step, 2] * top_x
        e_yz = ry[step, 4] * top_z
        e_zy = ry[step, 5] * top_y
        jr, kr = iota((CY, CZ), 0), iota((CY, CZ), 1)
        below_xy = rx[step, 1, 0] + DT * ez[0] - jnp.where(kr == CZ - 1, DT * e_xz, zero)
        below_xz = rx[step, 1, 1] - DT * ey[0] + jnp.where(jr == CY - 1, DT * e_xy, zero)
        ky = iota((CX, 1, CZ), 2)
        below_yx = ry[step, 2] - DT * ez[:, 0:1, :] + jnp.where(ky == CZ - 1, DT * e_yz[:, :, 0:1], zero)
        below_yz = ry[step, 3] + DT * ex[:, 0:1, :]
        below_yz = jnp.concatenate([below_yz[: CX - 1], (below_yz[CX - 1] - DT * e_yx)[None]], 0)
        below_z = unpacked(rz[step, 1])
        jz = iota((CX, CY, 1), 1)
        below_zx = below_z[0] + DT * ey[:, :, 0:1] - jnp.where(jz == CY - 1, DT * e_zy[:, :, CZ - 1 : CZ], zero)
        below_zy = below_z[1] - DT * ex[:, :, 0:1]
        below_zy = jnp.concatenate([below_zy[: CX - 1], (below_zy[CX - 1] + DT * e_zx)[None]], 0)

        first_y, first_z = jj == 0, kk == 0
        y_hx = jnp.where(first_y, low_y * below_yx, pltpu.roll(hx, 1, 1))
        y_hz = jnp.where(first_y, low_y * below_yz, pltpu.roll(hz, 1, 1))
        z_hx = jnp.where(first_z, low_z * below_zx, pltpu.roll(hx, 1, 2))
        z_hy = jnp.where(first_z, low_z * below_zy, pltpu.roll(hy, 1, 2))
        x_hy = jnp.concatenate([(low_x * below_xy)[None], hy[: CX - 1]], 0)
        x_hz = jnp.concatenate([(low_x * below_xz)[None], hz[: CX - 1]], 0)
        keep, gain = coef[0], coef[1]
        e_ref[0] = keep * ex + gain * (((hz - y_hz) - (hy - z_hy)) - j_ref[0])
        e_ref[1] = keep * ey + gain * (((hx - z_hx) - (hz - x_hz)) - j_ref[1])
        e_ref[2] = keep * ez + gain * (((hy - x_hy) - (hx - y_hx)) - j_ref[2])

    def stress(step):
        ex, ey, ez = e_ref[0], e_ref[1], e_ref[2]
        hx, hy, hz = h_ref[0], h_ref[1], h_ref[2]
        g = g_ref[step]
        xx, yy, zz = ex * ex + hx * hx, ey * ey + hy * hy, ez * ez + hz * hz
        energy = 0.5 * (xx + yy + zz)
        found = (xx - energy, ex * ey + hx * hy, ex * ez + hx * hz, yy - energy, ey * ez + hy * hz, zz - energy)
        for n, value in enumerate(found):
            tensor[n] = g * value if step == 0 else tensor[n] + g * value

    def ranks_and_buckets():
        owner = owner_ref[...]
        block = SLOTS // 4
        groups = NGX * NGY
        earlier = (iota((block, block), 0) < iota((block, block), 1)).astype(F32).astype(BF16)
        lane = iota((1, block), 1)
        before = jnp.zeros((groups, 1), F32)
        made = jnp.zeros((5 * NNEAR, LANES), F32)
        for b in range(4):
            cut = slice(b * block, (b + 1) * block)
            own = owner[:, cut]
            hot = (own == iota((groups, block), 0)).astype(F32)
            ahead = dot(hot.astype(BF16), earlier, (1, 0)) + before
            rank = jnp.sum(ahead * hot, axis=0, keepdims=True).astype(jnp.int32)
            before = before + jnp.sum(hot, axis=1, keepdims=True)
            place = rank * NFAR + (lax.shift_right_logical(own, 1) & (NFAR - 1))
            place_hot = (place == iota((LANES, block), 0)).astype(F32).astype(BF16)
            cell, normal = cell_ref[:, cut], normal_ref[:, cut]
            live = (lane + b * block < count_ref[0, 0, 0]).astype(F32)
            weight = live * (FACE_AREA * (1 - 2 * (normal & 1)).astype(F32))
            mine = lax.shift_right_logical(own, 5) * CORES + (own & 1) == iota((NNEAR, block), 0)
            entries = (
                (cell & 127).astype(F32),
                lax.shift_right_logical(cell, 7).astype(F32),
                weight,
                lax.shift_right_logical(normal, 1).astype(F32),
                tile_ref[:, cut].astype(F32),
            )
            rows = jnp.concatenate([jnp.where(mine, entry, zero) for entry in entries], 0)
            made = made + dot(rows.astype(BF16), place_hot, (1, 1))
        for n in range(5):
            bucket[n] = made[n * NNEAR : (n + 1) * NNEAR].reshape(NNEAR, 1, LANES)
        stl[...] = bucket[4]

    def to_near(src, dst, send, recv, d):
        n = lax.rem(near + d, NNEAR)
        return pltpu.make_async_remote_copy(
            src_ref=src.at[n],
            dst_ref=dst.at[near],
            send_sem=send.at[d],
            recv_sem=recv.at[d],
            device_id=near_at(n),
            device_id_type=MESH,
        )

    def from_near(src, dst, send, recv, d):
        n = lax.rem(near + NNEAR - d, NNEAR)
        return pltpu.make_async_remote_copy(
            src_ref=src.at[n],
            dst_ref=dst.at[n],
            send_sem=send.at[d],
            recv_sem=recv.at[d],
            device_id=near_at(n),
            device_id_type=MESH,
        )

    def lane_hots():
        for n in range(NNEAR):
            lane_hot[n] = (bucket[0, n] == iota((CZ, LANES), 0).astype(F32)).astype(F32).astype(BF16)

    def tile_hots():
        for d in range(1, NNEAR):
            from_near(stl, rtl, ts_sem, tr_sem, d).wait_recv()
        for n in range(NNEAR):
            tile_hot[n] = (rtl[n] == iota((TILE_DEV, LANES), 0).astype(F32)).astype(F32).astype(BF16)

    def coefficients():
        material = mat_ref[...]

        def of_material(table):
            result = jnp.where(material == 0, table[0], zero)
            for which in (1, 2):
                result = jnp.where(material == which, table[which], result)
            return result

        sigma, gamma, plasma = of_material(sig_ref), of_material(gam_ref), of_material(pla_ref)
        coef[0] = (1.0 - sigma * DT / 2) / (1.0 + sigma * DT / 2)
        coef[1] = DT / (1.0 + sigma * DT / 2)
        coef[2] = (1.0 - gamma * DT / 2) / (1.0 + gamma * DT / 2)
        coef[3] = plasma * DT / (1.0 + gamma * DT / 2)

    loads[0].wait()
    loads[1].wait()
    pl.semaphore_wait(barrier, greeted)

    for step in range(STEPS):
        send(step)
        if step == 0:
            for load in loads[2:]:
                load.wait()
            coefficients()
            ranks_and_buckets()
            for d in range(1, NNEAR):
                to_near(stl, rtl, ts_sem, tr_sem, d).start()
            rtl[near] = stl[near]
        else:
            stress(step - 1)
        if step == 1:
            lane_hots()
        if step == 2:
            tile_hots()
        update(step)
    stores = [
        pltpu.make_async_copy(src, dst, out_sem.at[n]) for n, (src, dst) in enumerate(((e_ref, e_out), (h_ref, h_out)))
    ]
    for store in stores:
        store.start()
    stress(STEPS - 1)

    cells = CX * CY
    high, low = halves(tensor[...].reshape(6 * cells, CZ))
    parts = jnp.concatenate([high, low], 1)
    for n in range(NNEAR):
        hot = lane_hot[n]
        read = dot(parts, jnp.concatenate([hot, hot], 0), (1, 0))
        row = bucket[1, n] == iota((cells, LANES), 0).astype(F32)
        xx, xy, xz, yy, yz, zz = [
            jnp.sum(jnp.where(row, read[c * cells : (c + 1) * cells], zero), axis=0, keepdims=True) for c in range(6)
        ]
        axis, weight = bucket[3, n], bucket[2, n]
        along_x, along_y = axis == 0.0, axis == 1.0
        sval[n, 0:1] = weight * jnp.where(along_x, xx, jnp.where(along_y, xy, xz))
        sval[n, 1:2] = weight * jnp.where(along_x, xy, jnp.where(along_y, yy, yz))
        sval[n, 2:3] = weight * jnp.where(along_x, xz, jnp.where(along_y, yz, zz))
    for d in range(1, NNEAR):
        to_near(sval, rval, vs_sem, vr_sem, d).start()
    rval[near] = sval[near]

    for d in range(1, NNEAR):
        from_near(sval, rval, vs_sem, vr_sem, d).wait_recv()
    row16 = iota((NFAR * 16, LANES), 0)
    mine = (lax.shift_right_logical(row16, 4) == (iota((NFAR * 16, LANES), 1) & (NFAR - 1))).astype(F32).astype(BF16)
    dense = jnp.zeros((NFAR * 16, TILE_DEV), F32)
    for n in range(NNEAR):
        value = jnp.concatenate([rval[n], jnp.zeros((5, LANES), F32)], 0)
        high = value.astype(BF16).astype(F32)
        both = jnp.concatenate([high, value - high], 0).astype(BF16)
        spread = jnp.concatenate([both] * NFAR, 0) * mine
        dense = dense + dot(spread, tile_hot[n], (1, 1))
    dense = dense.reshape(NFAR, 16, TILE_DEV)
    sdense[...] = (dense[:, 0:8] + dense[:, 8:16])[:, 0:3]

    def to_far(d):
        n = lax.rem(far + d, NFAR)
        return pltpu.make_async_remote_copy(
            src_ref=sdense.at[n],
            dst_ref=rdense.at[far],
            send_sem=ds_sem.at[d],
            recv_sem=dr_sem.at[d],
            device_id=far_at(n),
            device_id_type=MESH,
        )

    def from_far(d):
        n = lax.rem(far + NFAR - d, NFAR)
        return pltpu.make_async_remote_copy(
            src_ref=sdense.at[n],
            dst_ref=rdense.at[n],
            send_sem=ds_sem.at[d],
            recv_sem=dr_sem.at[d],
            device_id=far_at(n),
            device_id_type=MESH,
        )

    for d in range(1, NFAR):
        to_far(d).start()
    rdense[far] = sdense[far]
    for d in range(1, NFAR):
        from_far(d).wait_recv()
    force_ref[...] = jnp.sum(rdense[...], axis=0)

    for step in range(STEPS):
        for which in range(12):
            when(ROUTES[which][1], lambda which=which: message(step, which).wait_send())
    for d in range(1, NNEAR):
        to_near(stl, rtl, ts_sem, tr_sem, d).wait_send()
        to_near(sval, rval, vs_sem, vr_sem, d).wait_send()
    for d in range(1, NFAR):
        to_far(d).wait_send()
    last = pltpu.make_async_copy(force_ref, force_out, out_sem.at[2])
    last.start()
    for store in [*stores, last]:
        store.wait()


def hand_out(*refs):
    sem = refs[-1]
    copies = [pltpu.make_async_copy(refs[n], refs[n + 3], sem.at[n]) for n in range(3)]
    for copy in copies:
        copy.start()
    for copy in copies:
        copy.wait()


def local(
    e_field,
    h_field,
    current,
    material,
    sigma_table,
    gamma_table,
    plasma_table,
    g_kernel,
    surf_cell,
    surf_owner,
    surf_tile,
    surf_normal,
    row_count,
):
    field = jax.ShapeDtypeStruct((3, CX, CY, CZ), F32)
    hbm = pl.BlockSpec(memory_space=pltpu.HBM)
    dma = pltpu.SemaphoreType.DMA
    slots = [a.reshape(1, SLOTS) for a in (surf_cell, surf_owner, surf_tile, surf_normal)]
    operands = (e_field, h_field, current, material, *slots)
    operands += (sigma_table, gamma_table, plasma_table, g_kernel)
    operands = [pltpu.with_memory_space_constraint(a, pltpu.HBM) for a in operands]
    shapes = (field, field, jax.ShapeDtypeStruct((3, TILE_DEV), F32))
    made = pl.pallas_call(
        kernel,
        out_shape=shapes,
        in_specs=[hbm] * 12 + [pl.BlockSpec(memory_space=pltpu.SMEM)],
        out_specs=(hbm, hbm, hbm),
        scratch_shapes=[
            pltpu.VMEM((3, CX, CY, CZ), F32),
            pltpu.VMEM((3, CX, CY, CZ), F32),
            pltpu.VMEM((3, CX, CY, CZ), F32),
            pltpu.VMEM((3, CX, CY, CZ), F32),
            pltpu.VMEM((CX, CY, CZ), jnp.int32),
            pltpu.VMEM((1, SLOTS), jnp.int32),
            pltpu.VMEM((1, SLOTS), jnp.int32),
            pltpu.VMEM((1, SLOTS), jnp.int32),
            pltpu.VMEM((1, SLOTS), jnp.int32),
            pltpu.SMEM((3,), F32),
            pltpu.SMEM((3,), F32),
            pltpu.SMEM((3,), F32),
            pltpu.SMEM((STEPS,), F32),
            pltpu.VMEM((3, TILE_DEV), F32),
            pltpu.VMEM((4, CX, CY, CZ), F32),
            pltpu.VMEM((6, CX, CY, CZ), F32),
            pltpu.VMEM((STEPS, 2, 2, CY, CZ), F32),
            pltpu.VMEM((STEPS, 2, 2, CY, CZ), F32),
            pltpu.VMEM((STEPS, 6, CX, 1, CZ), F32),
            pltpu.VMEM((STEPS, 6, CX, 1, CZ), F32),
            pltpu.VMEM((STEPS, 2, 8, CZ), F32),
            pltpu.VMEM((STEPS, 2, 8, CZ), F32),
            pltpu.VMEM((STEPS, 4, 1, CZ), F32),
            pltpu.VMEM((STEPS, 4, 1, CZ), F32),
            pltpu.VMEM((5, NNEAR, 1, LANES), F32),
            pltpu.VMEM((NNEAR, CZ, LANES), BF16),
            pltpu.VMEM((NNEAR, TILE_DEV, LANES), BF16),
            pltpu.VMEM((NNEAR, 1, LANES), F32),
            pltpu.VMEM((NNEAR, 1, LANES), F32),
            pltpu.VMEM((NNEAR, 3, LANES), F32),
            pltpu.VMEM((NNEAR, 3, LANES), F32),
            pltpu.VMEM((NFAR, 3, TILE_DEV), F32),
            pltpu.VMEM((NFAR, 3, TILE_DEV), F32),
            dma((12,)),
            dma((3,)),
            dma((STEPS, 12)),
            dma((STEPS, 12)),
            dma((NNEAR,)),
            dma((NNEAR,)),
            dma((NNEAR,)),
            dma((NNEAR,)),
            dma((NFAR,)),
            dma((NFAR,)),
        ],
        compiler_params=pltpu.CompilerParams(
            collective_id=0, has_side_effects=True, vmem_limit_bytes=24 * 2**20
        ),
    )(*operands, row_count)
    return pl.pallas_call(
        hand_out,
        out_shape=shapes,
        in_specs=[hbm] * 3,
        out_specs=(hbm,) * 3,
        scratch_shapes=[dma((3,))],
        compiler_params=pltpu.CompilerParams(vmem_limit_bytes=24 * 2**20),
    )(*made)


def solution(mesh):
    cells = P("gx", "gy", "gz")
    field = P(None, "gx", "gy", "gz")
    slots = P("gx", "gy", "gz", None)
    return jax.shard_map(
        local,
        mesh=mesh,
        in_specs=(
            field,
            field,
            field,
            cells,
            P(),
            P(),
            P(),
            P(),
            slots,
            P("gx", "gy", "gz", None, None),
            slots,
            slots,
            cells,
        ),
        out_specs=(field, field, P(None, ("gx", "gy", "gz"))),
        check_vma=False,
    )
```

```python
import functools

import jax
import jax.numpy as jnp
from jax import lax
from jax.experimental import pallas as pl
from jax.experimental.pallas import tpu as pltpu
from jax.sharding import PartitionSpec as P

MESH = pl.DeviceIdType.MESH
F32 = jnp.float32
BF16 = jnp.bfloat16

DT = 0.5
FACE_AREA = 0.25
STEPS = 4
CX, CY, CZ = 4, 16, 128
SLOTS = 1024
TILE_DEV = 128
NGX, NGY, NGZ = 16, 8, 4
NY_CHIPS, NZ_HI, NZ_LO, CORES = 4, 4, 4, 2
NNEAR, NFAR = NY_CHIPS * CORES, NZ_HI * NZ_LO
LANES = 16 * NFAR

(XE, XQ, YE, YQ, ZE, ZQ, E_XZ, E_XY, E_YZ, E_YX, E_ZY, E_ZX) = range(12)
ROUTES = (
    (-1, 0, 0),
    (1, 0, 0),
    (0, -1, 0),
    (0, 1, 0),
    (0, 0, -1),
    (0, 0, 1),
    (1, 0, -1),
    (1, -1, 0),
    (0, 1, -1),
    (-1, 1, 0),
    (0, -1, 1),
    (-1, 0, 1),
)


def iota(shape, axis):
    return lax.broadcasted_iota(jnp.int32, shape, axis)


def dot(a, b, contract):
    return lax.dot_general(a, b, ((contract[:1], contract[1:]), ((), ())), preferred_element_type=F32)


def halves(x):
    high = x.astype(BF16)
    return high, (x - high.astype(F32)).astype(BF16)


def kernel(
    e_in,
    h_in,
    j_in,
    mat_in,
    cell_in,
    owner_in,
    tile_in,
    normal_in,
    sig_in,
    gam_in,
    pla_in,
    g_in,
    count_ref,
    e_out,
    h_out,
    force_out,
    e_ref,
    h_ref,
    j_ref,
    part,
    mat_ref,
    cell_ref,
    owner_ref,
    tile_ref,
    normal_ref,
    sig_ref,
    gam_ref,
    pla_ref,
    g_ref,
    force_ref,
    coef,
    tensor,
    sx,
    rx,
    sy,
    ry,
    sz,
    rz,
    sr,
    rr,
    bucket,
    lane_hot,
    tile_hot,
    stl,
    rtl,
    sval,
    rval,
    sdense,
    rdense,
    in_sem,
    out_sem,
    hs_sem,
    hr_sem,
    ts_sem,
    tr_sem,
    vs_sem,
    vr_sem,
    ds_sem,
    dr_sem,
):
    gx, gy, gz = lax.axis_index("gx"), lax.axis_index("gy"), lax.axis_index("gz")

    loads = [
        pltpu.make_async_copy(src, dst, in_sem.at[n])
        for n, (src, dst) in enumerate(
            (
                (e_in, e_ref),
                (h_in, h_ref),
                (j_in, j_ref),
                (mat_in, mat_ref),
                (sig_in, sig_ref),
                (gam_in, gam_ref),
                (pla_in, pla_ref),
                (g_in, g_ref),
                (cell_in, cell_ref),
                (owner_in, owner_ref),
                (tile_in, tile_ref),
                (normal_in, normal_ref),
            )
        )
    ]
    for load in loads:
        load.start()

    def at(dx, dy, dz):
        where = {}
        if dx:
            where["gx"] = lax.rem(gx + (dx + NGX), NGX)
        if dy:
            where["gy"] = gy + dy
        if dz:
            where["gz"] = lax.rem(gz + (dz + NGZ), NGZ)
        return where

    y_chip, z_hi = lax.div(gx, NZ_HI), lax.rem(gx, NZ_HI)
    z_lo, core = lax.div(gy, CORES), lax.rem(gy, CORES)
    near, far = y_chip * CORES + core, z_hi * NZ_LO + z_lo

    def near_at(n):
        return {"gx": lax.div(n, CORES) * NZ_HI + z_hi, "gy": z_lo * CORES + lax.rem(n, CORES)}

    def far_at(n):
        return {"gx": y_chip * NZ_HI + lax.div(n, NZ_LO), "gy": lax.rem(n, NZ_LO) * CORES + core}

    def sent(dy):
        return gy > 0 if dy < 0 else gy < NGY - 1

    def when(dy, do):
        if dy:
            pl.when(sent(dy))(do)
        else:
            do()

    @pl.when(gy == NGY - 1)
    def _():
        for step in range(STEPS):
            ry[step, 0:2] = jnp.zeros((2, CX, 1, CZ), F32)
            ry[step, 5] = jnp.zeros((CX, 1, CZ), F32)
            rr[step, 1] = jnp.zeros((1, CZ), F32)

    @pl.when(gy == 0)
    def _():
        for step in range(STEPS):
            ry[step, 2:5] = jnp.zeros((3, CX, 1, CZ), F32)
            rr[step, 2] = jnp.zeros((1, CZ), F32)

    barrier = pltpu.get_barrier_semaphore()

    def greet(where):
        pl.semaphore_signal(barrier, inc=1, device_id=where, device_id_type=MESH)

    for route in ROUTES:
        when(route[1], functools.partial(lambda r: greet(at(*r)), route))
    for d in range(1, NNEAR):
        greet(near_at(lax.rem(near + d, NNEAR)))
    for d in range(1, NFAR):
        greet(far_at(lax.rem(far + d, NFAR)))
    greeted = sum(route[1] == 0 for route in ROUTES) + NNEAR - 1 + NFAR - 1
    greeted = greeted + sum(route[1] < 0 for route in ROUTES) * jnp.where(gy > 0, 1, 0)
    greeted = greeted + sum(route[1] > 0 for route in ROUTES) * jnp.where(gy < NGY - 1, 1, 0)

    one, zero = jnp.float32(1.0), jnp.float32(0.0)
    low_x = jnp.where(gx > 0, one, zero)
    low_y = jnp.where(gy > 0, one, zero)
    low_z = jnp.where(gz > 0, one, zero)
    top_x = jnp.where(gx < NGX - 1, one, zero)
    top_y = jnp.where(gy < NGY - 1, one, zero)
    top_z = jnp.where(gz < NGZ - 1, one, zero)

    brick = (CX, CY, CZ)
    jj, kk = iota(brick, 1), iota(brick, 2)
    n_hot = (iota((16, 8, CZ), 0) == iota((16, 8, CZ), 2)).astype(F32)
    row_hot = (iota((CY, CZ), 0) == iota((CY, CZ), 1)).astype(F32)

    def y_next(f):
        return pltpu.roll(f, CY - 1, 1)

    def z_next(f):
        return pltpu.roll(f, CZ - 1, 2)

    def packed(columns):
        return jnp.sum(columns.reshape(16, 8, -1) * n_hot, axis=0)

    def unpacked(tile):
        return jnp.sum(tile[None] * n_hot, axis=2, keepdims=True).reshape(2, CX, CY, 1)

    def message(step, which):
        src, dst = {
            XE: (sx.at[step, 0], rx.at[step, 0]),
            XQ: (sx.at[step, 1], rx.at[step, 1]),
            YE: (sy.at[step, pl.ds(0, 2)], ry.at[step, pl.ds(0, 2)]),
            YQ: (sy.at[step, pl.ds(2, 2)], ry.at[step, pl.ds(2, 2)]),
            ZE: (sz.at[step, 0], rz.at[step, 0]),
            ZQ: (sz.at[step, 1], rz.at[step, 1]),
            E_XZ: (sr.at[step, 0], rr.at[step, 0]),
            E_XY: (sr.at[step, 1], rr.at[step, 1]),
            E_YX: (sr.at[step, 2], rr.at[step, 2]),
            E_ZX: (sr.at[step, 3], rr.at[step, 3]),
            E_YZ: (sy.at[step, 4], ry.at[step, 4]),
            E_ZY: (sy.at[step, 5], ry.at[step, 5]),
        }[which]
        return pltpu.make_async_remote_copy(
            src_ref=src,
            dst_ref=dst,
            send_sem=hs_sem.at[step, which],
            recv_sem=hr_sem.at[step, which],
            device_id=at(*ROUTES[which]),
            device_id_type=MESH,
        )

    def start(step, *which):
        for n in which:
            when(ROUTES[n][1], lambda n=n: message(step, n).start())

    def send_x(step):
        ex, ey, ez = e_ref[0], e_ref[1], e_ref[2]
        sr[step, 0] = jnp.sum(ex[CX - 1, :, 0:1] * row_hot, axis=0, keepdims=True)
        sr[step, 3] = jnp.sum(ez[0, :, CZ - 1 : CZ] * row_hot, axis=0, keepdims=True)
        start(step, E_XZ, E_ZX)
        sx[step, 0, 0] = ey[0]
        sx[step, 0, 1] = ez[0]
        start(step, XE)
        ex, ey, ez = ex[CX - 1], ey[CX - 1], ez[CX - 1]
        y_ex = jnp.where(jj[0] == CY - 1, zero, pltpu.roll(ex, CY - 1, 0))
        z_ex = jnp.where(kk[0] == CZ - 1, zero, pltpu.roll(ex, CZ - 1, 1))
        sx[step, 1, 0] = h_ref[1, CX - 1] - DT * ((z_ex - ex) + ez)
        sx[step, 1, 1] = h_ref[2, CX - 1] + DT * (ey + (y_ex - ex))
        start(step, XQ)
        sr[step, 1] = ex[0:1, :]
        sr[step, 2] = e_ref[1, 0, CY - 1 : CY, :]
        start(step, E_XY, E_YX)

    def send_yz(step):
        ex, ey, ez = e_ref[0], e_ref[1], e_ref[2]
        nothing = jnp.zeros((1, CY, CZ), F32)
        last_y, last_z = jj == CY - 1, kk == CZ - 1
        y_ez = jnp.where(last_y, zero, y_next(ez))
        y_ex = jnp.where(last_y, zero, y_next(ex))
        z_ey = jnp.where(last_z, zero, z_next(ey))
        z_ex = jnp.where(last_z, zero, z_next(ex))
        x_ez = jnp.concatenate([ez[1:], nothing], 0)
        x_ey = jnp.concatenate([ey[1:], nothing], 0)
        hx = h_ref[0] - DT * ((y_ez - ez) - (z_ey - ey))
        hy = h_ref[1] - DT * ((z_ex - ex) - (x_ez - ez))
        hz = h_ref[2] - DT * ((x_ey - ey) - (y_ex - ex))
        part[0], part[1], part[2] = hx, hy, hz
        sz[step, 0] = packed(e_ref[0:2][:, :, :, 0:1])
        sz[step, 1] = packed(part[0:2][:, :, :, CZ - 1 : CZ])
        start(step, ZE, ZQ)
        sy[step, 0] = ex[:, 0:1, :]
        sy[step, 1] = ez[:, 0:1, :]
        sy[step, 2] = hx[:, CY - 1 : CY, :]
        sy[step, 3] = hz[:, CY - 1 : CY, :]
        sy[step, 4] = ey[:, CY - 1 : CY, :]
        sy[step, 5] = ez[:, 0:1, :]
        start(step, YE, YQ, E_YZ, E_ZY)

    def wait(step, *which):
        for n in which:
            when(-ROUTES[n][1], lambda n=n: message(step, n).wait_recv())

    def current(step):
        j_ref[...] = coef[2][None] * j_ref[...] + coef[3][None] * e_ref[...]

    def update(step):
        last = CX - 1
        wait(step, ZE, ZQ, YE, YQ, E_YZ, E_ZY)
        ex, ey, ez = e_ref[0], e_ref[1], e_ref[2]
        hx, hy, hz = part[0], part[1], part[2]
        above_y = ry[step, 0:2]
        above_z = unpacked(rz[step, 0]) * top_z
        last_y, last_z = jj == CY - 1, kk == CZ - 1
        hx = hx + jnp.where(last_z, DT * above_z[1], zero) - jnp.where(last_y, DT * above_y[1], zero)
        hy = hy - jnp.where(last_z, DT * above_z[0], zero)
        hz = hz + jnp.where(last_y, DT * above_y[0], zero)
        e_yz = ry[step, 4] * top_z
        e_zy = ry[step, 5]
        ky, jz = iota((CX, 1, CZ), 2), iota((CX, CY, 1), 1)
        below_yx = ry[step, 2] - DT * ez[:, 0:1, :] + jnp.where(ky == CZ - 1, DT * e_yz[:, :, 0:1], zero)
        below_yz = ry[step, 3] + DT * ex[:, 0:1, :]
        below_z = unpacked(rz[step, 1])
        below_zx = below_z[0] + DT * ey[:, :, 0:1] - jnp.where(jz == CY - 1, DT * e_zy[:, :, CZ - 1 : CZ], zero)
        below_zy = below_z[1] - DT * ex[:, :, 0:1]
        first_y, first_z = jj == 0, kk == 0
        y_hx = jnp.where(first_y, low_y * below_yx, pltpu.roll(hx, 1, 1))
        y_hz = jnp.where(first_y, low_y * below_yz, pltpu.roll(hz, 1, 1))
        z_hx = jnp.where(first_z, low_z * below_zx, pltpu.roll(hx, 1, 2))
        z_hy = jnp.where(first_z, low_z * below_zy, pltpu.roll(hy, 1, 2))
        nothing = jnp.zeros((1, CY, CZ), F32)
        x_hy = jnp.concatenate([nothing, hy[:last]], 0)
        x_hz = jnp.concatenate([nothing, hz[:last]], 0)
        keep, gain = coef[0], coef[1]
        part[0] = keep * ex + gain * (((hz - y_hz) - (hy - z_hy)) - j_ref[0])
        part[1] = keep * ey + gain * (((hx - z_hx) - (hz - x_hz)) - j_ref[1])
        part[2] = keep * ez + gain * (((hy - x_hy) - (hx - y_hx)) - j_ref[2])
        h_ref[0], h_ref[1], h_ref[2] = hx, hy, hz

        wait(step, E_XY, E_YX, XE, XQ)
        jr, kr = jj[0], kk[0]
        more_y = (DT * top_x) * rx[step, 0, 1]
        more_z = (-DT * top_x) * rx[step, 0, 0]
        e_yx = rr[step, 2] * top_x
        h_ref[1, last] = h_ref[1, last] + more_y
        h_ref[2, last] = h_ref[2, last] + more_z
        y_more_z = jnp.where(jr == 0, (-DT * low_y) * e_yx, pltpu.roll(more_z, 1, 0))
        z_more_y = jnp.where(kr == 0, zero, pltpu.roll(more_y, 1, 1))
        gain = coef[1, last]
        e_ref[0, 0:last] = part[0, 0:last]
        e_ref[1, 1:last] = part[1, 1:last]
        e_ref[2, 1:last] = part[2, 1:last]
        x_last = part[0, last] + gain * ((more_z - y_more_z) - (more_y - z_more_y))
        e_ref[1, last] = part[1, last] - gain * more_z
        e_ref[2, last] = part[2, last] + gain * more_y
        below_xy = rx[step, 1, 0] + DT * e_ref[2, 0]
        below_xz = rx[step, 1, 1] - DT * e_ref[1, 0] + jnp.where(jr == CY - 1, DT * rr[step, 1], zero)
        gain_0 = low_x * coef[1, 0]
        z_first = part[2, 0] - gain_0 * below_xy
        e_ref[1, 0] = part[1, 0] + gain_0 * below_xz

        wait(step, E_XZ, E_ZX)
        e_xz = jnp.sum(rr[step, 0] * row_hot, axis=1, keepdims=True) * (DT * top_z)
        e_zx = jnp.sum(rr[step, 3] * row_hot, axis=1, keepdims=True) * (DT * top_x * low_z)
        e_ref[2, 0] = z_first + jnp.where(kr == CZ - 1, gain_0 * e_xz, zero)
        e_ref[0, last] = x_last + jnp.where(kr == 0, gain * e_zx, zero)

    def stress(step):
        ex, ey, ez = e_ref[0], e_ref[1], e_ref[2]
        hx, hy, hz = h_ref[0], h_ref[1], h_ref[2]
        g = g_ref[step]
        xx, yy, zz = ex * ex + hx * hx, ey * ey + hy * hy, ez * ez + hz * hz
        energy = 0.5 * (xx + yy + zz)
        found = (xx - energy, ex * ey + hx * hy, ex * ez + hx * hz, yy - energy, ey * ez + hy * hz, zz - energy)
        for n, value in enumerate(found):
            tensor[n] = g * value if step == 0 else tensor[n] + g * value

    def ranks_and_buckets():
        owner = owner_ref[...]
        block = SLOTS // 4
        groups = NGX * NGY
        earlier = (iota((block, block), 0) < iota((block, block), 1)).astype(F32).astype(BF16)
        lane = iota((1, block), 1)
        before = jnp.zeros((groups, 1), F32)
        made = jnp.zeros((5 * NNEAR, LANES), F32)
        for b in range(4):
            cut = slice(b * block, (b + 1) * block)
            own = owner[:, cut]
            hot = (own == iota((groups, block), 0)).astype(F32)
            ahead = dot(hot.astype(BF16), earlier, (1, 0)) + before
            rank = jnp.sum(ahead * hot, axis=0, keepdims=True).astype(jnp.int32)
            before = before + jnp.sum(hot, axis=1, keepdims=True)
            place = rank * NFAR + (lax.shift_right_logical(own, 1) & (NFAR - 1))
            place_hot = (place == iota((LANES, block), 0)).astype(F32).astype(BF16)
            cell, normal = cell_ref[:, cut], normal_ref[:, cut]
            live = (lane + b * block < count_ref[0, 0, 0]).astype(F32)
            weight = live * (FACE_AREA * (1 - 2 * (normal & 1)).astype(F32))
            mine = lax.shift_right_logical(own, 5) * CORES + (own & 1) == iota((NNEAR, block), 0)
            entries = (
                (cell & 127).astype(F32),
                lax.shift_right_logical(cell, 7).astype(F32),
                weight,
                lax.shift_right_logical(normal, 1).astype(F32),
                tile_ref[:, cut].astype(F32),
            )
            rows = jnp.concatenate([jnp.where(mine, entry, zero) for entry in entries], 0)
            made = made + dot(rows.astype(BF16), place_hot, (1, 1))
        for n in range(5):
            bucket[n] = made[n * NNEAR : (n + 1) * NNEAR].reshape(NNEAR, 1, LANES)
        stl[...] = bucket[4]

    def to_near(src, dst, send, recv, d):
        n = lax.rem(near + d, NNEAR)
        return pltpu.make_async_remote_copy(
            src_ref=src.at[n],
            dst_ref=dst.at[near],
            send_sem=send.at[d],
            recv_sem=recv.at[d],
            device_id=near_at(n),
            device_id_type=MESH,
        )

    def from_near(src, dst, send, recv, d):
        n = lax.rem(near + NNEAR - d, NNEAR)
        return pltpu.make_async_remote_copy(
            src_ref=src.at[n],
            dst_ref=dst.at[n],
            send_sem=send.at[d],
            recv_sem=recv.at[d],
            device_id=near_at(n),
            device_id_type=MESH,
        )

    def lane_hots():
        for n in range(NNEAR):
            lane_hot[n] = (bucket[0, n] == iota((CZ, LANES), 0).astype(F32)).astype(F32).astype(BF16)

    def tile_hots():
        for d in range(1, NNEAR):
            from_near(stl, rtl, ts_sem, tr_sem, d).wait_recv()
        for n in range(NNEAR):
            tile_hot[n] = (rtl[n] == iota((TILE_DEV, LANES), 0).astype(F32)).astype(F32).astype(BF16)

    def coefficients():
        material = mat_ref[...]

        def of_material(table):
            result = jnp.where(material == 0, table[0], zero)
            for which in (1, 2):
                result = jnp.where(material == which, table[which], result)
            return result

        sigma, gamma, plasma = of_material(sig_ref), of_material(gam_ref), of_material(pla_ref)
        coef[0] = (1.0 - sigma * DT / 2) / (1.0 + sigma * DT / 2)
        coef[1] = DT / (1.0 + sigma * DT / 2)
        coef[2] = (1.0 - gamma * DT / 2) / (1.0 + gamma * DT / 2)
        coef[3] = plasma * DT / (1.0 + gamma * DT / 2)

    loads[0].wait()
    loads[1].wait()
    pl.semaphore_wait(barrier, greeted)

    for step in range(STEPS):
        send_x(step)
        send_yz(step)
        if step == 0:
            for load in loads[2:]:
                load.wait()
            coefficients()
            current(step)
            ranks_and_buckets()
            for d in range(1, NNEAR):
                to_near(stl, rtl, ts_sem, tr_sem, d).start()
            rtl[near] = stl[near]
        else:
            current(step)
            stress(step - 1)
        if step == 1:
            lane_hots()
        if step == 2:
            tile_hots()
        update(step)
    stores = [
        pltpu.make_async_copy(src, dst, out_sem.at[n]) for n, (src, dst) in enumerate(((e_ref, e_out), (h_ref, h_out)))
    ]
    for store in stores:
        store.start()
    stress(STEPS - 1)

    cells = CX * CY
    high, low = halves(tensor[...].reshape(6 * cells, CZ))
    parts = jnp.concatenate([high, low], 1)
    for n in range(NNEAR):
        hot = lane_hot[n]
        read = dot(parts, jnp.concatenate([hot, hot], 0), (1, 0))
        row = bucket[1, n] == iota((cells, LANES), 0).astype(F32)
        xx, xy, xz, yy, yz, zz = [
            jnp.sum(jnp.where(row, read[c * cells : (c + 1) * cells], zero), axis=0, keepdims=True) for c in range(6)
        ]
        axis, weight = bucket[3, n], bucket[2, n]
        along_x, along_y = axis == 0.0, axis == 1.0
        sval[n, 0:1] = weight * jnp.where(along_x, xx, jnp.where(along_y, xy, xz))
        sval[n, 1:2] = weight * jnp.where(along_x, xy, jnp.where(along_y, yy, yz))
        sval[n, 2:3] = weight * jnp.where(along_x, xz, jnp.where(along_y, yz, zz))
    for d in range(1, NNEAR):
        to_near(sval, rval, vs_sem, vr_sem, d).start()
    rval[near] = sval[near]

    for d in range(1, NNEAR):
        from_near(sval, rval, vs_sem, vr_sem, d).wait_recv()
    rows = (NFAR * 8, LANES)
    mine = (lax.shift_right_logical(iota(rows, 0), 3) == (iota(rows, 1) & (NFAR - 1))).astype(F32)
    dense = jnp.zeros((NFAR * 8, TILE_DEV), F32)
    for n in range(NNEAR):
        value = rval[n]
        high = value.astype(BF16).astype(F32)
        both = jnp.concatenate([high, value - high, jnp.zeros((2, LANES), F32)], 0)
        spread = (jnp.concatenate([both] * NFAR, 0) * mine).astype(BF16)
        dense = dense + dot(spread, tile_hot[n], (1, 1))
    dense = dense.reshape(NFAR, 8, TILE_DEV)
    sdense[...] = dense[:, 0:3] + dense[:, 3:6]

    def to_far(d):
        n = lax.rem(far + d, NFAR)
        return pltpu.make_async_remote_copy(
            src_ref=sdense.at[n],
            dst_ref=rdense.at[far],
            send_sem=ds_sem.at[d],
            recv_sem=dr_sem.at[d],
            device_id=far_at(n),
            device_id_type=MESH,
        )

    def from_far(d):
        n = lax.rem(far + NFAR - d, NFAR)
        return pltpu.make_async_remote_copy(
            src_ref=sdense.at[n],
            dst_ref=rdense.at[n],
            send_sem=ds_sem.at[d],
            recv_sem=dr_sem.at[d],
            device_id=far_at(n),
            device_id_type=MESH,
        )

    for d in range(1, NFAR):
        to_far(d).start()
    rdense[far] = sdense[far]
    for d in range(1, NFAR):
        from_far(d).wait_recv()
    force_ref[...] = jnp.sum(rdense[...], axis=0)

    for step in range(STEPS):
        for which in range(12):
            when(ROUTES[which][1], lambda which=which: message(step, which).wait_send())
    for d in range(1, NNEAR):
        to_near(stl, rtl, ts_sem, tr_sem, d).wait_send()
        to_near(sval, rval, vs_sem, vr_sem, d).wait_send()
    for d in range(1, NFAR):
        to_far(d).wait_send()
    last = pltpu.make_async_copy(force_ref, force_out, out_sem.at[2])
    last.start()
    for store in [*stores, last]:
        store.wait()


def hand_out(*refs):
    sem = refs[-1]
    copies = [pltpu.make_async_copy(refs[n], refs[n + 3], sem.at[n]) for n in range(3)]
    for copy in copies:
        copy.start()
    for copy in copies:
        copy.wait()


def local(
    e_field,
    h_field,
    current,
    material,
    sigma_table,
    gamma_table,
    plasma_table,
    g_kernel,
    surf_cell,
    surf_owner,
    surf_tile,
    surf_normal,
    row_count,
):
    field = jax.ShapeDtypeStruct((3, CX, CY, CZ), F32)
    hbm = pl.BlockSpec(memory_space=pltpu.HBM)
    dma = pltpu.SemaphoreType.DMA
    slots = [a.reshape(1, SLOTS) for a in (surf_cell, surf_owner, surf_tile, surf_normal)]
    operands = (e_field, h_field, current, material, *slots)
    operands += (sigma_table, gamma_table, plasma_table, g_kernel)
    operands = [pltpu.with_memory_space_constraint(a, pltpu.HBM) for a in operands]
    shapes = (field, field, jax.ShapeDtypeStruct((3, TILE_DEV), F32))
    made = pl.pallas_call(
        kernel,
        out_shape=shapes,
        in_specs=[hbm] * 12 + [pl.BlockSpec(memory_space=pltpu.SMEM)],
        out_specs=(hbm, hbm, hbm),
        scratch_shapes=[
            pltpu.VMEM((3, CX, CY, CZ), F32),
            pltpu.VMEM((3, CX, CY, CZ), F32),
            pltpu.VMEM((3, CX, CY, CZ), F32),
            pltpu.VMEM((3, CX, CY, CZ), F32),
            pltpu.VMEM((CX, CY, CZ), jnp.int32),
            pltpu.VMEM((1, SLOTS), jnp.int32),
            pltpu.VMEM((1, SLOTS), jnp.int32),
            pltpu.VMEM((1, SLOTS), jnp.int32),
            pltpu.VMEM((1, SLOTS), jnp.int32),
            pltpu.SMEM((3,), F32),
            pltpu.SMEM((3,), F32),
            pltpu.SMEM((3,), F32),
            pltpu.SMEM((STEPS,), F32),
            pltpu.VMEM((3, TILE_DEV), F32),
            pltpu.VMEM((4, CX, CY, CZ), F32),
            pltpu.VMEM((6, CX, CY, CZ), F32),
            pltpu.VMEM((STEPS, 2, 2, CY, CZ), F32),
            pltpu.VMEM((STEPS, 2, 2, CY, CZ), F32),
            pltpu.VMEM((STEPS, 6, CX, 1, CZ), F32),
            pltpu.VMEM((STEPS, 6, CX, 1, CZ), F32),
            pltpu.VMEM((STEPS, 2, 8, CZ), F32),
            pltpu.VMEM((STEPS, 2, 8, CZ), F32),
            pltpu.VMEM((STEPS, 4, 1, CZ), F32),
            pltpu.VMEM((STEPS, 4, 1, CZ), F32),
            pltpu.VMEM((5, NNEAR, 1, LANES), F32),
            pltpu.VMEM((NNEAR, CZ, LANES), BF16),
            pltpu.VMEM((NNEAR, TILE_DEV, LANES), BF16),
            pltpu.VMEM((NNEAR, 1, LANES), F32),
            pltpu.VMEM((NNEAR, 1, LANES), F32),
            pltpu.VMEM((NNEAR, 3, LANES), F32),
            pltpu.VMEM((NNEAR, 3, LANES), F32),
            pltpu.VMEM((NFAR, 3, TILE_DEV), F32),
            pltpu.VMEM((NFAR, 3, TILE_DEV), F32),
            dma((12,)),
            dma((3,)),
            dma((STEPS, 12)),
            dma((STEPS, 12)),
            dma((NNEAR,)),
            dma((NNEAR,)),
            dma((NNEAR,)),
            dma((NNEAR,)),
            dma((NFAR,)),
            dma((NFAR,)),
        ],
        compiler_params=pltpu.CompilerParams(
            collective_id=0, has_side_effects=True, vmem_limit_bytes=24 * 2**20
        ),
    )(*operands, row_count)
    return pl.pallas_call(
        hand_out,
        out_shape=shapes,
        in_specs=[hbm] * 3,
        out_specs=(hbm,) * 3,
        scratch_shapes=[dma((3,))],
        compiler_params=pltpu.CompilerParams(vmem_limit_bytes=24 * 2**20),
    )(*made)


def solution(mesh):
    cells = P("gx", "gy", "gz")
    field = P(None, "gx", "gy", "gz")
    slots = P("gx", "gy", "gz", None)
    return jax.shard_map(
        local,
        mesh=mesh,
        in_specs=(
            field,
            field,
            field,
            cells,
            P(),
            P(),
            P(),
            P(),
            slots,
            P("gx", "gy", "gz", None, None),
            slots,
            slots,
            cells,
        ),
        out_specs=(field, field, P(None, ("gx", "gy", "gz"))),
        check_vma=False,
    )
```

```python
import functools

import jax
import jax.numpy as jnp
from jax import lax
from jax.experimental import pallas as pl
from jax.experimental.pallas import tpu as pltpu
from jax.sharding import PartitionSpec as P

MESH = pl.DeviceIdType.MESH
F32 = jnp.float32
BF16 = jnp.bfloat16

DT = 0.5
FACE_AREA = 0.25
STEPS = 4
CX, CY, CZ = 4, 16, 128
SLOTS = 1024
TILE_DEV = 128
NGX, NGY, NGZ = 16, 8, 4
NY_CHIPS, NZ_HI, NZ_LO, CORES = 4, 4, 4, 2
NNEAR, NFAR = NY_CHIPS * CORES, NZ_HI * NZ_LO
LANES = 16 * NFAR

(XE, XQ, YE, YQ, ZE, ZQ, E_XZ, E_XY, E_YZ, E_YX, E_ZY, E_ZX) = range(12)
ROUTES = (
    (-1, 0, 0),
    (1, 0, 0),
    (0, -1, 0),
    (0, 1, 0),
    (0, 0, -1),
    (0, 0, 1),
    (1, 0, -1),
    (1, -1, 0),
    (0, 1, -1),
    (-1, 1, 0),
    (0, -1, 1),
    (-1, 0, 1),
)


def iota(shape, axis):
    return lax.broadcasted_iota(jnp.int32, shape, axis)


def dot(a, b, contract):
    return lax.dot_general(a, b, ((contract[:1], contract[1:]), ((), ())), preferred_element_type=F32)


def halves(x):
    high = x.astype(BF16)
    return high, (x - high.astype(F32)).astype(BF16)


def kernel(
    e_in,
    h_in,
    j_in,
    mat_in,
    cell_in,
    owner_in,
    tile_in,
    normal_in,
    sig_in,
    gam_in,
    pla_in,
    g_in,
    count_ref,
    e_out,
    h_out,
    force_out,
    e_ref,
    h_ref,
    j_ref,
    part,
    mat_ref,
    cell_ref,
    owner_ref,
    tile_ref,
    normal_ref,
    sig_ref,
    gam_ref,
    pla_ref,
    g_ref,
    force_ref,
    coef,
    tensor,
    sx,
    rx,
    sy,
    ry,
    sz,
    rz,
    sr,
    rr,
    sg,
    rg,
    rest,
    bucket,
    lane_hot,
    tile_hot,
    stl,
    rtl,
    sval,
    rval,
    sdense,
    rdense,
    in_sem,
    out_sem,
    hs_sem,
    hr_sem,
    ts_sem,
    tr_sem,
    vs_sem,
    vr_sem,
    ds_sem,
    dr_sem,
    gs_sem,
    gr_sem,
):
    gx, gy, gz = lax.axis_index("gx"), lax.axis_index("gy"), lax.axis_index("gz")

    loads = [
        pltpu.make_async_copy(src, dst, in_sem.at[n])
        for n, (src, dst) in enumerate(
            (
                (e_in, e_ref),
                (h_in, h_ref),
                (j_in, j_ref),
                (mat_in, mat_ref),
                (sig_in, sig_ref),
                (gam_in, gam_ref),
                (pla_in, pla_ref),
                (g_in, g_ref),
                (cell_in, cell_ref),
                (owner_in, owner_ref),
                (tile_in, tile_ref),
                (normal_in, normal_ref),
            )
        )
    ]
    for load in loads:
        load.start()

    def at(dx, dy, dz):
        where = {}
        if dx:
            where["gx"] = lax.rem(gx + (dx + NGX), NGX)
        if dy:
            where["gy"] = gy + dy
        if dz:
            where["gz"] = lax.rem(gz + (dz + NGZ), NGZ)
        return where

    y_chip, z_hi = lax.div(gx, NZ_HI), lax.rem(gx, NZ_HI)
    z_lo, core = lax.div(gy, CORES), lax.rem(gy, CORES)
    near, far = y_chip * CORES + core, z_hi * NZ_LO + z_lo

    def near_at(n):
        return {"gx": lax.div(n, CORES) * NZ_HI + z_hi, "gy": z_lo * CORES + lax.rem(n, CORES)}

    def far_at(n):
        return {"gx": y_chip * NZ_HI + lax.div(n, NZ_LO), "gy": lax.rem(n, NZ_LO) * CORES + core}

    def sent(dy):
        return gy > 0 if dy < 0 else gy < NGY - 1

    def when(dy, do):
        if dy:
            pl.when(sent(dy))(do)
        else:
            do()

    @pl.when(gy == NGY - 1)
    def _():
        for step in range(STEPS):
            ry[step, 0:2] = jnp.zeros((2, CX, 1, CZ), F32)
            ry[step, 5] = jnp.zeros((CX, 1, CZ), F32)
            rr[step, 1] = jnp.zeros((1, CZ), F32)

    @pl.when(gy == 0)
    def _():
        for step in range(STEPS):
            ry[step, 2:5] = jnp.zeros((3, CX, 1, CZ), F32)
            rr[step, 2] = jnp.zeros((1, CZ), F32)

    barrier = pltpu.get_barrier_semaphore()

    def greet(where):
        pl.semaphore_signal(barrier, inc=1, device_id=where, device_id_type=MESH)

    for route in ROUTES:
        when(route[1], functools.partial(lambda r: greet(at(*r)), route))
    for d in range(1, NNEAR):
        greet(near_at(lax.rem(near + d, NNEAR)))
    for d in range(1, NFAR):
        greet(far_at(lax.rem(far + d, NFAR)))
    greeted = sum(route[1] == 0 for route in ROUTES) + NNEAR - 1 + NFAR - 1
    greeted = greeted + sum(route[1] < 0 for route in ROUTES) * jnp.where(gy > 0, 1, 0)
    greeted = greeted + sum(route[1] > 0 for route in ROUTES) * jnp.where(gy < NGY - 1, 1, 0)

    one, zero = jnp.float32(1.0), jnp.float32(0.0)
    low_x = jnp.where(gx > 0, one, zero)
    low_y = jnp.where(gy > 0, one, zero)
    low_z = jnp.where(gz > 0, one, zero)
    top_x = jnp.where(gx < NGX - 1, one, zero)
    top_y = jnp.where(gy < NGY - 1, one, zero)
    top_z = jnp.where(gz < NGZ - 1, one, zero)

    brick = (CX, CY, CZ)
    jj, kk = iota(brick, 1), iota(brick, 2)
    n_hot = (iota((16, 8, CZ), 0) == iota((16, 8, CZ), 2)).astype(F32)
    n_more = (iota((2, 8, CZ), 0) + 16 == iota((2, 8, CZ), 2)).astype(F32)
    row_hot = (iota((CY, CZ), 0) == iota((CY, CZ), 1)).astype(F32)

    def y_next(f):
        return pltpu.roll(f, CY - 1, 1)

    def z_next(f):
        return pltpu.roll(f, CZ - 1, 2)

    def packed(columns):
        return jnp.sum(columns.reshape(16, 8, -1) * n_hot, axis=0)

    def unpacked(tile):
        return jnp.sum(tile[None] * n_hot, axis=2, keepdims=True).reshape(2, CX, CY, 1)

    def message(step, which):
        src, dst = {
            XE: (sx.at[step, 0], rx.at[step, 0]),
            XQ: (sx.at[step, 1], rx.at[step, 1]),
            YE: (sy.at[step, pl.ds(0, 2)], ry.at[step, pl.ds(0, 2)]),
            YQ: (sy.at[step, pl.ds(2, 2)], ry.at[step, pl.ds(2, 2)]),
            ZE: (sz.at[step, 0], rz.at[step, 0]),
            ZQ: (sz.at[step, 1], rz.at[step, 1]),
            E_XZ: (sr.at[step, 0], rr.at[step, 0]),
            E_XY: (sr.at[step, 1], rr.at[step, 1]),
            E_YX: (sr.at[step, 2], rr.at[step, 2]),
            E_ZX: (sr.at[step, 3], rr.at[step, 3]),
            E_YZ: (sy.at[step, 4], ry.at[step, 4]),
            E_ZY: (sy.at[step, 5], ry.at[step, 5]),
        }[which]
        return pltpu.make_async_remote_copy(
            src_ref=src,
            dst_ref=dst,
            send_sem=hs_sem.at[step, which],
            recv_sem=hr_sem.at[step, which],
            device_id=at(*ROUTES[which]),
            device_id_type=MESH,
        )

    def start(step, *which):
        for n in which:
            when(ROUTES[n][1], lambda n=n: message(step, n).start())

    def as_row(column):
        return jnp.sum(column * row_hot, axis=0, keepdims=True)

    def as_column(row):
        return jnp.sum(row * row_hot, axis=1, keepdims=True)

    def send_edges(step, xz, zx):
        sr[step, 0] = as_row(xz)
        sr[step, 3] = as_row(zx)
        start(step, E_XZ, E_ZX)

    def edge_gain(n):
        return pltpu.make_async_remote_copy(
            src_ref=sg.at[n],
            dst_ref=rg.at[n],
            send_sem=gs_sem.at[n],
            recv_sem=gr_sem.at[n],
            device_id=at(*ROUTES[(E_XZ, E_ZX)[n]]),
            device_id_type=MESH,
        )

    def send_x(step):
        ex, ey, ez = e_ref[0], e_ref[1], e_ref[2]
        if step == 0:
            send_edges(0, ex[CX - 1, :, 0:1], ez[0, :, CZ - 1 : CZ])
        sx[step, 0, 0] = ey[0]
        sx[step, 0, 1] = ez[0]
        start(step, XE)
        ex, ey, ez = ex[CX - 1], ey[CX - 1], ez[CX - 1]
        y_ex = jnp.where(jj[0] == CY - 1, zero, pltpu.roll(ex, CY - 1, 0))
        z_ex = jnp.where(kk[0] == CZ - 1, zero, pltpu.roll(ex, CZ - 1, 1))
        sx[step, 1, 0] = h_ref[1, CX - 1] - DT * ((z_ex - ex) + ez)
        sx[step, 1, 1] = h_ref[2, CX - 1] + DT * (ey + (y_ex - ex))
        start(step, XQ)
        sr[step, 1] = ex[0:1, :]
        sr[step, 2] = e_ref[1, 0, CY - 1 : CY, :]
        start(step, E_XY, E_YX)

    def send_yz(step):
        ex, ey, ez = e_ref[0], e_ref[1], e_ref[2]
        nothing = jnp.zeros((1, CY, CZ), F32)
        last_y, last_z = jj == CY - 1, kk == CZ - 1
        y_ez = jnp.where(last_y, zero, y_next(ez))
        y_ex = jnp.where(last_y, zero, y_next(ex))
        z_ey = jnp.where(last_z, zero, z_next(ey))
        z_ex = jnp.where(last_z, zero, z_next(ex))
        x_ez = jnp.concatenate([ez[1:], nothing], 0)
        x_ey = jnp.concatenate([ey[1:], nothing], 0)
        hx = h_ref[0] - DT * ((y_ez - ez) - (z_ey - ey))
        hy = h_ref[1] - DT * ((z_ex - ex) - (x_ez - ez))
        hz = h_ref[2] - DT * ((x_ey - ey) - (y_ex - ex))
        part[0], part[1], part[2] = hx, hy, hz
        sz[step, 0] = packed(e_ref[0:2][:, :, :, 0:1]) + jnp.sum(ez[0].reshape(2, 8, CZ)[:, :, 0:1] * n_more, axis=0)
        sz[step, 1] = packed(part[0:2][:, :, :, CZ - 1 : CZ])
        start(step, ZE, ZQ)
        sy[step, 0] = ex[:, 0:1, :]
        sy[step, 1] = ez[:, 0:1, :]
        sy[step, 2] = hx[:, CY - 1 : CY, :]
        sy[step, 3] = hz[:, CY - 1 : CY, :]
        sy[step, 4] = ey[:, CY - 1 : CY, :]
        sy[step, 5] = ez[:, 0:1, :]
        start(step, YE, YQ, E_YZ, E_ZY)

    def wait(step, *which):
        for n in which:
            when(-ROUTES[n][1], lambda n=n: message(step, n).wait_recv())

    def current(step):
        j_ref[...] = coef[2][None] * j_ref[...] + coef[3][None] * e_ref[...]

    def update(step):
        last = CX - 1
        wait(step, ZE, ZQ, YE, YQ, E_YZ, E_ZY)
        ex, ey, ez = e_ref[0], e_ref[1], e_ref[2]
        hx, hy, hz = part[0], part[1], part[2]
        above_y = ry[step, 0:2]
        above_z = unpacked(rz[step, 0]) * top_z
        last_y, last_z = jj == CY - 1, kk == CZ - 1
        hx = hx + jnp.where(last_z, DT * above_z[1], zero) - jnp.where(last_y, DT * above_y[1], zero)
        hy = hy - jnp.where(last_z, DT * above_z[0], zero)
        hz = hz + jnp.where(last_y, DT * above_y[0], zero)
        e_yz = ry[step, 4] * top_z
        e_zy = ry[step, 5]
        ky, jz = iota((CX, 1, CZ), 2), iota((CX, CY, 1), 1)
        below_yx = ry[step, 2] - DT * ez[:, 0:1, :] + jnp.where(ky == CZ - 1, DT * e_yz[:, :, 0:1], zero)
        below_yz = ry[step, 3] + DT * ex[:, 0:1, :]
        below_z = unpacked(rz[step, 1])
        below_zx = below_z[0] + DT * ey[:, :, 0:1] - jnp.where(jz == CY - 1, DT * e_zy[:, :, CZ - 1 : CZ], zero)
        below_zy = below_z[1] - DT * ex[:, :, 0:1]
        first_y, first_z = jj == 0, kk == 0
        y_hx = jnp.where(first_y, low_y * below_yx, pltpu.roll(hx, 1, 1))
        y_hz = jnp.where(first_y, low_y * below_yz, pltpu.roll(hz, 1, 1))
        z_hx = jnp.where(first_z, low_z * below_zx, pltpu.roll(hx, 1, 2))
        z_hy = jnp.where(first_z, low_z * below_zy, pltpu.roll(hy, 1, 2))
        nothing = jnp.zeros((1, CY, CZ), F32)
        x_hy = jnp.concatenate([nothing, hy[:last]], 0)
        x_hz = jnp.concatenate([nothing, hz[:last]], 0)
        keep, gain = coef[0], coef[1]
        part[0] = keep * ex + gain * (((hz - y_hz) - (hy - z_hy)) - j_ref[0])
        part[1] = keep * ey + gain * (((hx - z_hx) - (hz - x_hz)) - j_ref[1])
        part[2] = keep * ez + gain * (((hy - x_hy) - (hx - y_hx)) - j_ref[2])
        h_ref[0], h_ref[1], h_ref[2] = hx, hy, hz
        jr, kr = jj[0], kk[0]
        if step < STEPS - 1:
            send_edges(step + 1, part[0, last, :, 0:1], part[2, 0, :, CZ - 1 : CZ])

        def edges():
            wait(step, E_XZ, E_ZX)
            e_xz, e_zx = as_column(rr[step, 0]), as_column(rr[step, 3])
            if step == 1:
                for n in range(2):
                    edge_gain(n).wait_recv()
            if step:
                e_xz = e_xz + as_column(rg[0]) * rest[0]
                e_zx = e_zx - as_column(rg[1]) * rest[1]
            e_xz, e_zx = e_xz * (DT * top_z), e_zx * (DT * top_x)
            if step < STEPS - 1:
                more_z = jnp.broadcast_to(-DT * above_z[1, 0], (CY, CZ))
                y_more_z = jnp.where(jr == 0, -DT * e_yz[0, :, 0:1], pltpu.roll(more_z, 1, 0))
                more_y = DT * jnp.sum(rz[step, 0][None] * n_more, axis=2, keepdims=True).reshape(CY, 1)
                rest[0] = (more_z - y_more_z) - (more_y - DT * ez[0, :, CZ - 1 : CZ])
                rest[1] = jnp.broadcast_to(below_zy[last] + e_zx, (CY, CZ))
            at_xz = jnp.where(kr == CZ - 1, low_x * coef[1, 0] * e_xz, zero)
            at_zx = jnp.where(kr == 0, low_z * coef[1, last] * e_zx, zero)
            return at_xz, at_zx

        if step:
            at_xz, at_zx = edges()
            part[2, 0] = part[2, 0] + at_xz
            part[0, last] = part[0, last] + at_zx

        wait(step, E_XY, E_YX, XE, XQ)
        more_y = (DT * top_x) * rx[step, 0, 1]
        more_z = (-DT * top_x) * rx[step, 0, 0]
        e_yx = rr[step, 2] * top_x
        h_ref[1, last] = h_ref[1, last] + more_y
        h_ref[2, last] = h_ref[2, last] + more_z
        y_more_z = jnp.where(jr == 0, (-DT * low_y) * e_yx, pltpu.roll(more_z, 1, 0))
        z_more_y = jnp.where(kr == 0, zero, pltpu.roll(more_y, 1, 1))
        gain = coef[1, last]
        e_ref[0, 0:last] = part[0, 0:last]
        e_ref[1, 1:last] = part[1, 1:last]
        e_ref[2, 1:last] = part[2, 1:last]
        x_last = part[0, last] + gain * ((more_z - y_more_z) - (more_y - z_more_y))
        e_ref[1, last] = part[1, last] - gain * more_z
        e_ref[2, last] = part[2, last] + gain * more_y
        below_xy = rx[step, 1, 0] + DT * e_ref[2, 0]
        below_xz = rx[step, 1, 1] - DT * e_ref[1, 0] + jnp.where(jr == CY - 1, DT * rr[step, 1], zero)
        gain_0 = low_x * coef[1, 0]
        z_first = part[2, 0] - gain_0 * below_xy
        e_ref[1, 0] = part[1, 0] + gain_0 * below_xz

        if step == 0:
            at_xz, at_zx = edges()
            z_first = z_first + at_xz
            x_last = x_last + at_zx
        e_ref[2, 0] = z_first
        e_ref[0, last] = x_last

    def stress(step):
        ex, ey, ez = e_ref[0], e_ref[1], e_ref[2]
        hx, hy, hz = h_ref[0], h_ref[1], h_ref[2]
        g = g_ref[step]
        xx, yy, zz = ex * ex + hx * hx, ey * ey + hy * hy, ez * ez + hz * hz
        energy = 0.5 * (xx + yy + zz)
        found = (xx - energy, ex * ey + hx * hy, ex * ez + hx * hz, yy - energy, ey * ez + hy * hz, zz - energy)
        for n, value in enumerate(found):
            tensor[n] = g * value if step == 0 else tensor[n] + g * value

    def ranks_and_buckets():
        owner = owner_ref[...]
        block = SLOTS // 4
        groups = NGX * NGY
        earlier = (iota((block, block), 0) < iota((block, block), 1)).astype(F32).astype(BF16)
        lane = iota((1, block), 1)
        before = jnp.zeros((groups, 1), F32)
        made = jnp.zeros((5 * NNEAR, LANES), F32)
        for b in range(4):
            cut = slice(b * block, (b + 1) * block)
            own = owner[:, cut]
            hot = (own == iota((groups, block), 0)).astype(F32)
            ahead = dot(hot.astype(BF16), earlier, (1, 0)) + before
            rank = jnp.sum(ahead * hot, axis=0, keepdims=True).astype(jnp.int32)
            before = before + jnp.sum(hot, axis=1, keepdims=True)
            place = rank * NFAR + (lax.shift_right_logical(own, 1) & (NFAR - 1))
            place_hot = (place == iota((LANES, block), 0)).astype(F32).astype(BF16)
            cell, normal = cell_ref[:, cut], normal_ref[:, cut]
            live = (lane + b * block < count_ref[0, 0, 0]).astype(F32)
            weight = live * (FACE_AREA * (1 - 2 * (normal & 1)).astype(F32))
            mine = lax.shift_right_logical(own, 5) * CORES + (own & 1) == iota((NNEAR, block), 0)
            entries = (
                (cell & 127).astype(F32),
                lax.shift_right_logical(cell, 7).astype(F32),
                weight,
                lax.shift_right_logical(normal, 1).astype(F32),
                tile_ref[:, cut].astype(F32),
            )
            rows = jnp.concatenate([jnp.where(mine, entry, zero) for entry in entries], 0)
            made = made + dot(rows.astype(BF16), place_hot, (1, 1))
        for n in range(5):
            bucket[n] = made[n * NNEAR : (n + 1) * NNEAR].reshape(NNEAR, 1, LANES)
        stl[...] = bucket[4]

    def to_near(src, dst, send, recv, d):
        n = lax.rem(near + d, NNEAR)
        return pltpu.make_async_remote_copy(
            src_ref=src.at[n],
            dst_ref=dst.at[near],
            send_sem=send.at[d],
            recv_sem=recv.at[d],
            device_id=near_at(n),
            device_id_type=MESH,
        )

    def from_near(src, dst, send, recv, d):
        n = lax.rem(near + NNEAR - d, NNEAR)
        return pltpu.make_async_remote_copy(
            src_ref=src.at[n],
            dst_ref=dst.at[n],
            send_sem=send.at[d],
            recv_sem=recv.at[d],
            device_id=near_at(n),
            device_id_type=MESH,
        )

    def lane_hots():
        for n in range(NNEAR):
            lane_hot[n] = (bucket[0, n] == iota((CZ, LANES), 0).astype(F32)).astype(F32).astype(BF16)

    def tile_hots():
        for d in range(1, NNEAR):
            from_near(stl, rtl, ts_sem, tr_sem, d).wait_recv()
        for n in range(NNEAR):
            tile_hot[n] = (rtl[n] == iota((TILE_DEV, LANES), 0).astype(F32)).astype(F32).astype(BF16)

    def coefficients():
        material = mat_ref[...]

        def of_material(table):
            result = jnp.where(material == 0, table[0], zero)
            for which in (1, 2):
                result = jnp.where(material == which, table[which], result)
            return result

        sigma, gamma, plasma = of_material(sig_ref), of_material(gam_ref), of_material(pla_ref)
        coef[0] = (1.0 - sigma * DT / 2) / (1.0 + sigma * DT / 2)
        coef[1] = DT / (1.0 + sigma * DT / 2)
        coef[2] = (1.0 - gamma * DT / 2) / (1.0 + gamma * DT / 2)
        coef[3] = plasma * DT / (1.0 + gamma * DT / 2)

    loads[0].wait()
    loads[1].wait()
    pl.semaphore_wait(barrier, greeted)

    for step in range(STEPS):
        send_x(step)
        send_yz(step)
        if step == 0:
            for load in loads[2:]:
                load.wait()
            coefficients()
            sg[0] = as_row(coef[1, CX - 1, :, 0:1])
            sg[1] = as_row(coef[1, 0, :, CZ - 1 : CZ])
            for n in range(2):
                edge_gain(n).start()
            current(step)
            ranks_and_buckets()
            for d in range(1, NNEAR):
                to_near(stl, rtl, ts_sem, tr_sem, d).start()
            rtl[near] = stl[near]
        else:
            current(step)
            stress(step - 1)
        if step == 1:
            lane_hots()
        if step == 2:
            tile_hots()
        update(step)
    stores = [
        pltpu.make_async_copy(src, dst, out_sem.at[n]) for n, (src, dst) in enumerate(((e_ref, e_out), (h_ref, h_out)))
    ]
    for store in stores:
        store.start()
    stress(STEPS - 1)

    cells = CX * CY
    high, low = halves(tensor[...].reshape(6 * cells, CZ))
    parts = jnp.concatenate([high, low], 1)
    for n in range(NNEAR):
        hot = lane_hot[n]
        read = dot(parts, jnp.concatenate([hot, hot], 0), (1, 0))
        row = bucket[1, n] == iota((cells, LANES), 0).astype(F32)
        xx, xy, xz, yy, yz, zz = [
            jnp.sum(jnp.where(row, read[c * cells : (c + 1) * cells], zero), axis=0, keepdims=True) for c in range(6)
        ]
        axis, weight = bucket[3, n], bucket[2, n]
        along_x, along_y = axis == 0.0, axis == 1.0
        sval[n, 0:1] = weight * jnp.where(along_x, xx, jnp.where(along_y, xy, xz))
        sval[n, 1:2] = weight * jnp.where(along_x, xy, jnp.where(along_y, yy, yz))
        sval[n, 2:3] = weight * jnp.where(along_x, xz, jnp.where(along_y, yz, zz))
    for d in range(1, NNEAR):
        to_near(sval, rval, vs_sem, vr_sem, d).start()
    rval[near] = sval[near]

    for d in range(1, NNEAR):
        from_near(sval, rval, vs_sem, vr_sem, d).wait_recv()
    rows = (NFAR * 8, LANES)
    mine = (lax.shift_right_logical(iota(rows, 0), 3) == (iota(rows, 1) & (NFAR - 1))).astype(F32)
    dense = jnp.zeros((NFAR * 8, TILE_DEV), F32)
    for n in range(NNEAR):
        value = rval[n]
        high = value.astype(BF16).astype(F32)
        both = jnp.concatenate([high, value - high, jnp.zeros((2, LANES), F32)], 0)
        spread = (jnp.concatenate([both] * NFAR, 0) * mine).astype(BF16)
        dense = dense + dot(spread, tile_hot[n], (1, 1))
    dense = dense.reshape(NFAR, 8, TILE_DEV)
    sdense[...] = dense[:, 0:3] + dense[:, 3:6]

    def to_far(d):
        n = lax.rem(far + d, NFAR)
        return pltpu.make_async_remote_copy(
            src_ref=sdense.at[n],
            dst_ref=rdense.at[far],
            send_sem=ds_sem.at[d],
            recv_sem=dr_sem.at[d],
            device_id=far_at(n),
            device_id_type=MESH,
        )

    def from_far(d):
        n = lax.rem(far + NFAR - d, NFAR)
        return pltpu.make_async_remote_copy(
            src_ref=sdense.at[n],
            dst_ref=rdense.at[n],
            send_sem=ds_sem.at[d],
            recv_sem=dr_sem.at[d],
            device_id=far_at(n),
            device_id_type=MESH,
        )

    for d in range(1, NFAR):
        to_far(d).start()
    rdense[far] = sdense[far]
    for d in range(1, NFAR):
        from_far(d).wait_recv()
    force_ref[...] = jnp.sum(rdense[...], axis=0)

    for step in range(STEPS):
        for which in range(12):
            when(ROUTES[which][1], lambda which=which: message(step, which).wait_send())
    for n in range(2):
        edge_gain(n).wait_send()
    for d in range(1, NNEAR):
        to_near(stl, rtl, ts_sem, tr_sem, d).wait_send()
        to_near(sval, rval, vs_sem, vr_sem, d).wait_send()
    for d in range(1, NFAR):
        to_far(d).wait_send()
    last = pltpu.make_async_copy(force_ref, force_out, out_sem.at[2])
    last.start()
    for store in [*stores, last]:
        store.wait()


def hand_out(*refs):
    sem = refs[-1]
    copies = [pltpu.make_async_copy(refs[n], refs[n + 3], sem.at[n]) for n in range(3)]
    for copy in copies:
        copy.start()
    for copy in copies:
        copy.wait()


def local(
    e_field,
    h_field,
    current,
    material,
    sigma_table,
    gamma_table,
    plasma_table,
    g_kernel,
    surf_cell,
    surf_owner,
    surf_tile,
    surf_normal,
    row_count,
):
    field = jax.ShapeDtypeStruct((3, CX, CY, CZ), F32)
    hbm = pl.BlockSpec(memory_space=pltpu.HBM)
    dma = pltpu.SemaphoreType.DMA
    slots = [a.reshape(1, SLOTS) for a in (surf_cell, surf_owner, surf_tile, surf_normal)]
    operands = (e_field, h_field, current, material, *slots)
    operands += (sigma_table, gamma_table, plasma_table, g_kernel)
    operands = [pltpu.with_memory_space_constraint(a, pltpu.HBM) for a in operands]
    shapes = (field, field, jax.ShapeDtypeStruct((3, TILE_DEV), F32))
    made = pl.pallas_call(
        kernel,
        out_shape=shapes,
        in_specs=[hbm] * 12 + [pl.BlockSpec(memory_space=pltpu.SMEM)],
        out_specs=(hbm, hbm, hbm),
        scratch_shapes=[
            pltpu.VMEM((3, CX, CY, CZ), F32),
            pltpu.VMEM((3, CX, CY, CZ), F32),
            pltpu.VMEM((3, CX, CY, CZ), F32),
            pltpu.VMEM((3, CX, CY, CZ), F32),
            pltpu.VMEM((CX, CY, CZ), jnp.int32),
            pltpu.VMEM((1, SLOTS), jnp.int32),
            pltpu.VMEM((1, SLOTS), jnp.int32),
            pltpu.VMEM((1, SLOTS), jnp.int32),
            pltpu.VMEM((1, SLOTS), jnp.int32),
            pltpu.SMEM((3,), F32),
            pltpu.SMEM((3,), F32),
            pltpu.SMEM((3,), F32),
            pltpu.SMEM((STEPS,), F32),
            pltpu.VMEM((3, TILE_DEV), F32),
            pltpu.VMEM((4, CX, CY, CZ), F32),
            pltpu.VMEM((6, CX, CY, CZ), F32),
            pltpu.VMEM((STEPS, 2, 2, CY, CZ), F32),
            pltpu.VMEM((STEPS, 2, 2, CY, CZ), F32),
            pltpu.VMEM((STEPS, 6, CX, 1, CZ), F32),
            pltpu.VMEM((STEPS, 6, CX, 1, CZ), F32),
            pltpu.VMEM((STEPS, 2, 8, CZ), F32),
            pltpu.VMEM((STEPS, 2, 8, CZ), F32),
            pltpu.VMEM((STEPS, 4, 1, CZ), F32),
            pltpu.VMEM((STEPS, 4, 1, CZ), F32),
            pltpu.VMEM((2, 1, CZ), F32),
            pltpu.VMEM((2, 1, CZ), F32),
            pltpu.VMEM((2, CY, CZ), F32),
            pltpu.VMEM((5, NNEAR, 1, LANES), F32),
            pltpu.VMEM((NNEAR, CZ, LANES), BF16),
            pltpu.VMEM((NNEAR, TILE_DEV, LANES), BF16),
            pltpu.VMEM((NNEAR, 1, LANES), F32),
            pltpu.VMEM((NNEAR, 1, LANES), F32),
            pltpu.VMEM((NNEAR, 3, LANES), F32),
            pltpu.VMEM((NNEAR, 3, LANES), F32),
            pltpu.VMEM((NFAR, 3, TILE_DEV), F32),
            pltpu.VMEM((NFAR, 3, TILE_DEV), F32),
            dma((12,)),
            dma((3,)),
            dma((STEPS, 12)),
            dma((STEPS, 12)),
            dma((NNEAR,)),
            dma((NNEAR,)),
            dma((NNEAR,)),
            dma((NNEAR,)),
            dma((NFAR,)),
            dma((NFAR,)),
            dma((2,)),
            dma((2,)),
        ],
        compiler_params=pltpu.CompilerParams(
            collective_id=0, has_side_effects=True, vmem_limit_bytes=24 * 2**20
        ),
    )(*operands, row_count)
    return pl.pallas_call(
        hand_out,
        out_shape=shapes,
        in_specs=[hbm] * 3,
        out_specs=(hbm,) * 3,
        scratch_shapes=[dma((3,))],
        compiler_params=pltpu.CompilerParams(vmem_limit_bytes=24 * 2**20),
    )(*made)


def solution(mesh):
    cells = P("gx", "gy", "gz")
    field = P(None, "gx", "gy", "gz")
    slots = P("gx", "gy", "gz", None)
    return jax.shard_map(
        local,
        mesh=mesh,
        in_specs=(
            field,
            field,
            field,
            cells,
            P(),
            P(),
            P(),
            P(),
            slots,
            P("gx", "gy", "gz", None, None),
            slots,
            slots,
            cells,
        ),
        out_specs=(field, field, P(None, ("gx", "gy", "gz"))),
        check_vma=False,
    )
```

```python
import functools

import jax
import jax.numpy as jnp
from jax import lax
from jax.experimental import pallas as pl
from jax.experimental.pallas import tpu as pltpu
from jax.sharding import PartitionSpec as P

MESH = pl.DeviceIdType.MESH
F32 = jnp.float32
BF16 = jnp.bfloat16

DT = 0.5
FACE_AREA = 0.25
STEPS = 4
CX, CY, CZ = 4, 16, 128
SLOTS = 1024
TILE_DEV = 128
NGX, NGY, NGZ = 16, 8, 4
NY_CHIPS, NZ_HI, NZ_LO, CORES = 4, 4, 4, 2
NNEAR, NFAR = NY_CHIPS * CORES, NZ_HI * NZ_LO
LANES = 16 * NFAR

(XE, XQ, YE, YQ, ZE, ZQ, E_XZ, E_XY, E_YZ, E_YX, E_ZY, E_ZX) = range(12)
ROUTES = (
    (-1, 0, 0),
    (1, 0, 0),
    (0, -1, 0),
    (0, 1, 0),
    (0, 0, -1),
    (0, 0, 1),
    (1, 0, -1),
    (1, -1, 0),
    (0, 1, -1),
    (-1, 1, 0),
    (0, -1, 1),
    (-1, 0, 1),
)


def iota(shape, axis):
    return lax.broadcasted_iota(jnp.int32, shape, axis)


def dot(a, b, contract):
    return lax.dot_general(a, b, ((contract[:1], contract[1:]), ((), ())), preferred_element_type=F32)


def halves(x):
    high = x.astype(BF16)
    return high, (x - high.astype(F32)).astype(BF16)


def kernel(
    e_in,
    h_in,
    j_in,
    mat_in,
    cell_in,
    owner_in,
    tile_in,
    normal_in,
    sig_in,
    gam_in,
    pla_in,
    g_in,
    count_ref,
    e_out,
    h_out,
    force_ref,
    e_ref,
    h_ref,
    j_ref,
    part,
    mat_ref,
    cell_ref,
    owner_ref,
    tile_ref,
    normal_ref,
    sig_ref,
    gam_ref,
    pla_ref,
    g_ref,
    coef,
    tensor,
    sx,
    rx,
    sy,
    ry,
    sz,
    rz,
    sr,
    rr,
    sg,
    rg,
    rest,
    bucket,
    lane_hot,
    tile_hot,
    stl,
    rtl,
    sval,
    rval,
    sdense,
    rdense,
    in_sem,
    out_sem,
    hs_sem,
    hr_sem,
    ts_sem,
    tr_sem,
    vs_sem,
    vr_sem,
    ds_sem,
    dr_sem,
    gs_sem,
    gr_sem,
):
    gx, gy, gz = lax.axis_index("gx"), lax.axis_index("gy"), lax.axis_index("gz")

    loads = [
        pltpu.make_async_copy(src, dst, in_sem.at[n])
        for n, (src, dst) in enumerate(
            (
                (e_in, e_ref),
                (h_in, h_ref),
                (j_in, j_ref),
                (mat_in, mat_ref),
                (sig_in, sig_ref),
                (gam_in, gam_ref),
                (pla_in, pla_ref),
                (g_in, g_ref),
                (cell_in, cell_ref),
                (owner_in, owner_ref),
                (tile_in, tile_ref),
                (normal_in, normal_ref),
            )
        )
    ]
    for load in loads[:2]:
        load.start()

    def at(dx, dy, dz):
        where = {}
        if dx:
            where["gx"] = lax.rem(gx + (dx + NGX), NGX)
        if dy:
            where["gy"] = gy + dy
        if dz:
            where["gz"] = lax.rem(gz + (dz + NGZ), NGZ)
        return where

    y_chip, z_hi = lax.div(gx, NZ_HI), lax.rem(gx, NZ_HI)
    z_lo, core = lax.div(gy, CORES), lax.rem(gy, CORES)
    near, far = y_chip * CORES + core, z_hi * NZ_LO + z_lo

    def near_at(n):
        return {"gx": lax.div(n, CORES) * NZ_HI + z_hi, "gy": z_lo * CORES + lax.rem(n, CORES)}

    def far_at(n):
        return {"gx": y_chip * NZ_HI + lax.div(n, NZ_LO), "gy": lax.rem(n, NZ_LO) * CORES + core}

    def sent(dy):
        return gy > 0 if dy < 0 else gy < NGY - 1

    def when(dy, do):
        if dy:
            pl.when(sent(dy))(do)
        else:
            do()

    barrier = pltpu.get_barrier_semaphore()

    def greet(where):
        pl.semaphore_signal(barrier, inc=1, device_id=where, device_id_type=MESH)

    for d in range(1, NZ_LO):
        greet({"gy": lax.rem(z_lo + d, NZ_LO) * CORES + core})
    for route in sorted(ROUTES, key=lambda r: -abs(r[0])):
        when(route[1], functools.partial(lambda r: greet(at(*r)), route))
    for d in range(1, NNEAR):
        greet(near_at(lax.rem(near + d, NNEAR)))
    for load in loads[2:]:
        load.start()
    greeted = sum(route[1] == 0 for route in ROUTES) + NNEAR - 1 + NZ_LO - 1
    greeted = greeted + sum(route[1] < 0 for route in ROUTES) * jnp.where(gy > 0, 1, 0)
    greeted = greeted + sum(route[1] > 0 for route in ROUTES) * jnp.where(gy < NGY - 1, 1, 0)

    @pl.when(gy == NGY - 1)
    def _():
        for step in range(STEPS):
            ry[step, 0:2] = jnp.zeros((2, CX, 1, CZ), F32)
            ry[step, 5] = jnp.zeros((CX, 1, CZ), F32)
            rr[step, 1] = jnp.zeros((1, CZ), F32)

    @pl.when(gy == 0)
    def _():
        for step in range(STEPS):
            ry[step, 2:5] = jnp.zeros((3, CX, 1, CZ), F32)
            rr[step, 2] = jnp.zeros((1, CZ), F32)

    one, zero = jnp.float32(1.0), jnp.float32(0.0)
    low_x = jnp.where(gx > 0, one, zero)
    low_y = jnp.where(gy > 0, one, zero)
    low_z = jnp.where(gz > 0, one, zero)
    top_x = jnp.where(gx < NGX - 1, one, zero)
    top_y = jnp.where(gy < NGY - 1, one, zero)
    top_z = jnp.where(gz < NGZ - 1, one, zero)

    brick = (CX, CY, CZ)
    jj, kk = iota(brick, 1), iota(brick, 2)
    n_hot = (iota((16, 8, CZ), 0) == iota((16, 8, CZ), 2)).astype(F32)
    n_more = (iota((2, 8, CZ), 0) + 16 == iota((2, 8, CZ), 2)).astype(F32)
    row_hot = (iota((CY, CZ), 0) == iota((CY, CZ), 1)).astype(F32)

    def y_next(f):
        return pltpu.roll(f, CY - 1, 1)

    def z_next(f):
        return pltpu.roll(f, CZ - 1, 2)

    def packed(columns):
        return jnp.sum(columns.reshape(16, 8, -1) * n_hot, axis=0)

    def unpacked(tile):
        return jnp.sum(tile[None] * n_hot, axis=2, keepdims=True).reshape(2, CX, CY, 1)

    def message(step, which):
        src, dst = {
            XE: (sx.at[step, 0], rx.at[step, 0]),
            XQ: (sx.at[step, 1], rx.at[step, 1]),
            YE: (sy.at[step, pl.ds(0, 2)], ry.at[step, pl.ds(0, 2)]),
            YQ: (sy.at[step, pl.ds(2, 2)], ry.at[step, pl.ds(2, 2)]),
            ZE: (sz.at[step, 0], rz.at[step, 0]),
            ZQ: (sz.at[step, 1], rz.at[step, 1]),
            E_XZ: (sr.at[step, 0], rr.at[step, 0]),
            E_XY: (sr.at[step, 1], rr.at[step, 1]),
            E_YX: (sr.at[step, 2], rr.at[step, 2]),
            E_ZX: (sr.at[step, 3], rr.at[step, 3]),
            E_YZ: (sy.at[step, 4], ry.at[step, 4]),
            E_ZY: (sy.at[step, 5], ry.at[step, 5]),
        }[which]
        return pltpu.make_async_remote_copy(
            src_ref=src,
            dst_ref=dst,
            send_sem=hs_sem.at[step, which],
            recv_sem=hr_sem.at[step, which],
            device_id=at(*ROUTES[which]),
            device_id_type=MESH,
        )

    def start(step, *which):
        for n in which:
            when(ROUTES[n][1], lambda n=n: message(step, n).start())

    def as_row(column):
        return jnp.sum(column * row_hot, axis=0, keepdims=True)

    def as_column(row):
        return jnp.sum(row * row_hot, axis=1, keepdims=True)

    def send_edges(step, xz, zx):
        sr[step, 0] = as_row(xz)
        sr[step, 3] = as_row(zx)
        start(step, E_XZ, E_ZX)

    def edge_gain(n):
        return pltpu.make_async_remote_copy(
            src_ref=sg.at[n],
            dst_ref=rg.at[n],
            send_sem=gs_sem.at[n],
            recv_sem=gr_sem.at[n],
            device_id=at(*ROUTES[(E_XZ, E_ZX)[n]]),
            device_id_type=MESH,
        )

    def send_sums(step, ex, ey, ez, hy, hz, y_first):
        y_ex = jnp.where(jj[0] == CY - 1, zero, pltpu.roll(ex, CY - 1, 0))
        z_ex = jnp.where(kk[0] == CZ - 1, zero, pltpu.roll(ex, CZ - 1, 1))
        sx[step, 1, 0] = hy - DT * ((z_ex - ex) + ez)
        sx[step, 1, 1] = hz + DT * (ey + (y_ex - ex))
        start(step, XQ)
        sr[step, 1] = ex[0:1, :]
        sr[step, 2] = y_first[CY - 1 : CY, :]
        start(step, E_XY, E_YX)

    def send_x():
        last = CX - 1
        ey, ez = e_ref[1, 0], e_ref[2, 0]
        send_edges(0, e_ref[0, last, :, 0:1], ez[:, CZ - 1 : CZ])
        sx[0, 0, 0] = ey
        sx[0, 0, 1] = ez
        start(0, XE)
        send_sums(0, e_ref[0, last], e_ref[1, last], e_ref[2, last], h_ref[1, last], h_ref[2, last], ey)

    def send_yz(step):
        ex, ey, ez = e_ref[0], e_ref[1], e_ref[2]
        nothing = jnp.zeros((1, CY, CZ), F32)
        last_y, last_z = jj == CY - 1, kk == CZ - 1
        y_ez = jnp.where(last_y, zero, y_next(ez))
        y_ex = jnp.where(last_y, zero, y_next(ex))
        z_ey = jnp.where(last_z, zero, z_next(ey))
        z_ex = jnp.where(last_z, zero, z_next(ex))
        x_ez = jnp.concatenate([ez[1:], nothing], 0)
        x_ey = jnp.concatenate([ey[1:], nothing], 0)
        hx = h_ref[0] - DT * ((y_ez - ez) - (z_ey - ey))
        hy = h_ref[1] - DT * ((z_ex - ex) - (x_ez - ez))
        hz = h_ref[2] - DT * ((x_ey - ey) - (y_ex - ex))
        part[0], part[1], part[2] = hx, hy, hz
        sz[step, 0] = packed(e_ref[0:2][:, :, :, 0:1]) + jnp.sum(ez[0].reshape(2, 8, CZ)[:, :, 0:1] * n_more, axis=0)
        sz[step, 1] = packed(part[0:2][:, :, :, CZ - 1 : CZ])
        start(step, ZE, ZQ)
        sy[step, 0] = ex[:, 0:1, :]
        sy[step, 1] = ez[:, 0:1, :]
        sy[step, 2] = hx[:, CY - 1 : CY, :]
        sy[step, 3] = hz[:, CY - 1 : CY, :]
        sy[step, 4] = ey[:, CY - 1 : CY, :]
        sy[step, 5] = ez[:, 0:1, :]
        start(step, YE, YQ, E_YZ, E_ZY)

    def wait(step, *which):
        for n in which:
            when(-ROUTES[n][1], lambda n=n: message(step, n).wait_recv())

    def current(step):
        j_ref[...] = coef[2][None] * j_ref[...] + coef[3][None] * e_ref[...]

    def update(step):
        last = CX - 1
        wait(step, ZE, ZQ, YE, YQ, E_YZ, E_ZY)
        ex, ey, ez = e_ref[0], e_ref[1], e_ref[2]
        hx, hy, hz = part[0], part[1], part[2]
        above_y = ry[step, 0:2]
        above_z = unpacked(rz[step, 0]) * top_z
        last_y, last_z = jj == CY - 1, kk == CZ - 1
        hx = hx + jnp.where(last_z, DT * above_z[1], zero) - jnp.where(last_y, DT * above_y[1], zero)
        hy = hy - jnp.where(last_z, DT * above_z[0], zero)
        hz = hz + jnp.where(last_y, DT * above_y[0], zero)
        e_yz = ry[step, 4] * top_z
        e_zy = ry[step, 5]
        ky, jz = iota((CX, 1, CZ), 2), iota((CX, CY, 1), 1)
        below_yx = ry[step, 2] - DT * ez[:, 0:1, :] + jnp.where(ky == CZ - 1, DT * e_yz[:, :, 0:1], zero)
        below_yz = ry[step, 3] + DT * ex[:, 0:1, :]
        below_z = unpacked(rz[step, 1])
        below_zx = below_z[0] + DT * ey[:, :, 0:1] - jnp.where(jz == CY - 1, DT * e_zy[:, :, CZ - 1 : CZ], zero)
        below_zy = below_z[1] - DT * ex[:, :, 0:1]
        first_y, first_z = jj == 0, kk == 0
        y_hx = jnp.where(first_y, low_y * below_yx, pltpu.roll(hx, 1, 1))
        y_hz = jnp.where(first_y, low_y * below_yz, pltpu.roll(hz, 1, 1))
        z_hx = jnp.where(first_z, low_z * below_zx, pltpu.roll(hx, 1, 2))
        z_hy = jnp.where(first_z, low_z * below_zy, pltpu.roll(hy, 1, 2))
        nothing = jnp.zeros((1, CY, CZ), F32)
        x_hy = jnp.concatenate([nothing, hy[:last]], 0)
        x_hz = jnp.concatenate([nothing, hz[:last]], 0)
        keep, gain = coef[0], coef[1]
        part[0] = keep * ex + gain * (((hz - y_hz) - (hy - z_hy)) - j_ref[0])
        part[1] = keep * ey + gain * (((hx - z_hx) - (hz - x_hz)) - j_ref[1])
        part[2] = keep * ez + gain * (((hy - x_hy) - (hx - y_hx)) - j_ref[2])
        h_ref[0], h_ref[1], h_ref[2] = hx, hy, hz
        jr, kr = jj[0], kk[0]
        if step < STEPS - 1:
            send_edges(step + 1, part[0, last, :, 0:1], part[2, 0, :, CZ - 1 : CZ])

        def edges():
            wait(step, E_XZ, E_ZX)
            e_xz, e_zx = as_column(rr[step, 0]), as_column(rr[step, 3])
            if step == 1:
                for n in range(2):
                    edge_gain(n).wait_recv()
            if step:
                e_xz = e_xz + as_column(rg[0]) * rest[0]
                e_zx = e_zx - as_column(rg[1]) * rest[1]
            e_xz, e_zx = e_xz * (DT * top_z), e_zx * (DT * top_x)
            if step < STEPS - 1:
                more_z = jnp.broadcast_to(-DT * above_z[1, 0], (CY, CZ))
                y_more_z = jnp.where(jr == 0, -DT * e_yz[0, :, 0:1], pltpu.roll(more_z, 1, 0))
                more_y = DT * jnp.sum(rz[step, 0][None] * n_more, axis=2, keepdims=True).reshape(CY, 1)
                rest[0] = (more_z - y_more_z) - (more_y - DT * ez[0, :, CZ - 1 : CZ])
                rest[1] = jnp.broadcast_to(below_zy[last] + e_zx, (CY, CZ))
            at_xz = jnp.where(kr == CZ - 1, low_x * coef[1, 0] * e_xz, zero)
            at_zx = jnp.where(kr == 0, low_z * coef[1, last] * e_zx, zero)
            return at_xz, at_zx

        if step:
            at_xz, at_zx = edges()
            part[2, 0] = part[2, 0] + at_xz
            part[0, last] = part[0, last] + at_zx

        gain_0 = low_x * coef[1, 0]
        wait(step, E_XY, XQ)
        below_xy = rx[step, 1, 0] + DT * ez[0]
        below_xz = rx[step, 1, 1] - DT * ey[0] + jnp.where(jr == CY - 1, DT * rr[step, 1], zero)
        y_first = part[1, 0] + gain_0 * below_xz
        z_first = part[2, 0] - gain_0 * below_xy
        if step == 0:
            at_xz, at_zx = edges()
            z_first = z_first + at_xz
            part[0, last] = part[0, last] + at_zx
        e_ref[1, 0], e_ref[2, 0] = y_first, z_first
        if step < STEPS - 1:
            sx[step + 1, 0, 0] = y_first
            sx[step + 1, 0, 1] = z_first
            start(step + 1, XE)
        wait(step, E_YX, XE)
        more_y = (DT * top_x) * rx[step, 0, 1]
        more_z = (-DT * top_x) * rx[step, 0, 0]
        e_yx = rr[step, 2] * top_x
        y_more_z = jnp.where(jr == 0, (-DT * low_y) * e_yx, pltpu.roll(more_z, 1, 0))
        z_more_y = jnp.where(kr == 0, zero, pltpu.roll(more_y, 1, 1))
        gain = coef[1, last]
        x_last = part[0, last] + gain * ((more_z - y_more_z) - (more_y - z_more_y))
        y_last = part[1, last] - gain * more_z
        z_last = part[2, last] + gain * more_y
        hy_last = h_ref[1, last] + more_y
        hz_last = h_ref[2, last] + more_z
        h_ref[1, last], h_ref[2, last] = hy_last, hz_last
        e_ref[0, last], e_ref[1, last], e_ref[2, last] = x_last, y_last, z_last
        if step < STEPS - 1:
            send_sums(step + 1, x_last, y_last, z_last, hy_last, hz_last, y_first)
        e_ref[0, 0:last] = part[0, 0:last]
        e_ref[1, 1:last] = part[1, 1:last]
        e_ref[2, 1:last] = part[2, 1:last]

    def stress(step):
        ex, ey, ez = e_ref[0], e_ref[1], e_ref[2]
        hx, hy, hz = h_ref[0], h_ref[1], h_ref[2]
        g = g_ref[step]
        xx, yy, zz = ex * ex + hx * hx, ey * ey + hy * hy, ez * ez + hz * hz
        energy = 0.5 * (xx + yy + zz)
        found = (xx - energy, ex * ey + hx * hy, ex * ez + hx * hz, yy - energy, ey * ez + hy * hz, zz - energy)
        for n, value in enumerate(found):
            tensor[n] = g * value if step == 0 else tensor[n] + g * value

    def ranks_and_buckets():
        owner = owner_ref[...]
        block = SLOTS // 4
        groups = NGX * NGY
        earlier = (iota((block, block), 0) < iota((block, block), 1)).astype(F32).astype(BF16)
        lane = iota((1, block), 1)
        before = jnp.zeros((groups, 1), F32)
        made = jnp.zeros((5 * NNEAR, LANES), F32)
        for b in range(4):
            cut = slice(b * block, (b + 1) * block)
            own = owner[:, cut]
            hot = (own == iota((groups, block), 0)).astype(F32)
            ahead = dot(hot.astype(BF16), earlier, (1, 0)) + before
            rank = jnp.sum(ahead * hot, axis=0, keepdims=True).astype(jnp.int32)
            before = before + jnp.sum(hot, axis=1, keepdims=True)
            place = rank * NFAR + (lax.shift_right_logical(own, 1) & (NFAR - 1))
            place_hot = (place == iota((LANES, block), 0)).astype(F32).astype(BF16)
            cell, normal = cell_ref[:, cut], normal_ref[:, cut]
            live = (lane + b * block < count_ref[0, 0, 0]).astype(F32)
            weight = live * (FACE_AREA * (1 - 2 * (normal & 1)).astype(F32))
            mine = lax.shift_right_logical(own, 5) * CORES + (own & 1) == iota((NNEAR, block), 0)
            entries = (
                (cell & 127).astype(F32),
                lax.shift_right_logical(cell, 7).astype(F32),
                weight,
                lax.shift_right_logical(normal, 1).astype(F32),
                tile_ref[:, cut].astype(F32),
            )
            rows = jnp.concatenate([jnp.where(mine, entry, zero) for entry in entries], 0)
            made = made + dot(rows.astype(BF16), place_hot, (1, 1))
        for n in range(5):
            bucket[n] = made[n * NNEAR : (n + 1) * NNEAR].reshape(NNEAR, 1, LANES)
        stl[...] = bucket[4]

    def to_near(src, dst, send, recv, d):
        n = lax.rem(near + d, NNEAR)
        return pltpu.make_async_remote_copy(
            src_ref=src.at[n],
            dst_ref=dst.at[near],
            send_sem=send.at[d],
            recv_sem=recv.at[d],
            device_id=near_at(n),
            device_id_type=MESH,
        )

    def from_near(src, dst, send, recv, d):
        n = lax.rem(near + NNEAR - d, NNEAR)
        return pltpu.make_async_remote_copy(
            src_ref=src.at[n],
            dst_ref=dst.at[n],
            send_sem=send.at[d],
            recv_sem=recv.at[d],
            device_id=near_at(n),
            device_id_type=MESH,
        )

    def lane_hots():
        for n in range(NNEAR):
            lane_hot[n] = (bucket[0, n] == iota((CZ, LANES), 0).astype(F32)).astype(F32).astype(BF16)

    def tile_hots():
        for d in range(1, NNEAR):
            from_near(stl, rtl, ts_sem, tr_sem, d).wait_recv()
        for n in range(NNEAR):
            tile_hot[n] = (rtl[n] == iota((TILE_DEV, LANES), 0).astype(F32)).astype(F32).astype(BF16)

    def coefficients():
        material = mat_ref[...]

        def of_material(table):
            result = jnp.where(material == 0, table[0], zero)
            for which in (1, 2):
                result = jnp.where(material == which, table[which], result)
            return result

        sigma, gamma, plasma = of_material(sig_ref), of_material(gam_ref), of_material(pla_ref)
        coef[0] = (1.0 - sigma * DT / 2) / (1.0 + sigma * DT / 2)
        coef[1] = DT / (1.0 + sigma * DT / 2)
        coef[2] = (1.0 - gamma * DT / 2) / (1.0 + gamma * DT / 2)
        coef[3] = plasma * DT / (1.0 + gamma * DT / 2)

    loads[0].wait()
    loads[1].wait()
    pl.semaphore_wait(barrier, greeted)

    for step in range(STEPS):
        if step == 0:
            send_x()
        send_yz(step)
        if step == 0:
            for load in loads[2:]:
                load.wait()
            coefficients()
            sg[0] = as_row(coef[1, CX - 1, :, 0:1])
            sg[1] = as_row(coef[1, 0, :, CZ - 1 : CZ])
            for n in range(2):
                edge_gain(n).start()
            current(step)
            ranks_and_buckets()
            for d in range(1, NNEAR):
                to_near(stl, rtl, ts_sem, tr_sem, d).start()
            rtl[near] = stl[near]
        else:
            current(step)
            stress(step - 1)
        if step == 1:
            lane_hots()
        if step == 2:
            tile_hots()
        update(step)
    stores = [
        pltpu.make_async_copy(src, dst, out_sem.at[n]) for n, (src, dst) in enumerate(((e_ref, e_out), (h_ref, h_out)))
    ]
    for store in stores:
        store.start()
    stress(STEPS - 1)

    cells = CX * CY
    high, low = halves(tensor[...].reshape(6 * cells, CZ))
    parts = jnp.concatenate([high, low], 1)
    for n in range(NNEAR):
        hot = lane_hot[n]
        read = dot(parts, jnp.concatenate([hot, hot], 0), (1, 0))
        row = bucket[1, n] == iota((cells, LANES), 0).astype(F32)
        xx, xy, xz, yy, yz, zz = [
            jnp.sum(jnp.where(row, read[c * cells : (c + 1) * cells], zero), axis=0, keepdims=True) for c in range(6)
        ]
        axis, weight = bucket[3, n], bucket[2, n]
        along_x, along_y = axis == 0.0, axis == 1.0
        sval[n, 0:1] = weight * jnp.where(along_x, xx, jnp.where(along_y, xy, xz))
        sval[n, 1:2] = weight * jnp.where(along_x, xy, jnp.where(along_y, yy, yz))
        sval[n, 2:3] = weight * jnp.where(along_x, xz, jnp.where(along_y, yz, zz))
    for d in range(1, NNEAR):
        to_near(sval, rval, vs_sem, vr_sem, d).start()
    rval[near] = sval[near]

    for d in range(1, NNEAR):
        from_near(sval, rval, vs_sem, vr_sem, d).wait_recv()
    rows = (NFAR * 8, LANES)
    mine = (lax.shift_right_logical(iota(rows, 0), 3) == (iota(rows, 1) & (NFAR - 1))).astype(F32)
    dense = jnp.zeros((NFAR * 8, TILE_DEV), F32)
    for n in range(NNEAR):
        value = rval[n]
        high = value.astype(BF16).astype(F32)
        both = jnp.concatenate([high, value - high, jnp.zeros((2, LANES), F32)], 0)
        spread = (jnp.concatenate([both] * NFAR, 0) * mine).astype(BF16)
        dense = dense + dot(spread, tile_hot[n], (1, 1))
    dense = dense.reshape(NFAR, 8, TILE_DEV)
    sdense[...] = dense[:, 0:3] + dense[:, 3:6]

    def to_far(d):
        n = lax.rem(far + d, NFAR)
        return pltpu.make_async_remote_copy(
            src_ref=sdense.at[n],
            dst_ref=rdense.at[far],
            send_sem=ds_sem.at[d],
            recv_sem=dr_sem.at[d],
            device_id=far_at(n),
            device_id_type=MESH,
        )

    def from_far(d):
        n = lax.rem(far + NFAR - d, NFAR)
        return pltpu.make_async_remote_copy(
            src_ref=sdense.at[n],
            dst_ref=rdense.at[n],
            send_sem=ds_sem.at[d],
            recv_sem=dr_sem.at[d],
            device_id=far_at(n),
            device_id_type=MESH,
        )

    for d in (8, 7, 9, 6, 10, 5, 11, 4, 12, 3, 13, 2, 14, 1, 15):
        to_far(d).start()
    rdense[far] = sdense[far]
    for step in range(STEPS):
        for which in range(12):
            when(ROUTES[which][1], lambda which=which: message(step, which).wait_send())
    for n in range(2):
        edge_gain(n).wait_send()
    for d in range(1, NNEAR):
        to_near(stl, rtl, ts_sem, tr_sem, d).wait_send()
        to_near(sval, rval, vs_sem, vr_sem, d).wait_send()
    for d in range(1, NFAR):
        to_far(d).wait_send()
    for store in stores:
        store.wait()
    for d in range(1, NFAR):
        from_far(d).wait_recv()
    force_ref[...] = jnp.sum(rdense[...], axis=0)


def hand_out(*refs):
    sem = refs[-1]
    copies = [pltpu.make_async_copy(refs[n], refs[n + 3], sem.at[n]) for n in range(3)]
    for copy in copies:
        copy.start()
    for copy in copies:
        copy.wait()


def local(
    e_field,
    h_field,
    current,
    material,
    sigma_table,
    gamma_table,
    plasma_table,
    g_kernel,
    surf_cell,
    surf_owner,
    surf_tile,
    surf_normal,
    row_count,
):
    field = jax.ShapeDtypeStruct((3, CX, CY, CZ), F32)
    hbm = pl.BlockSpec(memory_space=pltpu.HBM)
    dma = pltpu.SemaphoreType.DMA
    slots = [a.reshape(1, SLOTS) for a in (surf_cell, surf_owner, surf_tile, surf_normal)]
    operands = (e_field, h_field, current, material, *slots)
    operands += (sigma_table, gamma_table, plasma_table, g_kernel)
    operands = [pltpu.with_memory_space_constraint(a, pltpu.HBM) for a in operands]
    shapes = (field, field, jax.ShapeDtypeStruct((3, TILE_DEV), F32))
    made = pl.pallas_call(
        kernel,
        out_shape=shapes,
        in_specs=[hbm] * 12 + [pl.BlockSpec(memory_space=pltpu.SMEM)],
        out_specs=(hbm, hbm, pl.BlockSpec(memory_space=pltpu.VMEM)),
        scratch_shapes=[
            pltpu.VMEM((3, CX, CY, CZ), F32),
            pltpu.VMEM((3, CX, CY, CZ), F32),
            pltpu.VMEM((3, CX, CY, CZ), F32),
            pltpu.VMEM((3, CX, CY, CZ), F32),
            pltpu.VMEM((CX, CY, CZ), jnp.int32),
            pltpu.VMEM((1, SLOTS), jnp.int32),
            pltpu.VMEM((1, SLOTS), jnp.int32),
            pltpu.VMEM((1, SLOTS), jnp.int32),
            pltpu.VMEM((1, SLOTS), jnp.int32),
            pltpu.SMEM((3,), F32),
            pltpu.SMEM((3,), F32),
            pltpu.SMEM((3,), F32),
            pltpu.SMEM((STEPS,), F32),
            pltpu.VMEM((4, CX, CY, CZ), F32),
            pltpu.VMEM((6, CX, CY, CZ), F32),
            pltpu.VMEM((STEPS, 2, 2, CY, CZ), F32),
            pltpu.VMEM((STEPS, 2, 2, CY, CZ), F32),
            pltpu.VMEM((STEPS, 6, CX, 1, CZ), F32),
            pltpu.VMEM((STEPS, 6, CX, 1, CZ), F32),
            pltpu.VMEM((STEPS, 2, 8, CZ), F32),
            pltpu.VMEM((STEPS, 2, 8, CZ), F32),
            pltpu.VMEM((STEPS, 4, 1, CZ), F32),
            pltpu.VMEM((STEPS, 4, 1, CZ), F32),
            pltpu.VMEM((2, 1, CZ), F32),
            pltpu.VMEM((2, 1, CZ), F32),
            pltpu.VMEM((2, CY, CZ), F32),
            pltpu.VMEM((5, NNEAR, 1, LANES), F32),
            pltpu.VMEM((NNEAR, CZ, LANES), BF16),
            pltpu.VMEM((NNEAR, TILE_DEV, LANES), BF16),
            pltpu.VMEM((NNEAR, 1, LANES), F32),
            pltpu.VMEM((NNEAR, 1, LANES), F32),
            pltpu.VMEM((NNEAR, 3, LANES), F32),
            pltpu.VMEM((NNEAR, 3, LANES), F32),
            pltpu.VMEM((NFAR, 3, TILE_DEV), F32),
            pltpu.VMEM((NFAR, 3, TILE_DEV), F32),
            dma((12,)),
            dma((2,)),
            dma((STEPS, 12)),
            dma((STEPS, 12)),
            dma((NNEAR,)),
            dma((NNEAR,)),
            dma((NNEAR,)),
            dma((NNEAR,)),
            dma((NFAR,)),
            dma((NFAR,)),
            dma((2,)),
            dma((2,)),
        ],
        compiler_params=pltpu.CompilerParams(
            collective_id=0, has_side_effects=True, vmem_limit_bytes=24 * 2**20
        ),
    )(*operands, row_count)
    return pl.pallas_call(
        hand_out,
        out_shape=shapes,
        in_specs=[hbm] * 3,
        out_specs=(hbm,) * 3,
        scratch_shapes=[dma((3,))],
        compiler_params=pltpu.CompilerParams(vmem_limit_bytes=24 * 2**20),
    )(*made)


def solution(mesh):
    cells = P("gx", "gy", "gz")
    field = P(None, "gx", "gy", "gz")
    slots = P("gx", "gy", "gz", None)
    return jax.shard_map(
        local,
        mesh=mesh,
        in_specs=(
            field,
            field,
            field,
            cells,
            P(),
            P(),
            P(),
            P(),
            slots,
            P("gx", "gy", "gz", None, None),
            slots,
            slots,
            cells,
        ),
        out_specs=(field, field, P(None, ("gx", "gy", "gz"))),
        check_vma=False,
    )
```

```python
import functools

import jax
import jax.numpy as jnp
from jax import lax
from jax.experimental import pallas as pl
from jax.experimental.pallas import tpu as pltpu
from jax.sharding import PartitionSpec as P

MESH = pl.DeviceIdType.MESH
F32 = jnp.float32
BF16 = jnp.bfloat16

DT = 0.5
FACE_AREA = 0.25
STEPS = 4
CX, CY, CZ = 4, 16, 128
SLOTS = 1024
TILE_DEV = 128
NGX, NGY, NGZ = 16, 8, 4
NY_CHIPS, NZ_HI, NZ_LO, CORES = 4, 4, 4, 2
NNEAR, NFAR = NY_CHIPS * CORES, NZ_HI * NZ_LO
LANES = 16 * NFAR

(XE, XQ, YE, YQ, ZE, ZQ, E_XZ, E_XY, E_YZ, E_YX, E_ZY, E_ZX) = range(12)
ROUTES = (
    (-1, 0, 0),
    (1, 0, 0),
    (0, -1, 0),
    (0, 1, 0),
    (0, 0, -1),
    (0, 0, 1),
    (1, 0, -1),
    (1, -1, 0),
    (0, 1, -1),
    (-1, 1, 0),
    (0, -1, 1),
    (-1, 0, 1),
)


def iota(shape, axis):
    return lax.broadcasted_iota(jnp.int32, shape, axis)


def dot(a, b, contract):
    return lax.dot_general(a, b, ((contract[:1], contract[1:]), ((), ())), preferred_element_type=F32)


def halves(x):
    high = x.astype(BF16)
    return high, (x - high.astype(F32)).astype(BF16)


def kernel(
    e_in,
    h_in,
    j_in,
    mat_in,
    cell_in,
    owner_in,
    tile_in,
    normal_in,
    sig_in,
    gam_in,
    pla_in,
    g_in,
    count_ref,
    e_out,
    h_out,
    force_ref,
    e_ref,
    h_ref,
    j_ref,
    part,
    mat_ref,
    cell_ref,
    owner_ref,
    tile_ref,
    normal_ref,
    sig_ref,
    gam_ref,
    pla_ref,
    g_ref,
    coef,
    tensor,
    sx,
    rx,
    sy,
    ry,
    sz,
    rz,
    sr,
    rr,
    sg,
    rg,
    rest,
    bucket,
    lane_hot,
    tile_hot,
    stl,
    rtl,
    sval,
    rval,
    sdense,
    rdense,
    in_sem,
    out_sem,
    hs_sem,
    hr_sem,
    ts_sem,
    tr_sem,
    vs_sem,
    vr_sem,
    ds_sem,
    dr_sem,
    gs_sem,
    gr_sem,
):
    gx, gy, gz = lax.axis_index("gx"), lax.axis_index("gy"), lax.axis_index("gz")

    loads = [
        pltpu.make_async_copy(src, dst, in_sem.at[n])
        for n, (src, dst) in enumerate(
            (
                (e_in, e_ref),
                (h_in, h_ref),
                (j_in, j_ref),
                (mat_in, mat_ref),
                (sig_in, sig_ref),
                (gam_in, gam_ref),
                (pla_in, pla_ref),
                (g_in, g_ref),
                (cell_in, cell_ref),
                (owner_in, owner_ref),
                (tile_in, tile_ref),
                (normal_in, normal_ref),
            )
        )
    ]
    for load in loads[:2]:
        load.start()

    def at(dx, dy, dz):
        where = {}
        if dx:
            where["gx"] = gx + dx
        if dy:
            where["gy"] = gy + dy
        if dz:
            where["gz"] = lax.rem(gz + (dz + NGZ), NGZ)
        return where

    y_chip, z_hi = lax.div(gx, NZ_HI), lax.rem(gx, NZ_HI)
    z_lo, core = lax.div(gy, CORES), lax.rem(gy, CORES)
    near, far = y_chip * CORES + core, z_hi * NZ_LO + z_lo

    def near_at(n):
        return {"gx": lax.div(n, CORES) * NZ_HI + z_hi, "gy": z_lo * CORES + lax.rem(n, CORES)}

    def far_at(n):
        return {"gx": y_chip * NZ_HI + lax.div(n, NZ_LO), "gy": lax.rem(n, NZ_LO) * CORES + core}

    def inside(route, sign):
        has = [gx < NGX - 1 if sign * route[0] > 0 else gx > 0] if route[0] else []
        has += [gy < NGY - 1 if sign * route[1] > 0 else gy > 0] if route[1] else []
        return has

    def when(route, sign, do):
        has = inside(route, sign)
        if has:
            pl.when(functools.reduce(jnp.logical_and, has))(do)
        else:
            do()

    barrier = pltpu.get_barrier_semaphore()

    def greet(where):
        pl.semaphore_signal(barrier, inc=1, device_id=where, device_id_type=MESH)

    for d in range(1, NZ_LO):
        greet({"gy": lax.rem(z_lo + d, NZ_LO) * CORES + core})
    for route in sorted(ROUTES, key=lambda r: -abs(r[0])):
        when(route, 1, functools.partial(lambda r: greet(at(*r)), route))
    for d in range(1, NNEAR):
        greet(near_at(lax.rem(near + d, NNEAR)))
    for load in loads[2:]:
        load.start()
    greeted = NNEAR - 1 + NZ_LO - 1
    for route in ROUTES:
        found = 1
        for has in inside(route, 1):
            found = found * jnp.where(has, 1, 0)
        greeted = greeted + found

    @pl.when(gx == NGX - 1)
    def _():
        for step in range(STEPS):
            rx[step, 0] = jnp.zeros((2, CY, CZ), F32)
            rr[step, 2] = jnp.zeros((1, CZ), F32)
            rr[step, 3] = jnp.zeros((1, CZ), F32)
        rg[1] = jnp.zeros((1, CZ), F32)

    @pl.when(gx == 0)
    def _():
        for step in range(STEPS):
            rx[step, 1] = jnp.zeros((2, CY, CZ), F32)
            rr[step, 0] = jnp.zeros((1, CZ), F32)
            rr[step, 1] = jnp.zeros((1, CZ), F32)
        rg[0] = jnp.zeros((1, CZ), F32)

    @pl.when(gy == NGY - 1)
    def _():
        for step in range(STEPS):
            ry[step, 0:2] = jnp.zeros((2, CX, 1, CZ), F32)
            ry[step, 5] = jnp.zeros((CX, 1, CZ), F32)
            rr[step, 1] = jnp.zeros((1, CZ), F32)

    @pl.when(gy == 0)
    def _():
        for step in range(STEPS):
            ry[step, 2:5] = jnp.zeros((3, CX, 1, CZ), F32)
            rr[step, 2] = jnp.zeros((1, CZ), F32)

    one, zero = jnp.float32(1.0), jnp.float32(0.0)
    low_x = jnp.where(gx > 0, one, zero)
    low_y = jnp.where(gy > 0, one, zero)
    low_z = jnp.where(gz > 0, one, zero)
    top_x = jnp.where(gx < NGX - 1, one, zero)
    top_y = jnp.where(gy < NGY - 1, one, zero)
    top_z = jnp.where(gz < NGZ - 1, one, zero)

    brick = (CX, CY, CZ)
    jj, kk = iota(brick, 1), iota(brick, 2)
    n_hot = (iota((16, 8, CZ), 0) == iota((16, 8, CZ), 2)).astype(F32)
    n_more = (iota((2, 8, CZ), 0) + 16 == iota((2, 8, CZ), 2)).astype(F32)
    row_hot = (iota((CY, CZ), 0) == iota((CY, CZ), 1)).astype(F32)

    def y_next(f):
        return pltpu.roll(f, CY - 1, 1)

    def z_next(f):
        return pltpu.roll(f, CZ - 1, 2)

    def packed(columns):
        return jnp.sum(columns.reshape(16, 8, -1) * n_hot, axis=0)

    def unpacked(tile):
        return jnp.sum(tile[None] * n_hot, axis=2, keepdims=True).reshape(2, CX, CY, 1)

    def message(step, which):
        src, dst = {
            XE: (sx.at[step, 0], rx.at[step, 0]),
            XQ: (sx.at[step, 1], rx.at[step, 1]),
            YE: (sy.at[step, pl.ds(0, 2)], ry.at[step, pl.ds(0, 2)]),
            YQ: (sy.at[step, pl.ds(2, 2)], ry.at[step, pl.ds(2, 2)]),
            ZE: (sz.at[step, 0], rz.at[step, 0]),
            ZQ: (sz.at[step, 1], rz.at[step, 1]),
            E_XZ: (sr.at[step, 0], rr.at[step, 0]),
            E_XY: (sr.at[step, 1], rr.at[step, 1]),
            E_YX: (sr.at[step, 2], rr.at[step, 2]),
            E_ZX: (sr.at[step, 3], rr.at[step, 3]),
            E_YZ: (sy.at[step, 4], ry.at[step, 4]),
            E_ZY: (sy.at[step, 5], ry.at[step, 5]),
        }[which]
        return pltpu.make_async_remote_copy(
            src_ref=src,
            dst_ref=dst,
            send_sem=hs_sem.at[step, which],
            recv_sem=hr_sem.at[step, which],
            device_id=at(*ROUTES[which]),
            device_id_type=MESH,
        )

    def start(step, *which):
        for n in which:
            when(ROUTES[n], 1, lambda n=n: message(step, n).start())

    def as_row(column):
        return jnp.sum(column * row_hot, axis=0, keepdims=True)

    def as_column(row):
        return jnp.sum(row * row_hot, axis=1, keepdims=True)

    def send_edges(step, xz, zx):
        sr[step, 0] = as_row(xz)
        sr[step, 3] = as_row(zx)
        start(step, E_XZ, E_ZX)

    def edge_gain(n):
        return pltpu.make_async_remote_copy(
            src_ref=sg.at[n],
            dst_ref=rg.at[n],
            send_sem=gs_sem.at[n],
            recv_sem=gr_sem.at[n],
            device_id=at(*ROUTES[(E_XZ, E_ZX)[n]]),
            device_id_type=MESH,
        )

    def send_sums(step, ex, ey, ez, hy, hz):
        y_ex = jnp.where(jj[0] == CY - 1, zero, pltpu.roll(ex, CY - 1, 0))
        z_ex = jnp.where(kk[0] == CZ - 1, zero, pltpu.roll(ex, CZ - 1, 1))
        sx[step, 1, 0] = hy - DT * ((z_ex - ex) + ez)
        sx[step, 1, 1] = hz + DT * (ey + (y_ex - ex))
        start(step, XQ)
        sr[step, 1] = ex[0:1, :]
        start(step, E_XY)

    def send_x():
        last = CX - 1
        ey, ez = e_ref[1, 0], e_ref[2, 0]
        send_edges(0, e_ref[0, last, :, 0:1], ez[:, CZ - 1 : CZ])
        sx[0, 0, 0] = ey
        sx[0, 0, 1] = ez
        start(0, XE)
        send_sums(0, e_ref[0, last], e_ref[1, last], e_ref[2, last], h_ref[1, last], h_ref[2, last])
        sr[0, 2] = ey[CY - 1 : CY, :]
        start(0, E_YX)

    def send_yz(step):
        ex, ey, ez = e_ref[0], e_ref[1], e_ref[2]
        nothing = jnp.zeros((1, CY, CZ), F32)
        last_y, last_z = jj == CY - 1, kk == CZ - 1
        y_ez = jnp.where(last_y, zero, y_next(ez))
        y_ex = jnp.where(last_y, zero, y_next(ex))
        z_ey = jnp.where(last_z, zero, z_next(ey))
        z_ex = jnp.where(last_z, zero, z_next(ex))
        x_ez = jnp.concatenate([ez[1:], nothing], 0)
        x_ey = jnp.concatenate([ey[1:], nothing], 0)
        hx = h_ref[0] - DT * ((y_ez - ez) - (z_ey - ey))
        hy = h_ref[1] - DT * ((z_ex - ex) - (x_ez - ez))
        hz = h_ref[2] - DT * ((x_ey - ey) - (y_ex - ex))
        part[0], part[1], part[2] = hx, hy, hz
        sz[step, 0] = packed(e_ref[0:2][:, :, :, 0:1]) + jnp.sum(ez[0].reshape(2, 8, CZ)[:, :, 0:1] * n_more, axis=0)
        sz[step, 1] = packed(part[0:2][:, :, :, CZ - 1 : CZ])
        start(step, ZE, ZQ)
        sy[step, 0] = ex[:, 0:1, :]
        sy[step, 1] = ez[:, 0:1, :]
        sy[step, 2] = hx[:, CY - 1 : CY, :]
        sy[step, 3] = hz[:, CY - 1 : CY, :]
        sy[step, 4] = ey[:, CY - 1 : CY, :]
        sy[step, 5] = ez[:, 0:1, :]
        start(step, YE, YQ, E_YZ, E_ZY)

    def wait(step, *which):
        for n in which:
            when(ROUTES[n], -1, lambda n=n: message(step, n).wait_recv())

    def current(step):
        j_ref[...] = coef[2][None] * j_ref[...] + coef[3][None] * e_ref[...]

    def update(step):
        last = CX - 1
        wait(step, ZE, ZQ, YE, YQ, E_YZ, E_ZY)
        ex, ey, ez = e_ref[0], e_ref[1], e_ref[2]
        hx, hy, hz = part[0], part[1], part[2]
        above_y = ry[step, 0:2]
        above_z = unpacked(rz[step, 0]) * top_z
        last_y, last_z = jj == CY - 1, kk == CZ - 1
        hx = hx + jnp.where(last_z, DT * above_z[1], zero) - jnp.where(last_y, DT * above_y[1], zero)
        hy = hy - jnp.where(last_z, DT * above_z[0], zero)
        hz = hz + jnp.where(last_y, DT * above_y[0], zero)
        e_yz = ry[step, 4] * top_z
        e_zy = ry[step, 5]
        ky, jz = iota((CX, 1, CZ), 2), iota((CX, CY, 1), 1)
        below_yx = ry[step, 2] - DT * ez[:, 0:1, :] + jnp.where(ky == CZ - 1, DT * e_yz[:, :, 0:1], zero)
        below_yz = ry[step, 3] + DT * ex[:, 0:1, :]
        below_z = unpacked(rz[step, 1])
        below_zx = below_z[0] + DT * ey[:, :, 0:1] - jnp.where(jz == CY - 1, DT * e_zy[:, :, CZ - 1 : CZ], zero)
        below_zy = below_z[1] - DT * ex[:, :, 0:1]
        first_y, first_z = jj == 0, kk == 0
        y_hx = jnp.where(first_y, low_y * below_yx, pltpu.roll(hx, 1, 1))
        y_hz = jnp.where(first_y, low_y * below_yz, pltpu.roll(hz, 1, 1))
        z_hx = jnp.where(first_z, low_z * below_zx, pltpu.roll(hx, 1, 2))
        z_hy = jnp.where(first_z, low_z * below_zy, pltpu.roll(hy, 1, 2))
        nothing = jnp.zeros((1, CY, CZ), F32)
        x_hy = jnp.concatenate([nothing, hy[:last]], 0)
        x_hz = jnp.concatenate([nothing, hz[:last]], 0)
        keep, gain = coef[0], coef[1]
        part[0] = keep * ex + gain * (((hz - y_hz) - (hy - z_hy)) - j_ref[0])
        part[1] = keep * ey + gain * (((hx - z_hx) - (hz - x_hz)) - j_ref[1])
        part[2] = keep * ez + gain * (((hy - x_hy) - (hx - y_hx)) - j_ref[2])
        h_ref[0], h_ref[1], h_ref[2] = hx, hy, hz
        jr, kr = jj[0], kk[0]
        if step < STEPS - 1:
            send_edges(step + 1, part[0, last, :, 0:1], part[2, 0, :, CZ - 1 : CZ])

        def edges():
            wait(step, E_XZ, E_ZX)
            e_xz, e_zx = as_column(rr[step, 0]), as_column(rr[step, 3])
            if step == 1:
                for n in range(2):
                    when(ROUTES[(E_XZ, E_ZX)[n]], -1, edge_gain(n).wait_recv)
            if step:
                e_xz = e_xz + as_column(rg[0]) * rest[0]
                e_zx = e_zx - as_column(rg[1]) * rest[1]
            e_xz, e_zx = e_xz * (DT * top_z), e_zx * (DT * top_x)
            if step < STEPS - 1:
                more_z = jnp.broadcast_to(-DT * above_z[1, 0], (CY, CZ))
                y_more_z = jnp.where(jr == 0, -DT * e_yz[0, :, 0:1], pltpu.roll(more_z, 1, 0))
                more_y = DT * jnp.sum(rz[step, 0][None] * n_more, axis=2, keepdims=True).reshape(CY, 1)
                rest[0] = (more_z - y_more_z) - (more_y - DT * ez[0, :, CZ - 1 : CZ])
                rest[1] = jnp.broadcast_to(below_zy[last] + e_zx, (CY, CZ))
            at_xz = jnp.where(kr == CZ - 1, low_x * coef[1, 0] * e_xz, zero)
            at_zx = jnp.where(kr == 0, low_z * coef[1, last] * e_zx, zero)
            return at_xz, at_zx

        if step:
            at_xz, at_zx = edges()
            part[2, 0] = part[2, 0] + at_xz
            part[0, last] = part[0, last] + at_zx

        later = step < STEPS - 1
        gain_0, gain = low_x * coef[1, 0], coef[1, last]
        if step == 0:
            at_xz, at_zx = edges()
            part[2, 0] = part[2, 0] + at_xz
            part[0, last] = part[0, last] + at_zx

        def first_plane():
            wait(step, E_XY, XQ)
            below_xy = rx[step, 1, 0] + DT * ez[0]
            below_xz = rx[step, 1, 1] - DT * ey[0] + jnp.where(jr == CY - 1, DT * rr[step, 1], zero)
            y_first = part[1, 0] + gain_0 * below_xz
            z_first = part[2, 0] - gain_0 * below_xy
            if later:
                sx[step + 1, 0, 0] = y_first
                sx[step + 1, 0, 1] = z_first
                start(step + 1, XE)
                sr[step + 1, 2] = y_first[CY - 1 : CY, :]
                start(step + 1, E_YX)
            e_ref[1, 0], e_ref[2, 0] = y_first, z_first

        def last_plane():
            wait(step, E_YX, XE)
            more_y = (DT * top_x) * rx[step, 0, 1]
            more_z = (-DT * top_x) * rx[step, 0, 0]
            e_yx = rr[step, 2] * top_x
            y_more_z = jnp.where(jr == 0, (-DT * low_y) * e_yx, pltpu.roll(more_z, 1, 0))
            z_more_y = jnp.where(kr == 0, zero, pltpu.roll(more_y, 1, 1))
            x_last = part[0, last] + gain * ((more_z - y_more_z) - (more_y - z_more_y))
            y_last = part[1, last] - gain * more_z
            z_last = part[2, last] + gain * more_y
            hy_last = h_ref[1, last] + more_y
            hz_last = h_ref[2, last] + more_z
            if later:
                send_sums(step + 1, x_last, y_last, z_last, hy_last, hz_last)
            h_ref[1, last], h_ref[2, last] = hy_last, hz_last
            e_ref[0, last], e_ref[1, last], e_ref[2, last] = x_last, y_last, z_last

        for plane in (first_plane, last_plane):
            plane()
        e_ref[0, 0:last] = part[0, 0:last]
        e_ref[1, 1:last] = part[1, 1:last]
        e_ref[2, 1:last] = part[2, 1:last]

    def stress(step):
        ex, ey, ez = e_ref[0], e_ref[1], e_ref[2]
        hx, hy, hz = h_ref[0], h_ref[1], h_ref[2]
        g = g_ref[step]
        xx, yy, zz = ex * ex + hx * hx, ey * ey + hy * hy, ez * ez + hz * hz
        energy = 0.5 * (xx + yy + zz)
        found = (xx - energy, ex * ey + hx * hy, ex * ez + hx * hz, yy - energy, ey * ez + hy * hz, zz - energy)
        for n, value in enumerate(found):
            tensor[n] = g * value if step == 0 else tensor[n] + g * value

    def ranks_and_buckets():
        owner = owner_ref[...]
        block = SLOTS // 4
        groups = NGX * NGY
        earlier = (iota((block, block), 0) < iota((block, block), 1)).astype(F32).astype(BF16)
        lane = iota((1, block), 1)
        before = jnp.zeros((groups, 1), F32)
        made = jnp.zeros((5 * NNEAR, LANES), F32)
        for b in range(4):
            cut = slice(b * block, (b + 1) * block)
            own = owner[:, cut]
            hot = (own == iota((groups, block), 0)).astype(F32)
            ahead = dot(hot.astype(BF16), earlier, (1, 0)) + before
            rank = jnp.sum(ahead * hot, axis=0, keepdims=True).astype(jnp.int32)
            before = before + jnp.sum(hot, axis=1, keepdims=True)
            place = rank * NFAR + (lax.shift_right_logical(own, 1) & (NFAR - 1))
            place_hot = (place == iota((LANES, block), 0)).astype(F32).astype(BF16)
            cell, normal = cell_ref[:, cut], normal_ref[:, cut]
            live = (lane + b * block < count_ref[0, 0, 0]).astype(F32)
            weight = live * (FACE_AREA * (1 - 2 * (normal & 1)).astype(F32))
            mine = lax.shift_right_logical(own, 5) * CORES + (own & 1) == iota((NNEAR, block), 0)
            entries = (
                (cell & 127).astype(F32),
                lax.shift_right_logical(cell, 7).astype(F32),
                weight,
                lax.shift_right_logical(normal, 1).astype(F32),
                tile_ref[:, cut].astype(F32),
            )
            rows = jnp.concatenate([jnp.where(mine, entry, zero) for entry in entries], 0)
            made = made + dot(rows.astype(BF16), place_hot, (1, 1))
        for n in range(5):
            bucket[n] = made[n * NNEAR : (n + 1) * NNEAR].reshape(NNEAR, 1, LANES)
        stl[...] = bucket[4]

    def toward(k):
        return lax.rem(y_chip + k // CORES, NY_CHIPS) * CORES + lax.rem(core + k % CORES, CORES)

    def origin(k):
        return lax.rem(y_chip + NY_CHIPS - k // CORES, NY_CHIPS) * CORES + lax.rem(core + k % CORES, CORES)

    def to_near(src, dst, send, recv, k):
        return pltpu.make_async_remote_copy(
            src_ref=src,
            dst_ref=dst.at[near],
            send_sem=send.at[k],
            recv_sem=recv.at[k],
            device_id=near_at(toward(k)),
            device_id_type=MESH,
        )

    def from_near(dst, send, recv, k):
        n = origin(k)
        return pltpu.make_async_remote_copy(
            src_ref=dst.at[n],
            dst_ref=dst.at[n],
            send_sem=send.at[k],
            recv_sem=recv.at[k],
            device_id=near_at(n),
            device_id_type=MESH,
        )

    def tiles_to(k):
        return to_near(stl.at[toward(k)], rtl, ts_sem, tr_sem, k)

    def values_to(k):
        return to_near(sval.at[k], rval, vs_sem, vr_sem, k)

    def lane_hots():
        for n in range(NNEAR):
            lane_hot[n] = (bucket[0, n] == iota((CZ, LANES), 0).astype(F32)).astype(F32).astype(BF16)

    def tile_hots():
        for d in range(1, NNEAR):
            from_near(rtl, ts_sem, tr_sem, d).wait_recv()
        for n in range(NNEAR):
            tile_hot[n] = (rtl[n] == iota((TILE_DEV, LANES), 0).astype(F32)).astype(F32).astype(BF16)

    def coefficients():
        material = mat_ref[...]

        def of_material(table):
            result = jnp.where(material == 0, table[0], zero)
            for which in (1, 2):
                result = jnp.where(material == which, table[which], result)
            return result

        sigma, gamma, plasma = of_material(sig_ref), of_material(gam_ref), of_material(pla_ref)
        coef[0] = (1.0 - sigma * DT / 2) / (1.0 + sigma * DT / 2)
        coef[1] = DT / (1.0 + sigma * DT / 2)
        coef[2] = (1.0 - gamma * DT / 2) / (1.0 + gamma * DT / 2)
        coef[3] = plasma * DT / (1.0 + gamma * DT / 2)

    loads[0].wait()
    loads[1].wait()
    pl.semaphore_wait(barrier, greeted)

    for step in range(STEPS):
        if step == 0:
            send_x()
        send_yz(step)
        if step == 0:
            for load in loads[2:]:
                load.wait()
            coefficients()
            sg[0] = as_row(coef[1, CX - 1, :, 0:1])
            sg[1] = as_row(coef[1, 0, :, CZ - 1 : CZ])
            for n in range(2):
                when(ROUTES[(E_XZ, E_ZX)[n]], 1, edge_gain(n).start)
            current(step)
            ranks_and_buckets()
            for d in range(1, NNEAR):
                tiles_to(d).start()
            rtl[near] = stl[near]
        else:
            current(step)
            stress(step - 1)
        if step == 1:
            lane_hots()
        if step == 2:
            tile_hots()
        update(step)
    stores = [
        pltpu.make_async_copy(src, dst, out_sem.at[n]) for n, (src, dst) in enumerate(((e_ref, e_out), (h_ref, h_out)))
    ]
    for store in stores:
        store.start()
    stress(STEPS - 1)

    cells = CX * CY
    high, low = halves(tensor[...].reshape(6 * cells, CZ))
    parts = jnp.concatenate([high, low], 1)
    for k in (4, 5, 2, 3, 6, 7, 1, 0):
        n = toward(k)
        hot = lane_hot[n]
        read = dot(parts, jnp.concatenate([hot, hot], 0), (1, 0))
        row = bucket[1, n] == iota((cells, LANES), 0).astype(F32)
        xx, xy, xz, yy, yz, zz = [
            jnp.sum(jnp.where(row, read[c * cells : (c + 1) * cells], zero), axis=0, keepdims=True) for c in range(6)
        ]
        axis, weight = bucket[3, n], bucket[2, n]
        along_x, along_y = axis == 0.0, axis == 1.0
        sval[k, 0:1] = weight * jnp.where(along_x, xx, jnp.where(along_y, xy, xz))
        sval[k, 1:2] = weight * jnp.where(along_x, xy, jnp.where(along_y, yy, yz))
        sval[k, 2:3] = weight * jnp.where(along_x, xz, jnp.where(along_y, yz, zz))
        if k:
            values_to(k).start()
    rval[near] = sval[0]

    rows = (NFAR * 8, LANES)
    mine = (lax.shift_right_logical(iota(rows, 0), 3) == (iota(rows, 1) & (NFAR - 1))).astype(F32)
    dense = jnp.zeros((NFAR * 8, TILE_DEV), F32)
    for k in (0, 1, 2, 3, 6, 7, 4, 5):
        n = origin(k)
        if k:
            from_near(rval, vs_sem, vr_sem, k).wait_recv()
        value = rval[n]
        high = value.astype(BF16).astype(F32)
        both = jnp.concatenate([high, value - high, jnp.zeros((2, LANES), F32)], 0)
        spread = (jnp.concatenate([both] * NFAR, 0) * mine).astype(BF16)
        dense = dense + dot(spread, tile_hot[n], (1, 1))
    dense = dense.reshape(NFAR, 8, TILE_DEV)
    sdense[...] = dense[:, 0:3] + dense[:, 3:6]

    def to_far(d):
        n = lax.rem(far + d, NFAR)
        return pltpu.make_async_remote_copy(
            src_ref=sdense.at[n],
            dst_ref=rdense.at[far],
            send_sem=ds_sem.at[d],
            recv_sem=dr_sem.at[d],
            device_id=far_at(n),
            device_id_type=MESH,
        )

    def from_far(d):
        n = lax.rem(far + NFAR - d, NFAR)
        return pltpu.make_async_remote_copy(
            src_ref=sdense.at[n],
            dst_ref=rdense.at[n],
            send_sem=ds_sem.at[d],
            recv_sem=dr_sem.at[d],
            device_id=far_at(n),
            device_id_type=MESH,
        )

    for d in (8, 7, 9, 6, 10, 5, 11, 4, 12, 3, 13, 2, 14, 1, 15):
        to_far(d).start()
    rdense[far] = sdense[far]
    for step in range(STEPS):
        for which in range(12):
            when(ROUTES[which], 1, lambda which=which: message(step, which).wait_send())
    for n in range(2):
        when(ROUTES[(E_XZ, E_ZX)[n]], 1, edge_gain(n).wait_send)
    for d in range(1, NNEAR):
        tiles_to(d).wait_send()
        values_to(d).wait_send()
    for d in range(1, NFAR):
        to_far(d).wait_send()
    for store in stores:
        store.wait()
    for d in range(1, NFAR):
        from_far(d).wait_recv()
    force_ref[...] = jnp.sum(rdense[...], axis=0)


def hand_out(*refs):
    sem = refs[-1]
    copies = [pltpu.make_async_copy(refs[n], refs[n + 3], sem.at[n]) for n in range(3)]
    for copy in copies:
        copy.start()
    for copy in copies:
        copy.wait()


def local(
    e_field,
    h_field,
    current,
    material,
    sigma_table,
    gamma_table,
    plasma_table,
    g_kernel,
    surf_cell,
    surf_owner,
    surf_tile,
    surf_normal,
    row_count,
):
    field = jax.ShapeDtypeStruct((3, CX, CY, CZ), F32)
    hbm = pl.BlockSpec(memory_space=pltpu.HBM)
    dma = pltpu.SemaphoreType.DMA
    slots = [a.reshape(1, SLOTS) for a in (surf_cell, surf_owner, surf_tile, surf_normal)]
    operands = (e_field, h_field, current, material, *slots)
    operands += (sigma_table, gamma_table, plasma_table, g_kernel)
    operands = [pltpu.with_memory_space_constraint(a, pltpu.HBM) for a in operands]
    shapes = (field, field, jax.ShapeDtypeStruct((3, TILE_DEV), F32))
    made = pl.pallas_call(
        kernel,
        out_shape=shapes,
        in_specs=[hbm] * 12 + [pl.BlockSpec(memory_space=pltpu.SMEM)],
        out_specs=(hbm, hbm, pl.BlockSpec(memory_space=pltpu.VMEM)),
        scratch_shapes=[
            pltpu.VMEM((3, CX, CY, CZ), F32),
            pltpu.VMEM((3, CX, CY, CZ), F32),
            pltpu.VMEM((3, CX, CY, CZ), F32),
            pltpu.VMEM((3, CX, CY, CZ), F32),
            pltpu.VMEM((CX, CY, CZ), jnp.int32),
            pltpu.VMEM((1, SLOTS), jnp.int32),
            pltpu.VMEM((1, SLOTS), jnp.int32),
            pltpu.VMEM((1, SLOTS), jnp.int32),
            pltpu.VMEM((1, SLOTS), jnp.int32),
            pltpu.SMEM((3,), F32),
            pltpu.SMEM((3,), F32),
            pltpu.SMEM((3,), F32),
            pltpu.SMEM((STEPS,), F32),
            pltpu.VMEM((4, CX, CY, CZ), F32),
            pltpu.VMEM((6, CX, CY, CZ), F32),
            pltpu.VMEM((STEPS, 2, 2, CY, CZ), F32),
            pltpu.VMEM((STEPS, 2, 2, CY, CZ), F32),
            pltpu.VMEM((STEPS, 6, CX, 1, CZ), F32),
            pltpu.VMEM((STEPS, 6, CX, 1, CZ), F32),
            pltpu.VMEM((STEPS, 2, 8, CZ), F32),
            pltpu.VMEM((STEPS, 2, 8, CZ), F32),
            pltpu.VMEM((STEPS, 4, 1, CZ), F32),
            pltpu.VMEM((STEPS, 4, 1, CZ), F32),
            pltpu.VMEM((2, 1, CZ), F32),
            pltpu.VMEM((2, 1, CZ), F32),
            pltpu.VMEM((2, CY, CZ), F32),
            pltpu.VMEM((5, NNEAR, 1, LANES), F32),
            pltpu.VMEM((NNEAR, CZ, LANES), BF16),
            pltpu.VMEM((NNEAR, TILE_DEV, LANES), BF16),
            pltpu.VMEM((NNEAR, 1, LANES), F32),
            pltpu.VMEM((NNEAR, 1, LANES), F32),
            pltpu.VMEM((NNEAR, 3, LANES), F32),
            pltpu.VMEM((NNEAR, 3, LANES), F32),
            pltpu.VMEM((NFAR, 3, TILE_DEV), F32),
            pltpu.VMEM((NFAR, 3, TILE_DEV), F32),
            dma((12,)),
            dma((2,)),
            dma((STEPS, 12)),
            dma((STEPS, 12)),
            dma((NNEAR,)),
            dma((NNEAR,)),
            dma((NNEAR,)),
            dma((NNEAR,)),
            dma((NFAR,)),
            dma((NFAR,)),
            dma((2,)),
            dma((2,)),
        ],
        compiler_params=pltpu.CompilerParams(
            collective_id=0, has_side_effects=True, vmem_limit_bytes=24 * 2**20
        ),
    )(*operands, row_count)
    return pl.pallas_call(
        hand_out,
        out_shape=shapes,
        in_specs=[hbm] * 3,
        out_specs=(hbm,) * 3,
        scratch_shapes=[dma((3,))],
        compiler_params=pltpu.CompilerParams(vmem_limit_bytes=24 * 2**20),
    )(*made)


def solution(mesh):
    cells = P("gx", "gy", "gz")
    field = P(None, "gx", "gy", "gz")
    slots = P("gx", "gy", "gz", None)
    return jax.shard_map(
        local,
        mesh=mesh,
        in_specs=(
            field,
            field,
            field,
            cells,
            P(),
            P(),
            P(),
            P(),
            slots,
            P("gx", "gy", "gz", None, None),
            slots,
            slots,
            cells,
        ),
        out_specs=(field, field, P(None, ("gx", "gy", "gz"))),
        check_vma=False,
    )
```

```python
import functools

import jax
import jax.numpy as jnp
from jax import lax
from jax.experimental import pallas as pl
from jax.experimental.pallas import tpu as pltpu
from jax.sharding import PartitionSpec as P

MESH = pl.DeviceIdType.MESH
F32 = jnp.float32
BF16 = jnp.bfloat16

DT = 0.5
FACE_AREA = 0.25
STEPS = 4
CX, CY, CZ = 4, 16, 128
SLOTS = 1024
TILE_DEV = 128
NGX, NGY, NGZ = 16, 8, 4
NY_CHIPS, NZ_HI, NZ_LO, CORES = 4, 4, 4, 2
NNEAR, NFAR = NY_CHIPS * CORES, NZ_HI * NZ_LO
LANES = 16 * NFAR

(XE, XQ, YE, YQ, ZE, ZQ, E_XZ, E_XY, E_YZ, E_YX, E_ZY, E_ZX) = range(12)
ROUTES = (
    (-1, 0, 0),
    (1, 0, 0),
    (0, -1, 0),
    (0, 1, 0),
    (0, 0, -1),
    (0, 0, 1),
    (1, 0, -1),
    (1, -1, 0),
    (0, 1, -1),
    (-1, 1, 0),
    (0, -1, 1),
    (-1, 0, 1),
)


def iota(shape, axis):
    return lax.broadcasted_iota(jnp.int32, shape, axis)


def dot(a, b, contract):
    return lax.dot_general(a, b, ((contract[:1], contract[1:]), ((), ())), preferred_element_type=F32)


def halves(x):
    high = x.astype(BF16)
    return high, (x - high.astype(F32)).astype(BF16)


def kernel(
    e_in,
    h_in,
    j_in,
    mat_in,
    cell_in,
    owner_in,
    tile_in,
    normal_in,
    sig_in,
    gam_in,
    pla_in,
    g_in,
    count_ref,
    e_out,
    h_out,
    force_ref,
    e_ref,
    h_ref,
    j_ref,
    part,
    mat_ref,
    cell_ref,
    owner_ref,
    tile_ref,
    normal_ref,
    sig_ref,
    gam_ref,
    pla_ref,
    g_ref,
    coef,
    tensor,
    sx,
    rx,
    sy,
    ry,
    sz,
    rz,
    sr,
    rr,
    sg,
    rg,
    rest,
    bucket,
    lane_hot,
    tile_hot,
    stl,
    rtl,
    sval,
    rval,
    sdense,
    rdense,
    in_sem,
    out_sem,
    hs_sem,
    hr_sem,
    ts_sem,
    tr_sem,
    vs_sem,
    vr_sem,
    ds_sem,
    dr_sem,
    gs_sem,
    gr_sem,
):
    gx, gy, gz = lax.axis_index("gx"), lax.axis_index("gy"), lax.axis_index("gz")

    loads = [
        pltpu.make_async_copy(src, dst, in_sem.at[n])
        for n, (src, dst) in enumerate(
            (
                (e_in, e_ref),
                (h_in, h_ref),
                (j_in, j_ref),
                (mat_in, mat_ref),
                (sig_in, sig_ref),
                (gam_in, gam_ref),
                (pla_in, pla_ref),
                (g_in, g_ref),
                (cell_in, cell_ref),
                (owner_in, owner_ref),
                (tile_in, tile_ref),
                (normal_in, normal_ref),
            )
        )
    ]
    for load in loads[:2]:
        load.start()

    def at(dx, dy, dz):
        where = {}
        if dx:
            where["gx"] = gx + dx
        if dy:
            where["gy"] = gy + dy
        if dz:
            where["gz"] = gz + dz
        return where

    y_chip, z_hi = lax.div(gx, NZ_HI), lax.rem(gx, NZ_HI)
    z_lo, core = lax.div(gy, CORES), lax.rem(gy, CORES)
    near, far = y_chip * CORES + core, z_hi * NZ_LO + z_lo

    def near_at(n):
        return {"gx": lax.div(n, CORES) * NZ_HI + z_hi, "gy": z_lo * CORES + lax.rem(n, CORES)}

    def far_at(n):
        return {"gx": y_chip * NZ_HI + lax.div(n, NZ_LO), "gy": lax.rem(n, NZ_LO) * CORES + core}

    def inside(route, sign):
        has = [gx < NGX - 1 if sign * route[0] > 0 else gx > 0] if route[0] else []
        has += [gy < NGY - 1 if sign * route[1] > 0 else gy > 0] if route[1] else []
        has += [gz < NGZ - 1 if sign * route[2] > 0 else gz > 0] if route[2] else []
        return has

    def when(route, sign, do):
        has = inside(route, sign)
        if has:
            pl.when(functools.reduce(jnp.logical_and, has))(do)
        else:
            do()

    barrier = pltpu.get_barrier_semaphore()

    def greet(where):
        pl.semaphore_signal(barrier, inc=1, device_id=where, device_id_type=MESH)

    for d in range(1, NZ_LO):
        greet({"gy": lax.rem(z_lo + d, NZ_LO) * CORES + core})
    for route in sorted(ROUTES, key=lambda r: -abs(r[0])):
        when(route, 1, functools.partial(lambda r: greet(at(*r)), route))
    for d in range(1, NNEAR):
        greet(near_at(lax.rem(near + d, NNEAR)))
    for load in loads[2:]:
        load.start()
    greeted = NNEAR - 1 + NZ_LO - 1
    for route in ROUTES:
        found = 1
        for has in inside(route, 1):
            found = found * jnp.where(has, 1, 0)
        greeted = greeted + found

    @pl.when(gz == NGZ - 1)
    def _():
        for step in range(STEPS):
            rz[step, 0] = jnp.zeros((8, CZ), F32)
            ry[step, 4] = jnp.zeros((CX, 1, CZ), F32)
            rr[step, 0] = jnp.zeros((1, CZ), F32)
        rg[0] = jnp.zeros((1, CZ), F32)

    @pl.when(gz == 0)
    def _():
        for step in range(STEPS):
            rz[step, 1] = jnp.zeros((8, CZ), F32)
            ry[step, 5] = jnp.zeros((CX, 1, CZ), F32)
            rr[step, 3] = jnp.zeros((1, CZ), F32)
        rg[1] = jnp.zeros((1, CZ), F32)

    @pl.when(gx == NGX - 1)
    def _():
        for step in range(STEPS):
            rx[step, 0] = jnp.zeros((2, CY, CZ), F32)
            rr[step, 2] = jnp.zeros((1, CZ), F32)
            rr[step, 3] = jnp.zeros((1, CZ), F32)
        rg[1] = jnp.zeros((1, CZ), F32)

    @pl.when(gx == 0)
    def _():
        for step in range(STEPS):
            rx[step, 1] = jnp.zeros((2, CY, CZ), F32)
            rr[step, 0] = jnp.zeros((1, CZ), F32)
            rr[step, 1] = jnp.zeros((1, CZ), F32)
        rg[0] = jnp.zeros((1, CZ), F32)

    @pl.when(gy == NGY - 1)
    def _():
        for step in range(STEPS):
            ry[step, 0:2] = jnp.zeros((2, CX, 1, CZ), F32)
            ry[step, 5] = jnp.zeros((CX, 1, CZ), F32)
            rr[step, 1] = jnp.zeros((1, CZ), F32)

    @pl.when(gy == 0)
    def _():
        for step in range(STEPS):
            ry[step, 2:5] = jnp.zeros((3, CX, 1, CZ), F32)
            rr[step, 2] = jnp.zeros((1, CZ), F32)

    one, zero = jnp.float32(1.0), jnp.float32(0.0)
    low_x = jnp.where(gx > 0, one, zero)
    low_y = jnp.where(gy > 0, one, zero)
    low_z = jnp.where(gz > 0, one, zero)
    top_x = jnp.where(gx < NGX - 1, one, zero)
    top_y = jnp.where(gy < NGY - 1, one, zero)
    top_z = jnp.where(gz < NGZ - 1, one, zero)

    brick = (CX, CY, CZ)
    jj, kk = iota(brick, 1), iota(brick, 2)
    n_hot = (iota((16, 8, CZ), 0) == iota((16, 8, CZ), 2)).astype(F32)
    n_more = (iota((2, 8, CZ), 0) + 16 == iota((2, 8, CZ), 2)).astype(F32)
    row_hot = (iota((CY, CZ), 0) == iota((CY, CZ), 1)).astype(F32)

    def y_next(f):
        return pltpu.roll(f, CY - 1, 1)

    def z_next(f):
        return pltpu.roll(f, CZ - 1, 2)

    def packed(columns):
        return jnp.sum(columns.reshape(16, 8, -1) * n_hot, axis=0)

    def unpacked(tile):
        return jnp.sum(tile[None] * n_hot, axis=2, keepdims=True).reshape(2, CX, CY, 1)

    def message(step, which):
        src, dst = {
            XE: (sx.at[step, 0], rx.at[step, 0]),
            XQ: (sx.at[step, 1], rx.at[step, 1]),
            YE: (sy.at[step, pl.ds(0, 2)], ry.at[step, pl.ds(0, 2)]),
            YQ: (sy.at[step, pl.ds(2, 2)], ry.at[step, pl.ds(2, 2)]),
            ZE: (sz.at[step, 0], rz.at[step, 0]),
            ZQ: (sz.at[step, 1], rz.at[step, 1]),
            E_XZ: (sr.at[step, 0], rr.at[step, 0]),
            E_XY: (sr.at[step, 1], rr.at[step, 1]),
            E_YX: (sr.at[step, 2], rr.at[step, 2]),
            E_ZX: (sr.at[step, 3], rr.at[step, 3]),
            E_YZ: (sy.at[step, 4], ry.at[step, 4]),
            E_ZY: (sy.at[step, 5], ry.at[step, 5]),
        }[which]
        return pltpu.make_async_remote_copy(
            src_ref=src,
            dst_ref=dst,
            send_sem=hs_sem.at[step, which],
            recv_sem=hr_sem.at[step, which],
            device_id=at(*ROUTES[which]),
            device_id_type=MESH,
        )

    def start(step, *which):
        for n in which:
            when(ROUTES[n], 1, lambda n=n: message(step, n).start())

    def as_row(column):
        return jnp.sum(column * row_hot, axis=0, keepdims=True)

    def as_column(row):
        return jnp.sum(row * row_hot, axis=1, keepdims=True)

    def send_edges(step, xz, zx):
        sr[step, 0] = as_row(xz)
        sr[step, 3] = as_row(zx)
        start(step, E_XZ, E_ZX)

    def edge_gain(n):
        return pltpu.make_async_remote_copy(
            src_ref=sg.at[n],
            dst_ref=rg.at[n],
            send_sem=gs_sem.at[n],
            recv_sem=gr_sem.at[n],
            device_id=at(*ROUTES[(E_XZ, E_ZX)[n]]),
            device_id_type=MESH,
        )

    def send_sums(step, ex, ey, ez, hy, hz):
        y_ex = jnp.where(jj[0] == CY - 1, zero, pltpu.roll(ex, CY - 1, 0))
        z_ex = jnp.where(kk[0] == CZ - 1, zero, pltpu.roll(ex, CZ - 1, 1))
        sx[step, 1, 0] = hy - DT * ((z_ex - ex) + ez)
        sx[step, 1, 1] = hz + DT * (ey + (y_ex - ex))
        start(step, XQ)
        sr[step, 1] = ex[0:1, :]
        start(step, E_XY)

    def send_x():
        last = CX - 1
        ey, ez = e_ref[1, 0], e_ref[2, 0]
        send_edges(0, e_ref[0, last, :, 0:1], ez[:, CZ - 1 : CZ])
        sx[0, 0, 0] = ey
        sx[0, 0, 1] = ez
        start(0, XE)
        send_sums(0, e_ref[0, last], e_ref[1, last], e_ref[2, last], h_ref[1, last], h_ref[2, last])
        sr[0, 2] = ey[CY - 1 : CY, :]
        start(0, E_YX)

    def send_yz(step):
        ex, ey, ez = e_ref[0], e_ref[1], e_ref[2]
        nothing = jnp.zeros((1, CY, CZ), F32)
        last_y, last_z = jj == CY - 1, kk == CZ - 1
        y_ez = jnp.where(last_y, zero, y_next(ez))
        y_ex = jnp.where(last_y, zero, y_next(ex))
        z_ey = jnp.where(last_z, zero, z_next(ey))
        z_ex = jnp.where(last_z, zero, z_next(ex))
        x_ez = jnp.concatenate([ez[1:], nothing], 0)
        x_ey = jnp.concatenate([ey[1:], nothing], 0)
        hx = h_ref[0] - DT * ((y_ez - ez) - (z_ey - ey))
        hy = h_ref[1] - DT * ((z_ex - ex) - (x_ez - ez))
        hz = h_ref[2] - DT * ((x_ey - ey) - (y_ex - ex))
        part[0], part[1], part[2] = hx, hy, hz
        sz[step, 0] = packed(e_ref[0:2][:, :, :, 0:1]) + jnp.sum(ez[0].reshape(2, 8, CZ)[:, :, 0:1] * n_more, axis=0)
        sz[step, 1] = packed(part[0:2][:, :, :, CZ - 1 : CZ])
        start(step, ZE, ZQ)
        sy[step, 0] = ex[:, 0:1, :]
        sy[step, 1] = ez[:, 0:1, :]
        sy[step, 2] = hx[:, CY - 1 : CY, :]
        sy[step, 3] = hz[:, CY - 1 : CY, :]
        sy[step, 4] = ey[:, CY - 1 : CY, :]
        sy[step, 5] = ez[:, 0:1, :]
        start(step, YE, YQ, E_YZ, E_ZY)

    def wait(step, *which):
        for n in which:
            when(ROUTES[n], -1, lambda n=n: message(step, n).wait_recv())

    def current(step):
        j_ref[...] = coef[2][None] * j_ref[...] + coef[3][None] * e_ref[...]

    def update(step):
        last = CX - 1
        wait(step, ZE, ZQ, YE, YQ, E_YZ, E_ZY)
        ex, ey, ez = e_ref[0], e_ref[1], e_ref[2]
        hx, hy, hz = part[0], part[1], part[2]
        above_y = ry[step, 0:2]
        above_z = unpacked(rz[step, 0]) * top_z
        last_y, last_z = jj == CY - 1, kk == CZ - 1
        hx = hx + jnp.where(last_z, DT * above_z[1], zero) - jnp.where(last_y, DT * above_y[1], zero)
        hy = hy - jnp.where(last_z, DT * above_z[0], zero)
        hz = hz + jnp.where(last_y, DT * above_y[0], zero)
        e_yz = ry[step, 4] * top_z
        e_zy = ry[step, 5]
        ky, jz = iota((CX, 1, CZ), 2), iota((CX, CY, 1), 1)
        below_yx = ry[step, 2] - DT * ez[:, 0:1, :] + jnp.where(ky == CZ - 1, DT * e_yz[:, :, 0:1], zero)
        below_yz = ry[step, 3] + DT * ex[:, 0:1, :]
        below_z = unpacked(rz[step, 1])
        below_zx = below_z[0] + DT * ey[:, :, 0:1] - jnp.where(jz == CY - 1, DT * e_zy[:, :, CZ - 1 : CZ], zero)
        below_zy = below_z[1] - DT * ex[:, :, 0:1]
        first_y, first_z = jj == 0, kk == 0
        y_hx = jnp.where(first_y, low_y * below_yx, pltpu.roll(hx, 1, 1))
        y_hz = jnp.where(first_y, low_y * below_yz, pltpu.roll(hz, 1, 1))
        z_hx = jnp.where(first_z, low_z * below_zx, pltpu.roll(hx, 1, 2))
        z_hy = jnp.where(first_z, low_z * below_zy, pltpu.roll(hy, 1, 2))
        nothing = jnp.zeros((1, CY, CZ), F32)
        x_hy = jnp.concatenate([nothing, hy[:last]], 0)
        x_hz = jnp.concatenate([nothing, hz[:last]], 0)
        keep, gain = coef[0], coef[1]
        part[0] = keep * ex + gain * (((hz - y_hz) - (hy - z_hy)) - j_ref[0])
        part[1] = keep * ey + gain * (((hx - z_hx) - (hz - x_hz)) - j_ref[1])
        part[2] = keep * ez + gain * (((hy - x_hy) - (hx - y_hx)) - j_ref[2])
        h_ref[0], h_ref[1], h_ref[2] = hx, hy, hz
        jr, kr = jj[0], kk[0]
        if step < STEPS - 1:
            send_edges(step + 1, part[0, last, :, 0:1], part[2, 0, :, CZ - 1 : CZ])

        def edges():
            wait(step, E_XZ, E_ZX)
            e_xz, e_zx = as_column(rr[step, 0]), as_column(rr[step, 3])
            if step == 1:
                for n in range(2):
                    when(ROUTES[(E_XZ, E_ZX)[n]], -1, edge_gain(n).wait_recv)
            if step:
                e_xz = e_xz + as_column(rg[0]) * rest[0]
                e_zx = e_zx - as_column(rg[1]) * rest[1]
            e_xz, e_zx = e_xz * (DT * top_z), e_zx * (DT * top_x)
            if step < STEPS - 1:
                more_z = jnp.broadcast_to(-DT * above_z[1, 0], (CY, CZ))
                y_more_z = jnp.where(jr == 0, -DT * e_yz[0, :, 0:1], pltpu.roll(more_z, 1, 0))
                more_y = DT * jnp.sum(rz[step, 0][None] * n_more, axis=2, keepdims=True).reshape(CY, 1)
                rest[0] = (more_z - y_more_z) - (more_y - DT * ez[0, :, CZ - 1 : CZ])
                rest[1] = jnp.broadcast_to(below_zy[last] + e_zx, (CY, CZ))
            at_xz = jnp.where(kr == CZ - 1, low_x * coef[1, 0] * e_xz, zero)
            at_zx = jnp.where(kr == 0, low_z * coef[1, last] * e_zx, zero)
            return at_xz, at_zx

        if step:
            at_xz, at_zx = edges()
            part[2, 0] = part[2, 0] + at_xz
            part[0, last] = part[0, last] + at_zx

        later = step < STEPS - 1
        gain_0, gain = low_x * coef[1, 0], coef[1, last]
        if step == 0:
            at_xz, at_zx = edges()
            part[2, 0] = part[2, 0] + at_xz
            part[0, last] = part[0, last] + at_zx

        def first_plane():
            wait(step, E_XY, XQ)
            below_xy = rx[step, 1, 0] + DT * ez[0]
            below_xz = rx[step, 1, 1] - DT * ey[0] + jnp.where(jr == CY - 1, DT * rr[step, 1], zero)
            y_first = part[1, 0] + gain_0 * below_xz
            z_first = part[2, 0] - gain_0 * below_xy
            if later:
                sx[step + 1, 0, 0] = y_first
                sx[step + 1, 0, 1] = z_first
                start(step + 1, XE)
                sr[step + 1, 2] = y_first[CY - 1 : CY, :]
                start(step + 1, E_YX)
            e_ref[1, 0], e_ref[2, 0] = y_first, z_first

        def last_plane():
            wait(step, E_YX, XE)
            more_y = (DT * top_x) * rx[step, 0, 1]
            more_z = (-DT * top_x) * rx[step, 0, 0]
            e_yx = rr[step, 2] * top_x
            y_more_z = jnp.where(jr == 0, (-DT * low_y) * e_yx, pltpu.roll(more_z, 1, 0))
            z_more_y = jnp.where(kr == 0, zero, pltpu.roll(more_y, 1, 1))
            x_last = part[0, last] + gain * ((more_z - y_more_z) - (more_y - z_more_y))
            y_last = part[1, last] - gain * more_z
            z_last = part[2, last] + gain * more_y
            hy_last = h_ref[1, last] + more_y
            hz_last = h_ref[2, last] + more_z
            if later:
                send_sums(step + 1, x_last, y_last, z_last, hy_last, hz_last)
            h_ref[1, last], h_ref[2, last] = hy_last, hz_last
            e_ref[0, last], e_ref[1, last], e_ref[2, last] = x_last, y_last, z_last

        for plane in (first_plane, last_plane):
            plane()
        e_ref[0, 0:last] = part[0, 0:last]
        e_ref[1, 1:last] = part[1, 1:last]
        e_ref[2, 1:last] = part[2, 1:last]

    def stress(step):
        ex, ey, ez = e_ref[0], e_ref[1], e_ref[2]
        hx, hy, hz = h_ref[0], h_ref[1], h_ref[2]
        g = g_ref[step]
        xx, yy, zz = ex * ex + hx * hx, ey * ey + hy * hy, ez * ez + hz * hz
        energy = 0.5 * (xx + yy + zz)
        found = (xx - energy, ex * ey + hx * hy, ex * ez + hx * hz, yy - energy, ey * ez + hy * hz, zz - energy)
        for n, value in enumerate(found):
            tensor[n] = g * value if step == 0 else tensor[n] + g * value

    def ranks_and_buckets():
        owner = owner_ref[...]
        block = SLOTS // 4
        groups = NGX * NGY
        earlier = (iota((block, block), 0) < iota((block, block), 1)).astype(F32).astype(BF16)
        lane = iota((1, block), 1)
        before = jnp.zeros((groups, 1), F32)
        made = jnp.zeros((5 * NNEAR, LANES), F32)
        for b in range(4):
            cut = slice(b * block, (b + 1) * block)
            own = owner[:, cut]
            hot = (own == iota((groups, block), 0)).astype(F32)
            ahead = dot(hot.astype(BF16), earlier, (1, 0)) + before
            rank = jnp.sum(ahead * hot, axis=0, keepdims=True).astype(jnp.int32)
            before = before + jnp.sum(hot, axis=1, keepdims=True)
            place = rank * NFAR + (lax.shift_right_logical(own, 1) & (NFAR - 1))
            place_hot = (place == iota((LANES, block), 0)).astype(F32).astype(BF16)
            cell, normal = cell_ref[:, cut], normal_ref[:, cut]
            live = (lane + b * block < count_ref[0, 0, 0]).astype(F32)
            weight = live * (FACE_AREA * (1 - 2 * (normal & 1)).astype(F32))
            mine = lax.shift_right_logical(own, 5) * CORES + (own & 1) == iota((NNEAR, block), 0)
            entries = (
                (cell & 127).astype(F32),
                lax.shift_right_logical(cell, 7).astype(F32),
                weight,
                lax.shift_right_logical(normal, 1).astype(F32),
                tile_ref[:, cut].astype(F32),
            )
            rows = jnp.concatenate([jnp.where(mine, entry, zero) for entry in entries], 0)
            made = made + dot(rows.astype(BF16), place_hot, (1, 1))
        for n in range(5):
            bucket[n] = made[n * NNEAR : (n + 1) * NNEAR].reshape(NNEAR, 1, LANES)
        stl[...] = bucket[4]

    def toward(k):
        return lax.rem(y_chip + k // CORES, NY_CHIPS) * CORES + lax.rem(core + k % CORES, CORES)

    def origin(k):
        return lax.rem(y_chip + NY_CHIPS - k // CORES, NY_CHIPS) * CORES + lax.rem(core + k % CORES, CORES)

    def to_near(src, dst, send, recv, k):
        return pltpu.make_async_remote_copy(
            src_ref=src,
            dst_ref=dst.at[near],
            send_sem=send.at[k],
            recv_sem=recv.at[k],
            device_id=near_at(toward(k)),
            device_id_type=MESH,
        )

    def from_near(dst, send, recv, k):
        n = origin(k)
        return pltpu.make_async_remote_copy(
            src_ref=dst.at[n],
            dst_ref=dst.at[n],
            send_sem=send.at[k],
            recv_sem=recv.at[k],
            device_id=near_at(n),
            device_id_type=MESH,
        )

    def tiles_to(k):
        return to_near(stl.at[toward(k)], rtl, ts_sem, tr_sem, k)

    def values_to(k):
        return to_near(sval.at[k], rval, vs_sem, vr_sem, k)

    def lane_hots():
        for n in range(NNEAR):
            lane_hot[n] = (bucket[0, n] == iota((CZ, LANES), 0).astype(F32)).astype(F32).astype(BF16)

    def tile_hots():
        for d in range(1, NNEAR):
            from_near(rtl, ts_sem, tr_sem, d).wait_recv()
        for n in range(NNEAR):
            tile_hot[n] = (rtl[n] == iota((TILE_DEV, LANES), 0).astype(F32)).astype(F32).astype(BF16)

    def coefficients():
        material = mat_ref[...]

        def of_material(table):
            result = jnp.where(material == 0, table[0], zero)
            for which in (1, 2):
                result = jnp.where(material == which, table[which], result)
            return result

        sigma, gamma, plasma = of_material(sig_ref), of_material(gam_ref), of_material(pla_ref)
        coef[0] = (1.0 - sigma * DT / 2) / (1.0 + sigma * DT / 2)
        coef[1] = DT / (1.0 + sigma * DT / 2)
        coef[2] = (1.0 - gamma * DT / 2) / (1.0 + gamma * DT / 2)
        coef[3] = plasma * DT / (1.0 + gamma * DT / 2)

    loads[0].wait()
    loads[1].wait()
    pl.semaphore_wait(barrier, greeted)

    for step in range(STEPS):
        if step == 0:
            send_x()
        send_yz(step)
        if step == 0:
            for load in loads[2:]:
                load.wait()
            coefficients()
            sg[0] = as_row(coef[1, CX - 1, :, 0:1])
            sg[1] = as_row(coef[1, 0, :, CZ - 1 : CZ])
            for n in range(2):
                when(ROUTES[(E_XZ, E_ZX)[n]], 1, edge_gain(n).start)
            current(step)
            ranks_and_buckets()
            for d in range(1, NNEAR):
                tiles_to(d).start()
            rtl[near] = stl[near]
        else:
            current(step)
            stress(step - 1)
        if step == 1:
            lane_hots()
        if step == 2:
            tile_hots()
        update(step)
    stores = [
        pltpu.make_async_copy(src, dst, out_sem.at[n]) for n, (src, dst) in enumerate(((e_ref, e_out), (h_ref, h_out)))
    ]
    for store in stores:
        store.start()
    stress(STEPS - 1)

    cells = CX * CY
    high, low = halves(tensor[...].reshape(6 * cells, CZ))
    parts = jnp.concatenate([high, low], 1)
    for k in (4, 5, 2, 3, 6, 7, 1, 0):
        n = toward(k)
        hot = lane_hot[n]
        read = dot(parts, jnp.concatenate([hot, hot], 0), (1, 0))
        row = bucket[1, n] == iota((cells, LANES), 0).astype(F32)
        xx, xy, xz, yy, yz, zz = [
            jnp.sum(jnp.where(row, read[c * cells : (c + 1) * cells], zero), axis=0, keepdims=True) for c in range(6)
        ]
        axis, weight = bucket[3, n], bucket[2, n]
        along_x, along_y = axis == 0.0, axis == 1.0
        sval[k, 0:1] = weight * jnp.where(along_x, xx, jnp.where(along_y, xy, xz))
        sval[k, 1:2] = weight * jnp.where(along_x, xy, jnp.where(along_y, yy, yz))
        sval[k, 2:3] = weight * jnp.where(along_x, xz, jnp.where(along_y, yz, zz))
        if k:
            values_to(k).start()
    rval[near] = sval[0]

    rows = (NFAR * 8, LANES)
    mine = (lax.shift_right_logical(iota(rows, 0), 3) == (iota(rows, 1) & (NFAR - 1))).astype(F32)
    dense = jnp.zeros((NFAR * 8, TILE_DEV), F32)
    for k in (0, 1, 2, 3, 6, 7, 4, 5):
        n = origin(k)
        if k:
            from_near(rval, vs_sem, vr_sem, k).wait_recv()
        value = rval[n]
        high = value.astype(BF16).astype(F32)
        both = jnp.concatenate([high, value - high, jnp.zeros((2, LANES), F32)], 0)
        spread = (jnp.concatenate([both] * NFAR, 0) * mine).astype(BF16)
        dense = dense + dot(spread, tile_hot[n], (1, 1))
    dense = dense.reshape(NFAR, 8, TILE_DEV)
    sdense[...] = dense[:, 0:3] + dense[:, 3:6]

    def to_far(d):
        n = lax.rem(far + d, NFAR)
        return pltpu.make_async_remote_copy(
            src_ref=sdense.at[n],
            dst_ref=rdense.at[far],
            send_sem=ds_sem.at[d],
            recv_sem=dr_sem.at[d],
            device_id=far_at(n),
            device_id_type=MESH,
        )

    def from_far(d):
        n = lax.rem(far + NFAR - d, NFAR)
        return pltpu.make_async_remote_copy(
            src_ref=sdense.at[n],
            dst_ref=rdense.at[n],
            send_sem=ds_sem.at[d],
            recv_sem=dr_sem.at[d],
            device_id=far_at(n),
            device_id_type=MESH,
        )

    for d in (8, 7, 9, 6, 10, 5, 11, 4, 12, 3, 13, 2, 14, 1, 15):
        to_far(d).start()
    rdense[far] = sdense[far]
    for step in range(STEPS):
        for which in range(12):
            when(ROUTES[which], 1, lambda which=which: message(step, which).wait_send())
    for n in range(2):
        when(ROUTES[(E_XZ, E_ZX)[n]], 1, edge_gain(n).wait_send)
    for d in range(1, NNEAR):
        tiles_to(d).wait_send()
        values_to(d).wait_send()
    for d in range(1, NFAR):
        to_far(d).wait_send()
    for store in stores:
        store.wait()
    for d in range(1, NFAR):
        from_far(d).wait_recv()
    force_ref[...] = jnp.sum(rdense[...], axis=0)


def hand_out(*refs):
    sem = refs[-1]
    copies = [pltpu.make_async_copy(refs[n], refs[n + 3], sem.at[n]) for n in range(3)]
    for copy in copies:
        copy.start()
    for copy in copies:
        copy.wait()


def local(
    e_field,
    h_field,
    current,
    material,
    sigma_table,
    gamma_table,
    plasma_table,
    g_kernel,
    surf_cell,
    surf_owner,
    surf_tile,
    surf_normal,
    row_count,
):
    field = jax.ShapeDtypeStruct((3, CX, CY, CZ), F32)
    hbm = pl.BlockSpec(memory_space=pltpu.HBM)
    dma = pltpu.SemaphoreType.DMA
    slots = [a.reshape(1, SLOTS) for a in (surf_cell, surf_owner, surf_tile, surf_normal)]
    operands = (e_field, h_field, current, material, *slots)
    operands += (sigma_table, gamma_table, plasma_table, g_kernel)
    operands = [pltpu.with_memory_space_constraint(a, pltpu.HBM) for a in operands]
    shapes = (field, field, jax.ShapeDtypeStruct((3, TILE_DEV), F32))
    made = pl.pallas_call(
        kernel,
        out_shape=shapes,
        in_specs=[hbm] * 12 + [pl.BlockSpec(memory_space=pltpu.SMEM)],
        out_specs=(hbm, hbm, pl.BlockSpec(memory_space=pltpu.VMEM)),
        scratch_shapes=[
            pltpu.VMEM((3, CX, CY, CZ), F32),
            pltpu.VMEM((3, CX, CY, CZ), F32),
            pltpu.VMEM((3, CX, CY, CZ), F32),
            pltpu.VMEM((3, CX, CY, CZ), F32),
            pltpu.VMEM((CX, CY, CZ), jnp.int32),
            pltpu.VMEM((1, SLOTS), jnp.int32),
            pltpu.VMEM((1, SLOTS), jnp.int32),
            pltpu.VMEM((1, SLOTS), jnp.int32),
            pltpu.VMEM((1, SLOTS), jnp.int32),
            pltpu.SMEM((3,), F32),
            pltpu.SMEM((3,), F32),
            pltpu.SMEM((3,), F32),
            pltpu.SMEM((STEPS,), F32),
            pltpu.VMEM((4, CX, CY, CZ), F32),
            pltpu.VMEM((6, CX, CY, CZ), F32),
            pltpu.VMEM((STEPS, 2, 2, CY, CZ), F32),
            pltpu.VMEM((STEPS, 2, 2, CY, CZ), F32),
            pltpu.VMEM((STEPS, 6, CX, 1, CZ), F32),
            pltpu.VMEM((STEPS, 6, CX, 1, CZ), F32),
            pltpu.VMEM((STEPS, 2, 8, CZ), F32),
            pltpu.VMEM((STEPS, 2, 8, CZ), F32),
            pltpu.VMEM((STEPS, 4, 1, CZ), F32),
            pltpu.VMEM((STEPS, 4, 1, CZ), F32),
            pltpu.VMEM((2, 1, CZ), F32),
            pltpu.VMEM((2, 1, CZ), F32),
            pltpu.VMEM((2, CY, CZ), F32),
            pltpu.VMEM((5, NNEAR, 1, LANES), F32),
            pltpu.VMEM((NNEAR, CZ, LANES), BF16),
            pltpu.VMEM((NNEAR, TILE_DEV, LANES), BF16),
            pltpu.VMEM((NNEAR, 1, LANES), F32),
            pltpu.VMEM((NNEAR, 1, LANES), F32),
            pltpu.VMEM((NNEAR, 3, LANES), F32),
            pltpu.VMEM((NNEAR, 3, LANES), F32),
            pltpu.VMEM((NFAR, 3, TILE_DEV), F32),
            pltpu.VMEM((NFAR, 3, TILE_DEV), F32),
            dma((12,)),
            dma((2,)),
            dma((STEPS, 12)),
            dma((STEPS, 12)),
            dma((NNEAR,)),
            dma((NNEAR,)),
            dma((NNEAR,)),
            dma((NNEAR,)),
            dma((NFAR,)),
            dma((NFAR,)),
            dma((2,)),
            dma((2,)),
        ],
        compiler_params=pltpu.CompilerParams(
            collective_id=0, has_side_effects=True, vmem_limit_bytes=24 * 2**20
        ),
    )(*operands, row_count)
    return pl.pallas_call(
        hand_out,
        out_shape=shapes,
        in_specs=[hbm] * 3,
        out_specs=(hbm,) * 3,
        scratch_shapes=[dma((3,))],
        compiler_params=pltpu.CompilerParams(vmem_limit_bytes=24 * 2**20),
    )(*made)


def solution(mesh):
    cells = P("gx", "gy", "gz")
    field = P(None, "gx", "gy", "gz")
    slots = P("gx", "gy", "gz", None)
    return jax.shard_map(
        local,
        mesh=mesh,
        in_specs=(
            field,
            field,
            field,
            cells,
            P(),
            P(),
            P(),
            P(),
            slots,
            P("gx", "gy", "gz", None, None),
            slots,
            slots,
            cells,
        ),
        out_specs=(field, field, P(None, ("gx", "gy", "gz"))),
        check_vma=False,
    )
```

```python
import functools

import jax
import jax.numpy as jnp
from jax import lax
from jax.experimental import pallas as pl
from jax.experimental.pallas import tpu as pltpu
from jax.sharding import PartitionSpec as P

MESH = pl.DeviceIdType.MESH
F32 = jnp.float32
BF16 = jnp.bfloat16

DT = 0.5
FACE_AREA = 0.25
STEPS = 4
CX, CY, CZ = 4, 16, 128
SLOTS = 1024
TILE_DEV = 128
NGX, NGY, NGZ = 16, 8, 4
NY_CHIPS, NZ_HI, NZ_LO, CORES = 4, 4, 4, 2
NNEAR, NFAR = NY_CHIPS * CORES, NZ_HI * NZ_LO
LANES = 16 * NFAR

(XE, XQ, YE, YQ, ZE, ZQ, E_XZ, E_XY, E_YZ, E_YX, E_ZY, E_ZX) = range(12)
ROUTES = (
    (-1, 0, 0),
    (1, 0, 0),
    (0, -1, 0),
    (0, 1, 0),
    (0, 0, -1),
    (0, 0, 1),
    (1, 0, -1),
    (1, -1, 0),
    (0, 1, -1),
    (-1, 1, 0),
    (0, -1, 1),
    (-1, 0, 1),
)


def iota(shape, axis):
    return lax.broadcasted_iota(jnp.int32, shape, axis)


def dot(a, b, contract):
    return lax.dot_general(a, b, ((contract[:1], contract[1:]), ((), ())), preferred_element_type=F32)


def halves(x):
    high = x.astype(BF16)
    return high, (x - high.astype(F32)).astype(BF16)


def kernel(
    e_in,
    h_in,
    j_in,
    mat_in,
    cell_in,
    owner_in,
    tile_in,
    normal_in,
    sig_in,
    gam_in,
    pla_in,
    g_in,
    count_ref,
    e_out,
    h_out,
    force_ref,
    e_ref,
    h_ref,
    j_ref,
    part,
    mat_ref,
    cell_ref,
    owner_ref,
    tile_ref,
    normal_ref,
    sig_ref,
    gam_ref,
    pla_ref,
    g_ref,
    coef,
    tensor,
    sx,
    rx,
    sy,
    ry,
    sz,
    rz,
    sr,
    rr,
    sg,
    rg,
    rest,
    bucket,
    lane_hot,
    tile_hot,
    stl,
    rtl,
    sval,
    rval,
    sdense,
    rdense,
    in_sem,
    out_sem,
    hs_sem,
    hr_sem,
    ts_sem,
    tr_sem,
    vs_sem,
    vr_sem,
    ds_sem,
    dr_sem,
    gs_sem,
    gr_sem,
):
    gx, gy, gz = lax.axis_index("gx"), lax.axis_index("gy"), lax.axis_index("gz")

    loads = [
        pltpu.make_async_copy(src, dst, in_sem.at[n])
        for n, (src, dst) in enumerate(
            (
                (e_in, e_ref),
                (h_in, h_ref),
                (j_in, j_ref),
                (mat_in, mat_ref),
                (sig_in, sig_ref),
                (gam_in, gam_ref),
                (pla_in, pla_ref),
                (g_in, g_ref),
                (cell_in, cell_ref),
                (owner_in, owner_ref),
                (tile_in, tile_ref),
                (normal_in, normal_ref),
            )
        )
    ]
    for load in loads[:2]:
        load.start()

    def at(dx, dy, dz):
        where = {}
        if dx:
            where["gx"] = gx + dx
        if dy:
            where["gy"] = gy + dy
        if dz:
            where["gz"] = gz + dz
        return where

    y_chip, z_hi = lax.div(gx, NZ_HI), lax.rem(gx, NZ_HI)
    z_lo, core = lax.div(gy, CORES), lax.rem(gy, CORES)
    near, far = y_chip * CORES + core, z_hi * NZ_LO + z_lo

    def near_at(n):
        return {"gx": lax.div(n, CORES) * NZ_HI + z_hi, "gy": z_lo * CORES + lax.rem(n, CORES)}

    def far_at(n):
        return {"gx": y_chip * NZ_HI + lax.div(n, NZ_LO), "gy": lax.rem(n, NZ_LO) * CORES + core}

    def inside(route, sign):
        has = [gx < NGX - 1 if sign * route[0] > 0 else gx > 0] if route[0] else []
        has += [gy < NGY - 1 if sign * route[1] > 0 else gy > 0] if route[1] else []
        has += [gz < NGZ - 1 if sign * route[2] > 0 else gz > 0] if route[2] else []
        return has

    def when(route, sign, do):
        has = inside(route, sign)
        if has:
            pl.when(functools.reduce(jnp.logical_and, has))(do)
        else:
            do()

    barrier = pltpu.get_barrier_semaphore()

    def greet(where):
        pl.semaphore_signal(barrier, inc=1, device_id=where, device_id_type=MESH)

    for d in range(1, NZ_LO):
        greet({"gy": lax.rem(z_lo + d, NZ_LO) * CORES + core})
    for route in sorted(ROUTES, key=lambda r: -abs(r[0])):
        when(route, 1, functools.partial(lambda r: greet(at(*r)), route))
    for d in range(1, NNEAR):
        greet(near_at(lax.rem(near + d, NNEAR)))
    for load in loads[2:]:
        load.start()
    greeted = NNEAR - 1 + NZ_LO - 1
    for route in ROUTES:
        found = 1
        for has in inside(route, 1):
            found = found * jnp.where(has, 1, 0)
        greeted = greeted + found

    @pl.when(gz == NGZ - 1)
    def _():
        for step in range(STEPS):
            rz[step, 0] = jnp.zeros((8, CZ), F32)
            ry[step, 4] = jnp.zeros((CX, 1, CZ), F32)
            rr[step, 0] = jnp.zeros((1, CZ), F32)
        rg[0] = jnp.zeros((1, CZ), F32)

    @pl.when(gz == 0)
    def _():
        for step in range(STEPS):
            rz[step, 1] = jnp.zeros((8, CZ), F32)
            ry[step, 5] = jnp.zeros((CX, 1, CZ), F32)
            rr[step, 3] = jnp.zeros((1, CZ), F32)
        rg[1] = jnp.zeros((1, CZ), F32)

    @pl.when(gx == NGX - 1)
    def _():
        for step in range(STEPS):
            rx[step, 0] = jnp.zeros((2, CY, CZ), F32)
            rr[step, 2] = jnp.zeros((1, CZ), F32)
            rr[step, 3] = jnp.zeros((1, CZ), F32)
        rg[1] = jnp.zeros((1, CZ), F32)

    @pl.when(gx == 0)
    def _():
        for step in range(STEPS):
            rx[step, 1] = jnp.zeros((2, CY, CZ), F32)
            rr[step, 0] = jnp.zeros((1, CZ), F32)
            rr[step, 1] = jnp.zeros((1, CZ), F32)
        rg[0] = jnp.zeros((1, CZ), F32)

    @pl.when(gy == NGY - 1)
    def _():
        for step in range(STEPS):
            ry[step, 0:2] = jnp.zeros((2, CX, 1, CZ), F32)
            ry[step, 5] = jnp.zeros((CX, 1, CZ), F32)
            rr[step, 1] = jnp.zeros((1, CZ), F32)

    @pl.when(gy == 0)
    def _():
        for step in range(STEPS):
            ry[step, 2:5] = jnp.zeros((3, CX, 1, CZ), F32)
            rr[step, 2] = jnp.zeros((1, CZ), F32)

    one, zero = jnp.float32(1.0), jnp.float32(0.0)
    low_x = jnp.where(gx > 0, one, zero)
    low_y = jnp.where(gy > 0, one, zero)
    low_z = jnp.where(gz > 0, one, zero)
    top_x = jnp.where(gx < NGX - 1, one, zero)
    top_y = jnp.where(gy < NGY - 1, one, zero)
    top_z = jnp.where(gz < NGZ - 1, one, zero)

    brick = (CX, CY, CZ)
    jj, kk = iota(brick, 1), iota(brick, 2)
    n_hot = (iota((16, 8, CZ), 0) == iota((16, 8, CZ), 2)).astype(F32)
    n_more = (iota((2, 8, CZ), 0) + 16 == iota((2, 8, CZ), 2)).astype(F32)
    row_hot = (iota((CY, CZ), 0) == iota((CY, CZ), 1)).astype(F32)

    def y_next(f):
        return pltpu.roll(f, CY - 1, 1)

    def z_next(f):
        return pltpu.roll(f, CZ - 1, 2)

    def packed(columns):
        return jnp.sum(columns.reshape(16, 8, -1) * n_hot, axis=0)

    def unpacked(tile):
        return jnp.sum(tile[None] * n_hot, axis=2, keepdims=True).reshape(2, CX, CY, 1)

    def message(step, which):
        src, dst = {
            XE: (sx.at[step, 0], rx.at[step, 0]),
            XQ: (sx.at[step, 1], rx.at[step, 1]),
            YE: (sy.at[step, pl.ds(0, 2)], ry.at[step, pl.ds(0, 2)]),
            YQ: (sy.at[step, pl.ds(2, 2)], ry.at[step, pl.ds(2, 2)]),
            ZE: (sz.at[step, 0], rz.at[step, 0]),
            ZQ: (sz.at[step, 1], rz.at[step, 1]),
            E_XZ: (sr.at[step, 0], rr.at[step, 0]),
            E_XY: (sr.at[step, 1], rr.at[step, 1]),
            E_YX: (sr.at[step, 2], rr.at[step, 2]),
            E_ZX: (sr.at[step, 3], rr.at[step, 3]),
            E_YZ: (sy.at[step, 4], ry.at[step, 4]),
            E_ZY: (sy.at[step, 5], ry.at[step, 5]),
        }[which]
        return pltpu.make_async_remote_copy(
            src_ref=src,
            dst_ref=dst,
            send_sem=hs_sem.at[step, which],
            recv_sem=hr_sem.at[step, which],
            device_id=at(*ROUTES[which]),
            device_id_type=MESH,
        )

    entered, held = [], []

    def start(step, *which):
        if not entered:
            held.append((step, *which))
            return
        for n in which:
            when(ROUTES[n], 1, lambda n=n: message(step, n).start())

    def as_row(column):
        return jnp.sum(column * row_hot, axis=0, keepdims=True)

    def as_column(row):
        return jnp.sum(row * row_hot, axis=1, keepdims=True)

    def send_edges(step, xz, zx):
        sr[step, 0] = as_row(xz)
        sr[step, 3] = as_row(zx)
        start(step, E_XZ, E_ZX)

    def edge_gain(n):
        return pltpu.make_async_remote_copy(
            src_ref=sg.at[n],
            dst_ref=rg.at[n],
            send_sem=gs_sem.at[n],
            recv_sem=gr_sem.at[n],
            device_id=at(*ROUTES[(E_XZ, E_ZX)[n]]),
            device_id_type=MESH,
        )

    def send_sums(step, ex, ey, ez, hy, hz):
        y_ex = jnp.where(jj[0] == CY - 1, zero, pltpu.roll(ex, CY - 1, 0))
        z_ex = jnp.where(kk[0] == CZ - 1, zero, pltpu.roll(ex, CZ - 1, 1))
        sx[step, 1, 0] = hy - DT * ((z_ex - ex) + ez)
        sx[step, 1, 1] = hz + DT * (ey + (y_ex - ex))
        start(step, XQ)
        sr[step, 1] = ex[0:1, :]
        start(step, E_XY)

    def send_x():
        last = CX - 1
        ey, ez = e_ref[1, 0], e_ref[2, 0]
        send_edges(0, e_ref[0, last, :, 0:1], ez[:, CZ - 1 : CZ])
        sx[0, 0, 0] = ey
        sx[0, 0, 1] = ez
        start(0, XE)
        send_sums(0, e_ref[0, last], e_ref[1, last], e_ref[2, last], h_ref[1, last], h_ref[2, last])
        sr[0, 2] = ey[CY - 1 : CY, :]
        start(0, E_YX)

    def send_yz(step):
        ex, ey, ez = e_ref[0], e_ref[1], e_ref[2]
        nothing = jnp.zeros((1, CY, CZ), F32)
        last_y, last_z = jj == CY - 1, kk == CZ - 1
        y_ez = jnp.where(last_y, zero, y_next(ez))
        y_ex = jnp.where(last_y, zero, y_next(ex))
        z_ey = jnp.where(last_z, zero, z_next(ey))
        z_ex = jnp.where(last_z, zero, z_next(ex))
        x_ez = jnp.concatenate([ez[1:], nothing], 0)
        x_ey = jnp.concatenate([ey[1:], nothing], 0)
        hx = h_ref[0] - DT * ((y_ez - ez) - (z_ey - ey))
        hy = h_ref[1] - DT * ((z_ex - ex) - (x_ez - ez))
        hz = h_ref[2] - DT * ((x_ey - ey) - (y_ex - ex))
        part[0], part[1], part[2] = hx, hy, hz
        sz[step, 0] = packed(e_ref[0:2][:, :, :, 0:1]) + jnp.sum(ez[0].reshape(2, 8, CZ)[:, :, 0:1] * n_more, axis=0)
        sz[step, 1] = packed(part[0:2][:, :, :, CZ - 1 : CZ])
        start(step, ZE, ZQ)
        sy[step, 0] = ex[:, 0:1, :]
        sy[step, 1] = ez[:, 0:1, :]
        sy[step, 2] = hx[:, CY - 1 : CY, :]
        sy[step, 3] = hz[:, CY - 1 : CY, :]
        sy[step, 4] = ey[:, CY - 1 : CY, :]
        sy[step, 5] = ez[:, 0:1, :]
        start(step, YE, YQ, E_YZ, E_ZY)

    def wait(step, *which):
        for n in which:
            when(ROUTES[n], -1, lambda n=n: message(step, n).wait_recv())

    def current(step):
        j_ref[...] = coef[2][None] * j_ref[...] + coef[3][None] * e_ref[...]

    def update(step):
        last = CX - 1
        wait(step, ZE, ZQ, YE, YQ, E_YZ, E_ZY)
        ex, ey, ez = e_ref[0], e_ref[1], e_ref[2]
        hx, hy, hz = part[0], part[1], part[2]
        above_y = ry[step, 0:2]
        above_z = unpacked(rz[step, 0]) * top_z
        last_y, last_z = jj == CY - 1, kk == CZ - 1
        hx = hx + jnp.where(last_z, DT * above_z[1], zero) - jnp.where(last_y, DT * above_y[1], zero)
        hy = hy - jnp.where(last_z, DT * above_z[0], zero)
        hz = hz + jnp.where(last_y, DT * above_y[0], zero)
        e_yz = ry[step, 4] * top_z
        e_zy = ry[step, 5]
        ky, jz = iota((CX, 1, CZ), 2), iota((CX, CY, 1), 1)
        below_yx = ry[step, 2] - DT * ez[:, 0:1, :] + jnp.where(ky == CZ - 1, DT * e_yz[:, :, 0:1], zero)
        below_yz = ry[step, 3] + DT * ex[:, 0:1, :]
        below_z = unpacked(rz[step, 1])
        below_zx = below_z[0] + DT * ey[:, :, 0:1] - jnp.where(jz == CY - 1, DT * e_zy[:, :, CZ - 1 : CZ], zero)
        below_zy = below_z[1] - DT * ex[:, :, 0:1]
        first_y, first_z = jj == 0, kk == 0
        y_hx = jnp.where(first_y, low_y * below_yx, pltpu.roll(hx, 1, 1))
        y_hz = jnp.where(first_y, low_y * below_yz, pltpu.roll(hz, 1, 1))
        z_hx = jnp.where(first_z, low_z * below_zx, pltpu.roll(hx, 1, 2))
        z_hy = jnp.where(first_z, low_z * below_zy, pltpu.roll(hy, 1, 2))
        nothing = jnp.zeros((1, CY, CZ), F32)
        x_hy = jnp.concatenate([nothing, hy[:last]], 0)
        x_hz = jnp.concatenate([nothing, hz[:last]], 0)
        keep, gain = coef[0], coef[1]
        part[0] = keep * ex + gain * (((hz - y_hz) - (hy - z_hy)) - j_ref[0])
        part[1] = keep * ey + gain * (((hx - z_hx) - (hz - x_hz)) - j_ref[1])
        part[2] = keep * ez + gain * (((hy - x_hy) - (hx - y_hx)) - j_ref[2])
        h_ref[0], h_ref[1], h_ref[2] = hx, hy, hz
        jr, kr = jj[0], kk[0]
        if step < STEPS - 1:
            send_edges(step + 1, part[0, last, :, 0:1], part[2, 0, :, CZ - 1 : CZ])

        def edges():
            wait(step, E_XZ, E_ZX)
            e_xz, e_zx = as_column(rr[step, 0]), as_column(rr[step, 3])
            if step == 1:
                for n in range(2):
                    when(ROUTES[(E_XZ, E_ZX)[n]], -1, edge_gain(n).wait_recv)
            if step:
                e_xz = e_xz + as_column(rg[0]) * rest[0]
                e_zx = e_zx - as_column(rg[1]) * rest[1]
            e_xz, e_zx = e_xz * (DT * top_z), e_zx * (DT * top_x)
            if step < STEPS - 1:
                more_z = jnp.broadcast_to(-DT * above_z[1, 0], (CY, CZ))
                y_more_z = jnp.where(jr == 0, -DT * e_yz[0, :, 0:1], pltpu.roll(more_z, 1, 0))
                more_y = DT * jnp.sum(rz[step, 0][None] * n_more, axis=2, keepdims=True).reshape(CY, 1)
                rest[0] = (more_z - y_more_z) - (more_y - DT * ez[0, :, CZ - 1 : CZ])
                rest[1] = jnp.broadcast_to(below_zy[last] + e_zx, (CY, CZ))
            at_xz = jnp.where(kr == CZ - 1, low_x * coef[1, 0] * e_xz, zero)
            at_zx = jnp.where(kr == 0, low_z * coef[1, last] * e_zx, zero)
            return at_xz, at_zx

        if step:
            at_xz, at_zx = edges()
            part[2, 0] = part[2, 0] + at_xz
            part[0, last] = part[0, last] + at_zx

        later = step < STEPS - 1
        gain_0, gain = low_x * coef[1, 0], coef[1, last]
        if step == 0:
            at_xz, at_zx = edges()
            part[2, 0] = part[2, 0] + at_xz
            part[0, last] = part[0, last] + at_zx

        def first_plane():
            wait(step, E_XY, XQ)
            below_xy = rx[step, 1, 0] + DT * ez[0]
            below_xz = rx[step, 1, 1] - DT * ey[0] + jnp.where(jr == CY - 1, DT * rr[step, 1], zero)
            y_first = part[1, 0] + gain_0 * below_xz
            z_first = part[2, 0] - gain_0 * below_xy
            if later:
                sx[step + 1, 0, 0] = y_first
                sx[step + 1, 0, 1] = z_first
                start(step + 1, XE)
                sr[step + 1, 2] = y_first[CY - 1 : CY, :]
                start(step + 1, E_YX)
            e_ref[1, 0], e_ref[2, 0] = y_first, z_first

        def last_plane():
            wait(step, E_YX, XE)
            more_y = (DT * top_x) * rx[step, 0, 1]
            more_z = (-DT * top_x) * rx[step, 0, 0]
            e_yx = rr[step, 2] * top_x
            y_more_z = jnp.where(jr == 0, (-DT * low_y) * e_yx, pltpu.roll(more_z, 1, 0))
            z_more_y = jnp.where(kr == 0, zero, pltpu.roll(more_y, 1, 1))
            x_last = part[0, last] + gain * ((more_z - y_more_z) - (more_y - z_more_y))
            y_last = part[1, last] - gain * more_z
            z_last = part[2, last] + gain * more_y
            hy_last = h_ref[1, last] + more_y
            hz_last = h_ref[2, last] + more_z
            if later:
                send_sums(step + 1, x_last, y_last, z_last, hy_last, hz_last)
            h_ref[1, last], h_ref[2, last] = hy_last, hz_last
            e_ref[0, last], e_ref[1, last], e_ref[2, last] = x_last, y_last, z_last

        for plane in (last_plane, first_plane):
            plane()
        e_ref[0, 0:last] = part[0, 0:last]
        e_ref[1, 1:last] = part[1, 1:last]
        e_ref[2, 1:last] = part[2, 1:last]

    def stress(step):
        ex, ey, ez = e_ref[0], e_ref[1], e_ref[2]
        hx, hy, hz = h_ref[0], h_ref[1], h_ref[2]
        g = g_ref[step]
        xx, yy, zz = ex * ex + hx * hx, ey * ey + hy * hy, ez * ez + hz * hz
        energy = 0.5 * (xx + yy + zz)
        found = (xx - energy, ex * ey + hx * hy, ex * ez + hx * hz, yy - energy, ey * ez + hy * hz, zz - energy)
        for n, value in enumerate(found):
            tensor[n] = g * value if step == 0 else tensor[n] + g * value

    def ranks_and_buckets():
        owner = owner_ref[...]
        block = SLOTS // 4
        groups = NGX * NGY
        earlier = (iota((block, block), 0) < iota((block, block), 1)).astype(F32).astype(BF16)
        lane = iota((1, block), 1)
        before = jnp.zeros((groups, 1), F32)
        made = jnp.zeros((5 * NNEAR, LANES), F32)
        for b in range(4):
            cut = slice(b * block, (b + 1) * block)
            own = owner[:, cut]
            hot = (own == iota((groups, block), 0)).astype(F32)
            ahead = dot(hot.astype(BF16), earlier, (1, 0)) + before
            rank = jnp.sum(ahead * hot, axis=0, keepdims=True).astype(jnp.int32)
            before = before + jnp.sum(hot, axis=1, keepdims=True)
            place = rank * NFAR + (lax.shift_right_logical(own, 1) & (NFAR - 1))
            place_hot = (place == iota((LANES, block), 0)).astype(F32).astype(BF16)
            cell, normal = cell_ref[:, cut], normal_ref[:, cut]
            live = (lane + b * block < count_ref[0, 0, 0]).astype(F32)
            weight = live * (FACE_AREA * (1 - 2 * (normal & 1)).astype(F32))
            mine = lax.shift_right_logical(own, 5) * CORES + (own & 1) == iota((NNEAR, block), 0)
            entries = (
                (cell & 127).astype(F32),
                lax.shift_right_logical(cell, 7).astype(F32),
                weight,
                lax.shift_right_logical(normal, 1).astype(F32),
                tile_ref[:, cut].astype(F32),
            )
            rows = jnp.concatenate([jnp.where(mine, entry, zero) for entry in entries], 0)
            made = made + dot(rows.astype(BF16), place_hot, (1, 1))
        for n in range(5):
            bucket[n] = made[n * NNEAR : (n + 1) * NNEAR].reshape(NNEAR, 1, LANES)
        stl[...] = bucket[4]

    def toward(k):
        return lax.rem(y_chip + k // CORES, NY_CHIPS) * CORES + lax.rem(core + k % CORES, CORES)

    def origin(k):
        return lax.rem(y_chip + NY_CHIPS - k // CORES, NY_CHIPS) * CORES + lax.rem(core + k % CORES, CORES)

    def to_near(src, dst, send, recv, k):
        return pltpu.make_async_remote_copy(
            src_ref=src,
            dst_ref=dst.at[near],
            send_sem=send.at[k],
            recv_sem=recv.at[k],
            device_id=near_at(toward(k)),
            device_id_type=MESH,
        )

    def from_near(dst, send, recv, k):
        n = origin(k)
        return pltpu.make_async_remote_copy(
            src_ref=dst.at[n],
            dst_ref=dst.at[n],
            send_sem=send.at[k],
            recv_sem=recv.at[k],
            device_id=near_at(n),
            device_id_type=MESH,
        )

    def tiles_to(k):
        return to_near(stl.at[toward(k)], rtl, ts_sem, tr_sem, k)

    def values_to(k):
        return to_near(sval.at[k], rval, vs_sem, vr_sem, k)

    def lane_hots():
        for n in range(NNEAR):
            lane_hot[n] = (bucket[0, n] == iota((CZ, LANES), 0).astype(F32)).astype(F32).astype(BF16)

    def tile_hots():
        for d in range(1, NNEAR):
            from_near(rtl, ts_sem, tr_sem, d).wait_recv()
        for n in range(NNEAR):
            tile_hot[n] = (rtl[n] == iota((TILE_DEV, LANES), 0).astype(F32)).astype(F32).astype(BF16)

    def coefficients():
        material = mat_ref[...]

        def of_material(table):
            result = jnp.where(material == 0, table[0], zero)
            for which in (1, 2):
                result = jnp.where(material == which, table[which], result)
            return result

        sigma, gamma, plasma = of_material(sig_ref), of_material(gam_ref), of_material(pla_ref)
        coef[0] = (1.0 - sigma * DT / 2) / (1.0 + sigma * DT / 2)
        coef[1] = DT / (1.0 + sigma * DT / 2)
        coef[2] = (1.0 - gamma * DT / 2) / (1.0 + gamma * DT / 2)
        coef[3] = plasma * DT / (1.0 + gamma * DT / 2)

    loads[0].wait()
    loads[1].wait()
    send_x()
    send_yz(0)
    pl.semaphore_wait(barrier, greeted)
    entered.append(True)
    for which in held:
        start(*which)

    for step in range(STEPS):
        if step:
            send_yz(step)
        if step == 0:
            for load in loads[2:]:
                load.wait()
            coefficients()
            sg[0] = as_row(coef[1, CX - 1, :, 0:1])
            sg[1] = as_row(coef[1, 0, :, CZ - 1 : CZ])
            for n in range(2):
                when(ROUTES[(E_XZ, E_ZX)[n]], 1, edge_gain(n).start)
            current(step)
        else:
            current(step)
            stress(step - 1)
        if step == 1:
            ranks_and_buckets()
            for d in range(1, NNEAR):
                tiles_to(d).start()
            rtl[near] = stl[near]
        if step == 2:
            lane_hots()
        if step == 3:
            tile_hots()
        update(step)
    stores = [
        pltpu.make_async_copy(src, dst, out_sem.at[n]) for n, (src, dst) in enumerate(((e_ref, e_out), (h_ref, h_out)))
    ]
    for store in stores:
        store.start()
    stress(STEPS - 1)

    cells = CX * CY
    high, low = halves(tensor[...].reshape(6 * cells, CZ))
    parts = jnp.concatenate([high, low], 1)
    for k in (4, 5, 2, 3, 6, 7, 1, 0):
        n = toward(k)
        hot = lane_hot[n]
        read = dot(parts, jnp.concatenate([hot, hot], 0), (1, 0))
        row = bucket[1, n] == iota((cells, LANES), 0).astype(F32)
        xx, xy, xz, yy, yz, zz = [
            jnp.sum(jnp.where(row, read[c * cells : (c + 1) * cells], zero), axis=0, keepdims=True) for c in range(6)
        ]
        axis, weight = bucket[3, n], bucket[2, n]
        along_x, along_y = axis == 0.0, axis == 1.0
        sval[k, 0:1] = weight * jnp.where(along_x, xx, jnp.where(along_y, xy, xz))
        sval[k, 1:2] = weight * jnp.where(along_x, xy, jnp.where(along_y, yy, yz))
        sval[k, 2:3] = weight * jnp.where(along_x, xz, jnp.where(along_y, yz, zz))
        if k:
            values_to(k).start()
    rval[near] = sval[0]

    rows = (NFAR * 8, LANES)
    mine = (lax.shift_right_logical(iota(rows, 0), 3) == (iota(rows, 1) & (NFAR - 1))).astype(F32)
    dense = jnp.zeros((NFAR * 8, TILE_DEV), F32)
    for k in (0, 1, 2, 3, 6, 7, 4, 5):
        n = origin(k)
        if k:
            from_near(rval, vs_sem, vr_sem, k).wait_recv()
        value = rval[n]
        high = value.astype(BF16).astype(F32)
        both = jnp.concatenate([high, value - high, jnp.zeros((2, LANES), F32)], 0)
        spread = (jnp.concatenate([both] * NFAR, 0) * mine).astype(BF16)
        dense = dense + dot(spread, tile_hot[n], (1, 1))
    dense = dense.reshape(NFAR, 8, TILE_DEV)
    sdense[...] = dense[:, 0:3] + dense[:, 3:6]

    def to_far(d):
        n = lax.rem(far + d, NFAR)
        return pltpu.make_async_remote_copy(
            src_ref=sdense.at[n],
            dst_ref=rdense.at[far],
            send_sem=ds_sem.at[d],
            recv_sem=dr_sem.at[d],
            device_id=far_at(n),
            device_id_type=MESH,
        )

    def from_far(d):
        n = lax.rem(far + NFAR - d, NFAR)
        return pltpu.make_async_remote_copy(
            src_ref=sdense.at[n],
            dst_ref=rdense.at[n],
            send_sem=ds_sem.at[d],
            recv_sem=dr_sem.at[d],
            device_id=far_at(n),
            device_id_type=MESH,
        )

    for d in (8, 7, 9, 6, 10, 5, 11, 4, 12, 3, 13, 2, 14, 1, 15):
        to_far(d).start()
    rdense[far] = sdense[far]
    for step in range(STEPS):
        for which in range(12):
            when(ROUTES[which], 1, lambda which=which: message(step, which).wait_send())
    for n in range(2):
        when(ROUTES[(E_XZ, E_ZX)[n]], 1, edge_gain(n).wait_send)
    for d in range(1, NNEAR):
        tiles_to(d).wait_send()
        values_to(d).wait_send()
    for d in range(1, NFAR):
        to_far(d).wait_send()
    for store in stores:
        store.wait()
    for d in range(1, NFAR):
        from_far(d).wait_recv()
    force_ref[...] = jnp.sum(rdense[...], axis=0)


def hand_out(*refs):
    sem = refs[-1]
    copies = [pltpu.make_async_copy(refs[n], refs[n + 3], sem.at[n]) for n in range(3)]
    for copy in copies:
        copy.start()
    for copy in copies:
        copy.wait()


def local(
    e_field,
    h_field,
    current,
    material,
    sigma_table,
    gamma_table,
    plasma_table,
    g_kernel,
    surf_cell,
    surf_owner,
    surf_tile,
    surf_normal,
    row_count,
):
    field = jax.ShapeDtypeStruct((3, CX, CY, CZ), F32)
    hbm = pl.BlockSpec(memory_space=pltpu.HBM)
    dma = pltpu.SemaphoreType.DMA
    slots = [a.reshape(1, SLOTS) for a in (surf_cell, surf_owner, surf_tile, surf_normal)]
    operands = (e_field, h_field, current, material, *slots)
    operands += (sigma_table, gamma_table, plasma_table, g_kernel)
    operands = [pltpu.with_memory_space_constraint(a, pltpu.HBM) for a in operands]
    shapes = (field, field, jax.ShapeDtypeStruct((3, TILE_DEV), F32))
    made = pl.pallas_call(
        kernel,
        out_shape=shapes,
        in_specs=[hbm] * 12 + [pl.BlockSpec(memory_space=pltpu.SMEM)],
        out_specs=(hbm, hbm, pl.BlockSpec(memory_space=pltpu.VMEM)),
        scratch_shapes=[
            pltpu.VMEM((3, CX, CY, CZ), F32),
            pltpu.VMEM((3, CX, CY, CZ), F32),
            pltpu.VMEM((3, CX, CY, CZ), F32),
            pltpu.VMEM((3, CX, CY, CZ), F32),
            pltpu.VMEM((CX, CY, CZ), jnp.int32),
            pltpu.VMEM((1, SLOTS), jnp.int32),
            pltpu.VMEM((1, SLOTS), jnp.int32),
            pltpu.VMEM((1, SLOTS), jnp.int32),
            pltpu.VMEM((1, SLOTS), jnp.int32),
            pltpu.SMEM((3,), F32),
            pltpu.SMEM((3,), F32),
            pltpu.SMEM((3,), F32),
            pltpu.SMEM((STEPS,), F32),
            pltpu.VMEM((4, CX, CY, CZ), F32),
            pltpu.VMEM((6, CX, CY, CZ), F32),
            pltpu.VMEM((STEPS, 2, 2, CY, CZ), F32),
            pltpu.VMEM((STEPS, 2, 2, CY, CZ), F32),
            pltpu.VMEM((STEPS, 6, CX, 1, CZ), F32),
            pltpu.VMEM((STEPS, 6, CX, 1, CZ), F32),
            pltpu.VMEM((STEPS, 2, 8, CZ), F32),
            pltpu.VMEM((STEPS, 2, 8, CZ), F32),
            pltpu.VMEM((STEPS, 4, 1, CZ), F32),
            pltpu.VMEM((STEPS, 4, 1, CZ), F32),
            pltpu.VMEM((2, 1, CZ), F32),
            pltpu.VMEM((2, 1, CZ), F32),
            pltpu.VMEM((2, CY, CZ), F32),
            pltpu.VMEM((5, NNEAR, 1, LANES), F32),
            pltpu.VMEM((NNEAR, CZ, LANES), BF16),
            pltpu.VMEM((NNEAR, TILE_DEV, LANES), BF16),
            pltpu.VMEM((NNEAR, 1, LANES), F32),
            pltpu.VMEM((NNEAR, 1, LANES), F32),
            pltpu.VMEM((NNEAR, 3, LANES), F32),
            pltpu.VMEM((NNEAR, 3, LANES), F32),
            pltpu.VMEM((NFAR, 3, TILE_DEV), F32),
            pltpu.VMEM((NFAR, 3, TILE_DEV), F32),
            dma((12,)),
            dma((2,)),
            dma((STEPS, 12)),
            dma((STEPS, 12)),
            dma((NNEAR,)),
            dma((NNEAR,)),
            dma((NNEAR,)),
            dma((NNEAR,)),
            dma((NFAR,)),
            dma((NFAR,)),
            dma((2,)),
            dma((2,)),
        ],
        compiler_params=pltpu.CompilerParams(
            collective_id=0, has_side_effects=True, vmem_limit_bytes=24 * 2**20
        ),
    )(*operands, row_count)
    return pl.pallas_call(
        hand_out,
        out_shape=shapes,
        in_specs=[hbm] * 3,
        out_specs=(hbm,) * 3,
        scratch_shapes=[dma((3,))],
        compiler_params=pltpu.CompilerParams(vmem_limit_bytes=24 * 2**20),
    )(*made)


def solution(mesh):
    cells = P("gx", "gy", "gz")
    field = P(None, "gx", "gy", "gz")
    slots = P("gx", "gy", "gz", None)
    return jax.shard_map(
        local,
        mesh=mesh,
        in_specs=(
            field,
            field,
            field,
            cells,
            P(),
            P(),
            P(),
            P(),
            slots,
            P("gx", "gy", "gz", None, None),
            slots,
            slots,
            cells,
        ),
        out_specs=(field, field, P(None, ("gx", "gy", "gz"))),
        check_vma=False,
    )
```
